32 devices in a mesh: dp: 8 (over z, x), fsdp: 4 (over y, core).
Axes of the slice: x: 2, y: 2, z: 4, core: 2. Of those that a mesh axis runs over, the one named last changes fastest.
Arguments:
- tokens: bfloat16 [65536, 512], P(('dp', 'fsdp')), may hold values from -6 to 6
- lengths: int32 [64], P(('dp', 'fsdp')), may hold values from 640 to 1024, as said below
- norm_gains: bfloat16 [2, 512], P(None, 'fsdp'), may hold values from 0.25 to 1.75
- ema_params: bfloat16 [4, 512, 16], P(None, 'fsdp'), may hold values from -5 to 3
- qk_affine: bfloat16 [4, 128], P(None, 'fsdp'), may hold values from -2 to 2
- w_z: bfloat16 [512, 128], P('fsdp'), may hold values from -0.25 to 0.25
- w_v: bfloat16 [512, 1024], P('fsdp'), may hold values from -0.25 to 0.25
- w_r: bfloat16 [512, 1024], P('fsdp'), may hold values from -0.25 to 0.25
- w_u: bfloat16 [512, 512], P('fsdp'), may hold values from -0.25 to 0.25
- w_h: bfloat16 [512, 512], P('fsdp'), may hold values from -0.25 to 0.25
- u_h: bfloat16 [1024, 512], P('fsdp'), may hold values from -0.5 to 0.5
- w_in: bfloat16 [512, 1024], P('fsdp'), may hold values from -0.25 to 0.25
- w_out: bfloat16 [1024, 512], P('fsdp'), may hold values from -0.1875 to 0.1875
- cotangent: bfloat16 [65536, 512], P(('dp', 'fsdp')), may hold values from -6 to 6
Outputs:
- output: bfloat16 [65536, 512], P(('dp', 'fsdp'))
- grad_tokens: bfloat16 [65536, 512], P(('dp', 'fsdp'))
- grad_norm_gains: float32 [2, 512], P(None, 'fsdp')
- grad_ema_params: float32 [4, 512, 16], P(None, 'fsdp')
- grad_qk_affine: float32 [4, 128], P(None, 'fsdp')
- grad_w_z: float32 [512, 128], P('fsdp')
- grad_w_v: float32 [512, 1024], P('fsdp')
- grad_w_r: float32 [512, 1024], P('fsdp')
- grad_w_u: float32 [512, 512], P('fsdp')
- grad_w_h: float32 [512, 512], P('fsdp')
- grad_u_h: float32 [1024, 512], P('fsdp')
- grad_w_in: float32 [512, 1024], P('fsdp')
- grad_w_out: float32 [1024, 512], P('fsdp')
The draws below stay inside these ranges and needn't reach their ends.
Inputs may be any that keep to these rules, and one draw needn't show every extreme that they name: `lengths`: some slot holds 1024 valid tokens in every draw.
All inputs are finite; a program needn't handle non-finite values.
Results may differ from the reference program's by a relative error of at most 0.038.
Values may be sent and summed in bfloat16 or wider, within the bound.
A program may use at most 320 MiB of HBM per device.

```python
import jax
import jax.numpy as jnp
from jax import lax

D = 512
ZD = 128
VD = 1024
NDIM = 16
FF = 1024
SPAN = 128
LEN = 1024
SEQS = 64
TOKENS = 65536


def draw_lengths(key, part):
    key = jax.random.fold_in(key, 11)
    first_key, second_key = jax.random.split(key)
    drawn = jax.random.randint(first_key, (SEQS,), LEN * 5 // 8, LEN + 1)
    chosen = jax.random.randint(second_key, (), 0, SEQS)
    return jnp.where(jnp.arange(SEQS) == chosen, LEN, drawn).astype(jnp.int32)


def draw_ema_params(key, part):
    key = jax.random.fold_in(key, 23)
    subkeys = jax.random.split(key, 4)
    table_shape = (D, NDIM)
    rate_logit = jax.random.uniform(subkeys[0], table_shape, jnp.float32, -3.0, 1.0)
    damp_logit = jax.random.uniform(subkeys[1], table_shape, jnp.float32, -5.0, 0.0)
    expand = jnp.clip(jax.random.normal(subkeys[2], table_shape, jnp.float32), -3.0, 3.0)
    readout = 0.25 * jnp.clip(jax.random.normal(subkeys[3], table_shape, jnp.float32), -3.0, 3.0)
    return jnp.stack([rate_logit, damp_logit, expand, readout]).astype(jnp.bfloat16)


def strengthened(values, stream_key, source, target, parts, factor):
    owner, partner = [(jnp.arange(values.shape[dim]) // (values.shape[dim] // parts)).reshape([-1 if axis == dim else 1 for axis in range(values.ndim)]) for dim in (source, target)]
    chosen = jax.random.permutation(stream_key, parts)[partner]
    strong = (owner == chosen) | (owner == (partner + parts // 2) % parts)
    return jnp.where(strong, factor * values, values)


def level_of(stream_key, shape, cuts, low, top_value):
    def one(position, parts):
        steps = jax.random.uniform(jax.random.fold_in(jax.random.fold_in(stream_key, 6), position), (parts,), jnp.float32, low / len(cuts), top_value / len(cuts))
        return jnp.repeat(jnp.exp(steps), shape[position] // parts).reshape((-1,) + (1,) * (len(shape) - position - 1))

    level = one(*cuts[0])
    for cut in cuts[1:]:
        level = level * one(*cut)
    return level


def normal_values(rng, dims, width, bound, shards=(), kind=jnp.bfloat16):
    gain = level_of(rng, dims, shards, -0.22, 0.18) if shards else 1.0
    values = jax.random.normal(rng, dims, jnp.float32) * width * gain
    return jnp.minimum(jnp.maximum(values, -bound), bound).astype(kind)


def bell_draw_with(rng, extent, spread, most, cuts, heavy, held_as=jnp.bfloat16):
    values = spread * jax.random.normal(rng, extent, jnp.float32)
    if cuts:
        values = values * level_of(rng, extent, cuts, -0.22, 0.18)
    return jnp.clip(strengthened(values, jax.random.fold_in(rng, 3), *heavy), -most, most).astype(held_as)


def setup_inputs(seed: int = 0) -> dict:
    splits = jax.random.split(jax.random.key(seed), 15)
    return {
        "tokens": bell_draw_with(splits[0], (TOKENS, D), 1.0, 6.0, ((0, 32),), (0, 1, 32, 2.75)),
        "lengths": draw_lengths(jax.random.fold_in(splits[14], 71), 0),
        "norm_gains": jnp.clip(1.0 + 0.15 * jax.random.normal(splits[2], (2, D), jnp.float32), 0.25, 1.75).astype(jnp.bfloat16),
        "ema_params": draw_ema_params(jax.random.fold_in(splits[14], 71), 0),
        "qk_affine": normal_values(splits[4], (4, ZD), 0.5, 2.0, ((1, 4),)),
        "w_z": normal_values(splits[5], (D, ZD), D ** -0.5, 0.25, ((0, 4),)),
        "w_v": normal_values(splits[6], (D, VD), D ** -0.5, 0.25, ((0, 4),)),
        "w_r": normal_values(splits[7], (D, VD), D ** -0.5, 0.25, ((0, 4),)),
        "w_u": normal_values(splits[8], (D, D), D ** -0.5, 0.25, ((0, 4),)),
        "w_h": normal_values(splits[9], (D, D), D ** -0.5, 0.25, ((0, 4),)),
        "u_h": normal_values(splits[10], (VD, D), (VD // 8) ** -0.5, 0.5, ((0, 4),)),
        "w_in": normal_values(splits[11], (D, FF), D ** -0.5, 0.25, ((0, 4),)),
        "w_out": normal_values(splits[12], (FF, D), FF ** -0.5, 0.1875, ((0, 4),)),
        "cotangent": normal_values(splits[13], (TOKENS, D), 1.0, 6.0, ((0, 32),)),
    }


@jax.custom_vjp
def low(v):
    return lax.optimization_barrier(v.astype(jnp.bfloat16)).astype(jnp.float32)

@jax.custom_vjp
def low_back(v):
    return v

def low_keep(v):
    return (low(v), None)

def low_pass(kept, grad):
    return (grad,)

def back_keep(v):
    return (v, None)

def back_low(kept, grad):
    return (low(grad),)
low.defvjp(low_keep, low_pass)
low_back.defvjp(back_keep, back_low)
epsilon = 1e-06
highest = lax.Precision.HIGHEST

def silu_act(inputs):
    return inputs * jax.nn.sigmoid(inputs)

def normalize(values, scales):
    mean_sq = lax.optimization_barrier(jnp.mean(values * values, axis=-1, keepdims=True))
    return values * lax.rsqrt(mean_sq + epsilon) * scales

def smooth(inputs, params):
    batch_size, seq_length, model_width = inputs.shape
    block_count = seq_length // SPAN
    rate_in = jax.nn.sigmoid(params[0])
    damping = jax.nn.sigmoid(params[1])
    expand = params[2]
    readout = params[3]
    retain = 1.0 - rate_in * damping
    log_keep = jnp.log(retain)
    offsets = jnp.arange(SPAN).astype(inputs.dtype)
    powers = jnp.exp(offsets[:, None, None] * log_keep[None])
    kernel = jnp.einsum('tjh,jh->jt', powers, rate_in * expand * readout, precision=highest)
    lag_table = (jnp.arange(SPAN)[:, None] - jnp.arange(SPAN)[None, :]).astype(jnp.int32)
    toeplitz = jnp.where(lag_table[None] >= 0, jnp.take(kernel, jnp.maximum(lag_table, 0), axis=1), 0.0)
    emit_table = powers * retain[None] * readout[None]
    absorb_table = powers[::-1] * (rate_in * expand)[None]
    carry_decay = powers[-1] * retain
    pieces = inputs.reshape(batch_size, block_count, SPAN, model_width)
    local_part = jnp.einsum('jts,bcsj->bctj', toeplitz, pieces, precision=highest)

    def advance(state_in, block_in):
        following = state_in * carry_decay[None] + jnp.einsum('sjh,bsj->bjh', absorb_table, block_in, precision=highest)
        return (following, state_in)
    ordered = jnp.swapaxes(pieces, 0, 1)
    initial = jnp.zeros((batch_size, model_width, params.shape[-1]), inputs.dtype)
    unused, states = lax.scan(jax.checkpoint(advance), initial, ordered)
    carried = jnp.einsum('tjh,cbjh->bctj', emit_table, states, precision=highest)
    return (local_part + carried).reshape(batch_size, seq_length, model_width)

def attend(queries, keys_low, values_low, lens):
    batch_size, seq_length, zwidth = queries.shape
    block_count = seq_length // SPAN
    positions = jnp.arange(seq_length).astype(jnp.int32)
    valid = positions[None, :] < lens[:, None]
    query_blocks = queries.reshape(batch_size, block_count, SPAN, zwidth)
    key_blocks = keys_low.reshape(batch_size, block_count, SPAN, zwidth)
    value_blocks = values_low.reshape(batch_size, block_count, SPAN, -1)
    raw_scores = jnp.einsum('bctz,bcsz->bcts', query_blocks, key_blocks, precision=highest)
    scores = low_back(raw_scores * zwidth ** (-0.5))
    masked = jnp.where(valid.reshape(batch_size, block_count, 1, SPAN), scores, -1000000000.0)
    probs = jax.nn.softmax(masked, axis=-1)
    mixed = low_back(jnp.einsum('bcts,bcsv->bctv', low(probs), value_blocks, precision=highest))
    return mixed.reshape(batch_size, seq_length, -1) * valid[..., None].astype(queries.dtype)

def project(left, right):
    return jnp.einsum('bnd,de->bne', left, right, precision=highest)

def layer(inputs, gains, params, affine, w_z, w_v, w_r, w_u, w_h, u_h, w_in, w_out, lens):
    normed = normalize(inputs, gains[0])
    smoothed = smooth(normed, params)
    normed_low = low(normed)
    smooth_low = low(smoothed)
    shared_pre = low_back(project(smooth_low, w_z))
    value_pre = low_back(project(normed_low, w_v))
    reset_pre = low_back(project(smooth_low, w_r))
    update_pre = low_back(project(smooth_low, w_u))
    shared = silu_act(shared_pre)
    queries = low(shared * affine[0] + affine[1])
    keys_low = low(shared * affine[2] + affine[3])
    values_low = low(silu_act(value_pre))
    attended = attend(queries, keys_low, values_low, lens)
    reset = silu_act(reset_pre)
    update = jax.nn.sigmoid(update_pre)
    gated = low(reset * attended)
    hidden_pre = low_back(project(smooth_low, w_h) + project(gated, u_h))
    candidate = silu_act(hidden_pre)
    middle = inputs + update * (candidate - inputs)
    ffn_in = low(normalize(middle, gains[1]))
    ffn_pre = low_back(project(ffn_in, w_in))
    ffn_act = low(silu_act(ffn_pre))
    return middle + project(ffn_act, w_out)

def reference(tokens, lengths, norm_gains, ema_params, qk_affine, w_z, w_v, w_r, w_u, w_h, u_h, w_in, w_out, cotangent):
    weights = tuple((array.astype(jnp.float32) for array in (norm_gains, ema_params, qk_affine, w_z, w_v, w_r, w_u, w_h, u_h, w_in, w_out)))
    group_count = SEQS // 4
    inputs_all = tokens.astype(jnp.float32).reshape(group_count, 4, LEN, D)
    cots_all = cotangent.astype(jnp.float32).reshape(group_count, 4, LEN, D)
    lens_all = lengths.reshape(group_count, 4)

    def one_group(totals, packed):
        inputs, cots, lens = packed

        def forward(inputs_in, *params_in):
            return layer(inputs_in, *params_in, lens)
        result, pullback = jax.vjp(forward, inputs, *weights)
        grads = pullback(cots)
        new_totals = tuple((total + grad for total, grad in zip(totals, grads[1:])))
        return (new_totals, (result.astype(jnp.bfloat16), grads[0].astype(jnp.bfloat16)))
    initial = tuple((jnp.zeros_like(array) for array in weights))
    totals, (results, input_grads) = lax.scan(one_group, initial, (inputs_all, cots_all, lens_all))
    return (results.reshape(TOKENS, D), input_grads.reshape(TOKENS, D), totals[0], totals[1], totals[2], totals[3], totals[4], totals[5], totals[6], totals[7], totals[8], totals[9], totals[10])
```

```python
import functools

import jax
import jax.numpy as jnp
import numpy as np
from jax import lax
from jax.experimental import pallas as pl
from jax.experimental.pallas import tpu as pltpu
from jax.sharding import PartitionSpec as P

bf = jnp.bfloat16
f32 = jnp.float32
SPAN = 128
CH = 256
NH = 16
LG = 128
eps = 1e-6


def dft_tables():
    f=np.arange(CH)[:,None]+0.5
    m=np.arange(-CH,CH)[None,:]
    ang=2*np.pi*f*m/(2*CH)
    both=np.concatenate([np.cos(ang),np.sin(ang)],axis=0)
    return both.astype(np.float32)

def mm(a,b): return jnp.dot(a,b,preferred_element_type=f32)
def mm_tn(a,b): return lax.dot_general(a,b,(((0,),(0,)),((),())),preferred_element_type=f32)
def mm_nt(a,b): return lax.dot_general(a,b,(((1,),(1,)),((),())),preferred_element_type=f32)

def ema_rates(p):
    a=jax.nn.sigmoid(p[0]); g=jax.nn.sigmoid(p[1])
    return a,g,p[2],p[3],1.0-a*g

def power_of(base, n):
    out=None
    sq=base
    while n:
        if n&1: out = sq if out is None else out*sq
        n>>=1
        if n: sq=sq*sq
    return out

def ladder(keep, width):
    r=lax.broadcasted_iota(jnp.int32,(width,keep.shape[-1]),0)
    acc=jnp.ones((width,keep.shape[-1]),f32)
    sq=keep
    bit=1
    while bit<width:
        acc=acc*jnp.where((r&bit)!=0, sq, 1.0)
        sq=sq*sq
        bit*=2
    return acc

MESH = pl.DeviceIdType.MESH


def flip(i, bit):
    return i + bit - 2 * bit * ((i // bit) % 2)


def const_spec(a):
    nd = len(a.shape)
    return pl.BlockSpec(a.shape, lambda i: (0,) * nd, pipeline_mode=pl.Buffered(1))


ANY = pl.BlockSpec(memory_space=pl.ANY)


class Gather:
    def __init__(self, shards, outs, pieces, send, recv, local):
        self.shards, self.outs, self.pieces = shards, outs, pieces
        self.send, self.recv, self.local = send, recv, local
        self.dp = lax.axis_index("dp")
        self.fs = lax.axis_index("fsdp")
        self.x = self.dp % 2
        self.core_peer = (self.dp, flip(self.fs, 1))
        self.y_peer = (self.dp, flip(self.fs, 2))
        self.x_peer = (flip(self.dp, 1), self.fs)

    def peers(self):
        return [self.core_peer, self.y_peer, self.x_peer]

    def copy(self, p, k):
        a, first, r = self.pieces[p]
        shard, out = self.shards[a], self.outs[a]
        n = shard.shape[0]
        h = n // 2
        half = self.x * h + first
        other = (1 - self.x) * h + first
        far = flip(self.fs, 2) * n
        at = lambda ref, row: ref.at[pl.ds(pl.multiple_of(row, r), r)]
        src, dst, peer = (
            (at(shard, half), at(out, self.fs * n + half), self.y_peer),
            (at(out, far + half), at(out, far + half), self.x_peer),
            (at(out, far + half), at(out, far + half), self.core_peer),
            (at(out, far + other), at(out, far + other), self.core_peer),
        )[k]
        return pltpu.make_async_remote_copy(
            src_ref=src, dst_ref=dst, send_sem=self.send.at[4 * p + k], recv_sem=self.recv.at[4 * p + k],
            device_id=peer, device_id_type=MESH)

    def whole(self, a):
        n = self.shards[a].shape[0]
        slot = 4 * len(self.pieces) + a
        return pltpu.make_async_remote_copy(
            src_ref=self.shards[a], dst_ref=self.outs[a].at[pl.ds(pl.multiple_of(self.fs * n, n), n)],
            send_sem=self.send.at[slot], recv_sem=self.recv.at[slot], device_id=self.core_peer, device_id_type=MESH)

    def own(self, a):
        n = self.shards[a].shape[0]
        mine = pl.ds(pl.multiple_of(self.fs * n, n), n)
        return pltpu.make_async_copy(self.shards[a], self.outs[a].at[mine], self.local.at[a])

    def begin(self):
        for p in range(len(self.pieces)):
            self.copy(p, 0).start()
        for a in range(len(self.shards)):
            self.whole(a).start()
            self.own(a).start()

    def relay(self, p):
        self.copy(p, 0).wait_recv()
        self.copy(p, 1).start()
        self.copy(p, 2).start()

    def last(self, p):
        self.copy(p, 1).wait_recv()
        self.copy(p, 3).start()

    def finish(self):
        for p in range(len(self.pieces)):
            for k in range(4):
                self.copy(p, k).wait_send()
            for k in (2, 3):
                self.copy(p, k).wait_recv()
        for a in range(len(self.shards)):
            self.whole(a).wait()
            self.own(a).wait()


def gather_sems(arrays, pieces):
    sem = pltpu.SemaphoreType.DMA((4 * pieces + arrays,))
    return [sem, sem, pltpu.SemaphoreType.DMA((arrays,))]


SMALL = 4 * NH + 8
PIECES = ((0, 0, 32), (0, 32, 32), (1, 0, 128))


def ema_fwd_kernel(nseq, seqlen, remote, tok, dft, *rest):
    rest = list(rest)

    def take(n):
        out = rest[:n]
        del rest[:n]
        return out

    g = pl.program_id(0)
    nch = seqlen // CH
    rows = nseq * seqlen
    if remote:
        ema_i, gain_i, aff_i, *parts = take(9)
    else:
        small, = take(1)
    normed_o, smooth_o, xs_o, ks_o = take(4)
    if remote:
        small_o, aff_o, w_full, u_full = take(4)
    nscr, kscr, kspec, xspec, yspec = take(5)
    if remote:
        small, own, s1, r1, *sems = take(7)
        fs = lax.axis_index("fsdp")
        gather = Gather((own, parts[5]), (w_full, u_full), PIECES, *sems)
        across = [pltpu.make_async_remote_copy(
            src_ref=small.at[fs], dst_ref=small.at[fs], send_sem=s1.at[k], recv_sem=r1.at[k],
            device_id=peer, device_id_type=MESH) for k, peer in enumerate(fsdp_peers())]

    def slot(at, fn):
        if remote:
            pl.when(g == at)(fn)

    def open_up():
        greet(fsdp_peers() + [gather.x_peer])
        for i in range(4):
            small[fs, i * NH:(i + 1) * NH, :] = ema_i[i].astype(f32)
        tail = [gain_i[...].astype(f32), jnp.concatenate([aff_i[...].astype(f32)] * 4, axis=1),
                jnp.zeros((2, LG), f32)]
        small[fs, 4 * NH:, :] = jnp.concatenate(tail, axis=0)
        at = 0
        for w in parts[:5]:
            own[:, at:at + w.shape[1]] = w[...]
            at += w.shape[1]
        met(4)
        for c in across:
            c.start()
        gather.begin()

    slot(0, open_up)

    @pl.when(g == 0)
    def _():
        def body(i, _):
            r = pl.ds(pl.multiple_of(i * 256, 256), 256)
            x = tok[r, :].astype(f32)
            n = x * lax.rsqrt(jnp.mean(x * x, axis=-1, keepdims=True) + eps)
            for q in range(x.shape[1] // LG):
                nscr[q, r, :] = n[:, q * LG:(q + 1) * LG]
            return 0
        lax.fori_loop(0, rows // 256, body, 0)

    def settle():
        for c in across:
            c.wait()
        small_o[...] = small[...]
        for q in range(4):
            n = aff_i.shape[1]
            aff_o[:, q * n:(q + 1) * n] = small[q, 4 * NH + 2:4 * NH + 6, 0:n]

    slot(0, settle)
    slot(1, lambda: gather.relay(0))
    slot(2, lambda: gather.relay(1))
    slot(3, lambda: gather.relay(2))
    p = [small[g, i * NH:(i + 1) * NH, :] for i in range(4)]
    normed = (nscr[g] * small[g, 4 * NH:4 * NH + 1, :]).astype(bf)
    normed_o[...] = normed
    a, gg, ex, ro, keep = ema_rates(p)
    w = a * ex * ro * (1.0 / CH)
    step = power_of(keep, 16)
    z0 = []
    st = []
    for h in range(NH):
        z0.append(ladder(keep[h:h + 1, :], 16) * w[h:h + 1, :])
        st.append(jnp.broadcast_to(step[h:h + 1, :], (8, LG)))

    def kgen(i, zs):
        acc = zs[0]
        for h in range(1, NH):
            acc = acc + zs[h]
        kscr[pl.ds(pl.multiple_of(CH + i * 16, 16), 16), :] = acc.astype(bf)
        return tuple(jnp.concatenate([zs[h][:8] * st[h], zs[h][8:] * st[h]], axis=0) for h in range(NH))

    lax.fori_loop(0, seqlen // 16, kgen, tuple(z0), unroll=2)
    kscr[0:CH, :] = jnp.zeros((CH, LG), bf)
    for d in range(nch):
        kd = mm(dft[...], kscr[d * CH:(d + 2) * CH, :])
        kspec[d] = kd
        ks_o[d] = kd.astype(bf)
    fwd = dft[:, CH:]
    for c in range(nseq * nch):
        xd = mm(fwd, normed[c * CH:(c + 1) * CH, :])
        xspec[c] = xd
        xs_o[c] = xd.astype(bf)

    slot(2, lambda: gather.last(0))
    slot(3, lambda: gather.last(1))

    def point(i, _):
        rc = pl.ds(pl.multiple_of(i * 16, 16), 16)
        rs = pl.ds(pl.multiple_of(CH + i * 16, 16), 16)
        kc = [kspec[d, rc, :] for d in range(nch)]
        ks = [kspec[d, rs, :] for d in range(nch)]
        for b in range(nseq):
            xc = [xspec[b * nch + c, rc, :] for c in range(nch)]
            xs = [xspec[b * nch + c, rs, :] for c in range(nch)]
            for c in range(nch):
                yc = 0.
                ys = 0.
                for d in range(c + 1):
                    yc = yc + kc[d] * xc[c - d] - ks[d] * xs[c - d]
                    ys = ys + kc[d] * xs[c - d] + ks[d] * xc[c - d]
                yspec[b * nch + c, rc, :] = yc.astype(bf)
                yspec[b * nch + c, rs, :] = ys.astype(bf)
        return 0

    lax.fori_loop(0, CH // 16, point, 0)
    for c in range(nseq * nch):
        smooth_o[c * CH:(c + 1) * CH, :] = mm_tn(fwd, yspec[c]).astype(bf)

    def close():
        gather.last(2)
        gather.finish()

    slot(3, close)


def ema_forward(tokens, dft, nseq, small=None, comm_in=None):
    rows, D = tokens.shape
    seqlen = rows // nseq
    nch = seqlen // CH
    ng = D // LG
    nchunks = nseq * nch
    remote = comm_in is not None
    col = pl.BlockSpec((rows, LG), lambda g: (0, g))
    ins = [tokens, dft] + (list(comm_in) if remote else [small])
    wide = jax.ShapeDtypeStruct((rows, D), bf)
    outs = [(wide, col), (wide, col),
            (jax.ShapeDtypeStruct((nchunks, 2 * CH, D), bf), pl.BlockSpec((nchunks, 2 * CH, LG), lambda g: (0, 0, g))),
            (jax.ShapeDtypeStruct((nch, 2 * CH, D), bf), pl.BlockSpec((nch, 2 * CH, LG), lambda g: (0, 0, g)))]
    scratch = [pltpu.VMEM((ng, rows, LG), f32), pltpu.VMEM((seqlen + CH, LG), bf), pltpu.VMEM((nch, 2 * CH, LG), f32),
               pltpu.VMEM((nchunks, 2 * CH, LG), f32), pltpu.VMEM((nchunks, 2 * CH, LG), bf)]
    params = {}
    if remote:
        n = sum(w.shape[1] for w in comm_in[3:8])
        u = comm_in[8]
        a = jax.ShapeDtypeStruct((4, SMALL, LG), f32)
        b = jax.ShapeDtypeStruct((4, 4 * comm_in[2].shape[1]), f32)
        outs += [(a, const_spec(a)), (b, const_spec(b)), (jax.ShapeDtypeStruct((D, n), bf), ANY),
                 (jax.ShapeDtypeStruct((4 * u.shape[0], D), bf), ANY)]
        sem = pltpu.SemaphoreType.DMA((3,))
        scratch += [pltpu.VMEM(a.shape, f32), pltpu.VMEM((D // 4, n), bf), sem, sem] + gather_sems(2, len(PIECES))
        params = dict(collective_id=1, has_side_effects=True)
    return pl.pallas_call(
        functools.partial(ema_fwd_kernel, nseq, seqlen, remote),
        grid=(ng,),
        in_specs=[const_spec(a) for a in ins],
        out_specs=[o[1] for o in outs],
        out_shape=[o[0] for o in outs],
        scratch_shapes=scratch,
        compiler_params=pltpu.CompilerParams(vmem_limit_bytes=60 * 2**20, **params),
        name="ema_fwd",
    )(*ins)


class Reduce:
    def __init__(self, q, send, recv, **refs):
        self.q, self.send, self.recv = q, send, recv
        self.__dict__.update(refs)
        self.dp = lax.axis_index("dp")
        self.fs = lax.axis_index("fsdp")
        self.x = self.dp % 2
        self.z = self.dp // 2
        self.y = self.fs // 2

    def rows(self, at, count):
        return pl.ds(pl.multiple_of(at, self.q), count)

    def remote(self, src, dst, slot, device):
        return pltpu.make_async_remote_copy(
            src_ref=src, dst_ref=dst, send_sem=self.send.at[slot], recv_sem=self.recv.at[slot],
            device_id=device, device_id_type=MESH)

    def line(self):
        for i, oz in enumerate((3, 2, 1)):
            dp = self.dp
            if oz & 1:
                dp = flip(dp, 2)
            if oz & 2:
                dp = flip(dp, 4)
            yield i, dp

    def copies(self, stage):
        q = self.q
        if stage == "core":
            return [self.remote(self.give, self.core_in, 0, (self.dp, flip(self.fs, 1)))]
        if stage == "y":
            return [self.remote(self.core_in.at[1 - self.y], self.y_in, 1, (self.dp, flip(self.fs, 2)))]
        if stage == "x":
            return [self.remote(self.y_in.at[self.rows((1 - self.x) * 4 * q, 4 * q)], self.x_in, 2,
                                (flip(self.dp, 1), self.fs))]
        if stage == "z":
            return [self.remote(self.x_in.at[self.rows((dp // 2) * q, q)], self.z_in.at[i], 3 + i, (dp, self.fs))
                    for i, dp in self.line()]
        if stage == "back_z":
            mine = self.full.at[self.own_piece()]
            return [self.remote(mine, mine, 6 + i, (dp, self.fs)) for i, dp in self.line()]
        half = self.full.at[self.rows(self.x * 4 * q, 4 * q)]
        return [self.remote(half, half, 9, (flip(self.dp, 1), self.fs))]

    def start(self, stage):
        for c in self.copies(stage):
            c.start()

    def wait(self, stage):
        for c in self.copies(stage):
            c.wait()

    def add_core(self):
        self.wait("core")
        step = 2 * self.q
        for y in range(2):
            @pl.loop(0, 4)
            def _(i):
                r = pl.ds(pl.multiple_of(i * step, step), step)
                self.core_in[y, r, :] = (self.core_in[y, r, :].astype(f32) + self.keep[y, r, :].astype(f32)).astype(bf)

    def add_y(self):
        self.wait("y")
        step = 2 * self.q

        @pl.loop(0, 4)
        def _(i):
            r = pl.ds(pl.multiple_of(i * step, step), step)
            self.y_in[r, :] = (self.y_in[r, :].astype(f32) + self.core_in[self.y, r, :].astype(f32)).astype(bf)

    def add_x(self):
        self.wait("x")
        q = self.q

        @pl.loop(0, 4)
        def _(i):
            r = self.rows(i * q, q)
            k = self.rows((self.x * 4 + i) * q, q)
            self.x_in[r, :] = (self.x_in[r, :].astype(f32) + self.y_in[k, :].astype(f32)).astype(bf)

    def add_z(self):
        self.wait("z")
        q = self.q
        total = self.x_in[self.rows(self.z * q, q), :].astype(f32)
        for i in range(3):
            total += self.z_in[i].astype(f32)
        return total.astype(bf)

    def own_piece(self):
        return self.rows((self.x * 4 + self.z) * self.q, self.q)


def greet(peers):
    sem = pltpu.get_barrier_semaphore()
    for peer in peers:
        pl.semaphore_signal(sem, inc=1, device_id=peer, device_id_type=MESH)


def met(count):
    pl.semaphore_wait(pltpu.get_barrier_semaphore(), count)


def dp_peers():
    dp, fs = lax.axis_index("dp"), lax.axis_index("fsdp")
    out = []
    for k in range(1, 8):
        d = dp
        for bit in (1, 2, 4):
            if k & bit:
                d = flip(d, bit)
        out.append((d, fs))
    return out


def fsdp_peers():
    dp, fs = lax.axis_index("dp"), lax.axis_index("fsdp")
    return [(dp, flip(fs, 1)), (dp, flip(fs, 2)), (dp, flip(flip(fs, 1), 2))]


def blocks(accs, shard):
    at = 0
    for acc in accs:
        n = acc.shape[0] // 4
        rows = pl.ds(pl.multiple_of(shard * n, n), n)
        for j in range(acc.shape[1] // LG):
            yield at, n, acc[rows, j * LG:(j + 1) * LG]
            at += n


def pack(accs, dst, core):
    for y in range(2):
        for at, n, block in blocks(accs, 2 * y + core):
            dst[y, at:at + n, :] = block.astype(bf)


def pack_add(accs, dst, core):
    for y in range(2):
        for at, n, block in blocks(accs, 2 * y + core):
            dst[y, at:at + n, :] = (block + dst[y, at:at + n, :].astype(f32)).astype(bf)


def unpack(full, outs):
    at = 0
    for out in outs:
        n = out.shape[0]
        for j in range(out.shape[1] // LG):
            out[:, j * LG:(j + 1) * LG] = full[at:at + n, :].astype(f32)
            at += n


RT = 512


def sigm(v):
    return 0.5 * jnp.tanh(0.5 * v) + 0.5


def tile_valid(lens, step, seqlen):
    row0 = step * RT
    seq = row0 // seqlen
    return row0 - seq * seqlen, lens[seq]


def split_pack(w_a):
    zd = SPAN
    d = w_a.shape[0]
    vd = (w_a.shape[1] - zd - 2 * d) // 2
    cuts = [0, zd, zd + vd, zd + vd + d, zd + vd + 2 * d, zd + 2 * vd + 2 * d]
    return [w_a.at[:, lo:hi] for lo, hi in zip(cuts, cuts[1:])]


def forward_kernel(seqlen, remote, lens, sm, nm, tok, aff, w_a, u_h, *rest):
    shards, rest = (rest[:2], rest[2:]) if remote else ((), rest)
    middle_o, upd_o, u2_o, uh_o, val_o, vsl_o, gat_o, rv_o, a2_o, pr_o, qk_o = rest[:11]
    rest = rest[11:]
    if remote:
        gather = Gather(shards, rest[:2], ((0, 0, 64), (1, 0, 128)), *rest[3:])
        rest = rest[2:]
    gscr = rest[0]

    def slot(at, fn):
        if remote:
            pl.when(pl.program_id(0) == at)(fn)

    slot(0, lambda: greet(gather.peers()))

    w_z, w_r, w_u, w_h, w_v = split_pack(w_a)
    base, length = tile_valid(lens, pl.program_id(0), seqlen)
    zd = w_z.shape[1]
    vd = w_v.shape[1]
    s = sm[...]
    n = nm[...]
    scale = zd ** -0.5
    zp = mm(s, w_z[...])
    sg = sigm(zp)
    sh = zp * sg
    ssl = sg + sh * (1.0 - sg)
    q = (sh * aff[0:1, :] + aff[1:2, :]).astype(bf)
    k = (sh * aff[2:3, :] + aff[3:4, :]).astype(bf)
    qk_o[0] = q
    qk_o[1] = k
    qk_o[2] = sh.astype(bf)
    qk_o[3] = ssl.astype(bf)
    probs = []
    for b in range(RT // SPAN):
        r = slice(b * SPAN, (b + 1) * SPAN)
        sc = mm_nt(q[r], k[r]) * scale
        keys = base + b * SPAN + lax.broadcasted_iota(jnp.int32, (1, SPAN), 1)
        sc = jnp.where(keys < length, sc, -1e9)
        e = jnp.exp(sc - jnp.max(sc, axis=-1, keepdims=True))
        p = (e / jnp.sum(e, axis=-1, keepdims=True)).astype(bf)
        pr_o[r, :] = p
        probs.append(p)
    rows = base + lax.broadcasted_iota(jnp.int32, (RT, 1), 0)
    live = (rows < length).astype(f32)
    for j in range(vd // 256):
        c = slice(j * 256, (j + 1) * 256)
        vp = mm(n, w_v[:, c])
        sg = sigm(vp)
        v = vp * sg
        vl = v.astype(bf)
        val_o[:, c] = vl
        vsl_o[:, c] = (sg + v - v * sg).astype(bf)
        att = jnp.concatenate(
            [mm(probs[b], vl[b * SPAN:(b + 1) * SPAN]) for b in range(RT // SPAN)], axis=0)
        rp = mm(s, w_r[:, c])
        sg = sigm(rp)
        re = rp * sg
        att = att * live
        ga = (re * att).astype(bf)
        gat_o[:, c] = ga
        gscr[:, c] = ga
        rv_o[:, c] = (re * live).astype(bf)
        a2_o[:, c] = (att * (sg + re - re * sg)).astype(bf)
    for j in range(w_h.shape[1] // 256):
        c = slice(j * 256, (j + 1) * 256)
        hp = mm(s, w_h[:, c]) + mm(gscr[...], u_h[:, c])
        up = sigm(mm(s, w_u[:, c]))
        x = tok[:, c].astype(f32)
        sg = sigm(hp)
        cand = hp * sg
        diff = cand - x
        ud = up * diff
        middle_o[:, c] = (x + ud).astype(bf)
        upd_o[:, c] = up.astype(bf)
        u2_o[:, c] = (ud - ud * up).astype(bf)
        uh_o[:, c] = (up * (sg + cand - cand * sg)).astype(bf)


    def begin():
        met(3)
        gather.begin()

    def relay():
        gather.relay(0)
        gather.relay(1)

    def last():
        gather.last(0)
        gather.last(1)

    slot(0, begin)
    slot(1, relay)
    slot(2, last)
    slot(3, lambda: gather.finish())


def row_spec(width):
    return pl.BlockSpec((RT, width), lambda i: (i, 0))


SMEM = pl.BlockSpec(memory_space=pltpu.SMEM)


def forward_main(lengths, smooth, normed, tokens, affine, w_a, u_h, shards=()):
    rows, D = tokens.shape
    nseq = lengths.shape[0]
    vd = u_h.shape[0]
    zd = affine.shape[1]
    d_out = jax.ShapeDtypeStruct((rows, D), bf)
    v_out = jax.ShapeDtypeStruct((rows, vd), bf)
    ds, vs = row_spec(D), row_spec(vd)
    ws = (affine, w_a, u_h)
    remote = len(shards) > 0
    params = dict(collective_id=4, has_side_effects=True) if remote else {}
    fulls = [jax.ShapeDtypeStruct((4 * w.shape[0], w.shape[1]), bf) for w in shards]
    return pl.pallas_call(
        functools.partial(forward_kernel, rows // nseq, remote),
        grid=(rows // RT,),
        in_specs=[SMEM, ds, ds, ds] + [const_spec(w) for w in (*ws, *shards)],
        out_specs=[ds] * 4 + [vs] * 5 + [row_spec(SPAN), pl.BlockSpec((4, RT, zd), lambda i: (0, i, 0))]
        + [ANY] * len(shards),
        out_shape=[d_out] * 4 + [v_out] * 5
        + [jax.ShapeDtypeStruct((rows, SPAN), bf), jax.ShapeDtypeStruct((4, rows, zd), bf)] + fulls,
        scratch_shapes=[pltpu.VMEM((RT, vd), bf)] + (gather_sems(2, 2) if remote else []),
        compiler_params=pltpu.CompilerParams(vmem_limit_bytes=60 * 2**20, **params),
        name="forward_main",
    )(lengths, smooth, normed, tokens, *ws, *shards)


def ffn_kernel(packed, fs, middle, cot, gain, w_in, w_out, out_o, dm_o, dg_o, *rest):
    if packed:
        keep_o, give_o, gwi, gwo, ascr, gscr = rest
    else:
        gwi, gwo, ascr, gscr = rest

    @pl.when(pl.program_id(0) == 0)
    def _():
        gwi[...] = jnp.zeros_like(gwi)
        gwo[...] = jnp.zeros_like(gwo)
        dg_o[...] = jnp.zeros_like(dg_o)

    m = middle[...].astype(f32)
    inv = lax.rsqrt(jnp.mean(m * m, axis=-1, keepdims=True) + eps)
    gn = lane_row(gain, 4 * NH + 1)
    mr = m * inv
    y = (mr * gn).astype(bf)
    cl = cot[...]
    for j in range(w_in.shape[1] // 256):
        c = slice(j * 256, (j + 1) * 256)
        pre = mm(y, w_in[:, c])
        sg = sigm(pre)
        act = pre * sg
        al = act.astype(bf)
        ascr[:, c] = al
        ga = mm_nt(cl, w_out[c, :])
        gf = (ga * (sg + act - act * sg)).astype(bf)
        gscr[:, c] = gf
        gwo[c, :] += mm_tn(al, cl)
        gwi[:, c] += mm_tn(y, gf)
    out_o[...] = (m + mm(ascr[...], w_out[...])).astype(bf)
    dy = mm_nt(gscr[...], w_in[...])
    dg_o[...] += jnp.sum((dy * mr).reshape(RT // 8, 8, m.shape[1]), axis=0)
    dyg = dy * gn
    inner = jnp.mean(dyg * mr, axis=-1, keepdims=True)
    dm_o[...] = (cl.astype(f32) + inv * (dyg - mr * inner)).astype(bf)
    if packed:
        @pl.when(pl.program_id(0) == pl.num_programs(0) - 1)
        def _():
            core = fs[0] % 2
            pack((gwi, gwo), give_o, 1 - core)
            pack((gwi, gwo), keep_o, core)


def ffn_main(fs, middle, cot, gains, w_in, w_out, packed):
    rows, D = middle.shape
    ff = w_in.shape[1]
    ds = row_spec(D)
    accs = [(D, ff), (ff, D)]
    pair = [jax.ShapeDtypeStruct((2, (D * ff + ff * D) // 4 // LG, LG), bf)] * 2
    extra = pair if packed else [jax.ShapeDtypeStruct(s, f32) for s in accs]
    gain = jax.ShapeDtypeStruct((8, D), f32)
    return pl.pallas_call(
        functools.partial(ffn_kernel, packed),
        grid=(rows // RT,),
        in_specs=[SMEM, ds, ds] + [const_spec(w) for w in (gains, w_in, w_out)],
        out_specs=[ds, ds] + [const_spec(a) for a in [gain] + extra],
        out_shape=[jax.ShapeDtypeStruct((rows, D), bf)] * 2 + [gain] + extra,
        scratch_shapes=([pltpu.VMEM(s, f32) for s in accs] if packed else [])
        + [pltpu.VMEM((RT, ff), bf), pltpu.VMEM((RT, ff), bf)],
        compiler_params=pltpu.CompilerParams(vmem_limit_bytes=60 * 2**20),
        name="ffn_main",
    )(fs, middle, cot, gains, w_in, w_out)


def backward_kernel(qs, remote, dm, upd, u2, uh, gat, rv, a2, sm, val, vsl, pr, qk, nm, aff, u_h, *rest):
    rest = list(rest)

    def take(n):
        out = rest[:n]
        del rest[:n]
        return out

    if remote:
        keep1, give1 = take(2)
    dxd_o, gh_o, gu_o, gr_o, gv_o, gsp_o, ga_o = take(7)
    if remote:
        piece1_o, sum2_o, sum3_o, keep4_o, give4_o = take(5)
    gz, gv, gr, gu, gh_w, guh = take(6)
    ascr, = take(1)
    step = pl.program_id(0)
    tiles = pl.num_programs(0) // 2
    if remote:
        core1, y1, x1, z1, s1, r1 = take(6)
        give2, core2, y2, s2, r2 = take(5)
        give3, core3, s3, r3 = take(4)
        one = Reduce(qs[0], s1, r1, keep=keep1, give=give1, core_in=core1, y_in=y1, x_in=x1, z_in=z1)
        two = Reduce(qs[1], s2, r2, give=give2, core_in=core2, y_in=y2)
        three = Reduce(qs[2], s3, r3, give=give3, core_in=core3)
        core = lax.axis_index("fsdp") % 2

    def slot(at, fn):
        if remote:
            pl.when(step == at)(fn)

    @pl.when(step == 0)
    def _():
        for o in (gz, gv, gr, gu, gh_w, guh, ga_o):
            o[...] = jnp.zeros_like(o)

    def open_up():
        greet(fsdp_peers() + dp_peers())
        met(10)
        one.start("core")

    slot(0, open_up)

    def first():
        one.add_core()
        one.start("y")

    slot(1, first)

    def second():
        pack((gh_w, guh, gu), give2, 1 - core)
        two.start("core")
        one.add_y()
        one.start("x")

    slot(tiles, second)

    def third():
        two.wait("core")
        pack_add((gh_w, guh, gu), core2, core)
        two.start("y")
        pack((gr,), give3, 1 - core)
        three.start("core")

    slot(tiles + 1, third)

    def fourth():
        one.add_x()
        one.start("z")

    slot(tiles + 3, fourth)

    @pl.when(step < tiles)
    def _():
        vd = u_h.shape[0]
        d = dm[...].astype(f32)
        gh = (d * uh[...].astype(f32)).astype(bf)
        gu_l = (d * u2[...].astype(f32)).astype(bf)
        gh_o[...] = gh
        gu_o[...] = gu_l
        dxd_o[...] = (d - d * upd[...].astype(f32)).astype(bf)
        s = sm[...]
        gh_w[...] += mm_tn(s, gh)
        gu[...] += mm_tn(s, gu_l)
        at = pl.ds(pl.multiple_of(step * RT, RT), RT)
        for j in range(vd // 256):
            c = slice(j * 256, (j + 1) * 256)
            dg = mm_nt(gh, u_h[c, :])
            gr_l = (dg * a2[:, c].astype(f32)).astype(bf)
            gr_o[:, c] = gr_l
            ascr[at, c] = (dg * rv[:, c].astype(f32)).astype(bf)
            guh[c, :] += mm_tn(gat[:, c], gh)
            gr[:, c] += mm_tn(s, gr_l)

    @pl.when(step >= tiles)
    def _():
        vd = u_h.shape[0]
        zd = aff.shape[1]
        scale = zd ** -0.5
        gsp = []
        sums = [0.0] * 4
        for b in range(RT // SPAN):
            r = slice(b * SPAN, (b + 1) * SPAN)
            p = pr[r, :]
            pf = p.astype(f32)
            ga = ascr[pl.ds(pl.multiple_of((step - tiles) * RT + b * SPAN, SPAN), SPAN), :]
            dp = mm_nt(ga, val[r, :])
            inner = jnp.sum(dp * pf, axis=-1, keepdims=True)
            gs = (pf * (dp - inner)).astype(bf)
            dq = mm(gs, qk[1, r, :]) * scale
            dk = mm_tn(gs, qk[0, r, :]) * scale
            sh = qk[2, r, :].astype(f32)
            for i, t in enumerate((dq * sh, dq, dk * sh, dk)):
                sums[i] = sums[i] + jnp.sum(t.reshape(SPAN // 8, 8, zd), axis=0)
            gsp.append(((dq * aff[0:1, :] + dk * aff[2:3, :]) * qk[3, r, :].astype(f32)).astype(bf))
            dv = mm_tn(p, ga)
            gv_o[r, :] = (dv * vsl[r, :].astype(f32)).astype(bf)
        for i in range(4):
            ga_o[i] += sums[i]
        gsp = jnp.concatenate(gsp, axis=0)
        gsp_o[...] = gsp
        gz[...] += mm_tn(sm[...], gsp)
        n = nm[...]
        for j in range(vd // 256):
            c = slice(j * 256, (j + 1) * 256)
            gv[:, c] += mm_tn(n, gv_o[:, c])

    def close():
        pack((gv, gz), give4_o, 1 - core)
        pack((gv, gz), keep4_o, core)
        three.wait("core")
        sum3_o[...] = core3[...]
        pack_add((gr,), sum3_o, core)
        two.add_y()
        sum2_o[...] = y2[...]
        piece1_o[...] = one.add_z()

    slot(2 * tiles - 1, close)


def backward_main(dm, saved, smooth, normed, affine, u_h, chunk1=None):
    rows, D = dm.shape
    vd = u_h.shape[0]
    zd = affine.shape[1]
    remote = chunk1 is not None
    tiles = rows // RT
    upd, u2, uh, val, vsl, gat, rv, a2, pr, qk = saved

    def early(width):
        return pl.BlockSpec((RT, width), lambda i: (jnp.minimum(i, tiles - 1), 0))

    def late(width):
        return pl.BlockSpec((RT, width), lambda i: (jnp.maximum(i - tiles, 0), 0))

    de, ve, vl, dl = early(D), early(vd), late(vd), late(D)
    accs = [(D, zd), (D, vd), (D, vd), (D, D), (D, D), (vd, D)]
    ga = jax.ShapeDtypeStruct((4, 8, zd), f32)
    both = pl.BlockSpec((RT, D), lambda i: (i % tiles, 0))
    ins = [(dm, de), (upd, de), (u2, de), (uh, de), (gat, ve), (rv, ve), (a2, ve), (smooth, both),
           (val, vl), (vsl, vl), (pr, late(SPAN)),
           (qk, pl.BlockSpec((4, RT, zd), lambda i: (0, jnp.maximum(i - tiles, 0), 0))), (normed, dl),
           (affine, const_spec(affine)), (u_h, const_spec(u_h))]
    wide = lambda n: jax.ShapeDtypeStruct((rows, n), bf)
    outs = [(wide(D), de), (wide(D), de), (wide(D), de), (wide(vd), ve), (wide(vd), vl), (wide(zd), late(zd)),
            (ga, const_spec(ga))]
    scratch = [pltpu.VMEM((rows, vd), bf)]
    comm = {}
    qs = ()
    if remote:
        n = [chunk1[0].shape[1], (2 * D * D + vd * D) // 4 // LG, D * vd // 4 // LG, (D * vd + D * zd) // 4 // LG]
        qs = [a // 8 for a in n]
        ins += [(c, const_spec(c)) for c in chunk1]
        buf = lambda *s: jax.ShapeDtypeStruct(s + (LG,), bf)
        outs += [(s, const_spec(s)) for s in (buf(qs[0]), buf(n[1]), buf(2, n[2]), buf(2, n[3]), buf(2, n[3]))]
        v = lambda *s: pltpu.VMEM(s + (LG,), bf)
        sem = pltpu.SemaphoreType.DMA((10,))
        scratch = [pltpu.VMEM(a, f32) for a in accs] + scratch
        scratch += [v(2, n[0]), v(n[0]), v(n[0] // 2), v(3, qs[0]), sem, sem, v(2, n[1]), v(2, n[1]), v(n[1]), sem, sem,
                    v(2, n[2]), v(2, n[2]), sem, sem]
        comm = dict(collective_id=2, has_side_effects=True)
    else:
        outs += [(s, const_spec(s)) for s in (jax.ShapeDtypeStruct(a, f32) for a in accs)]
    return pl.pallas_call(
        functools.partial(backward_kernel, qs, remote),
        grid=(2 * tiles,),
        in_specs=[i[1] for i in ins],
        out_specs=[o[1] for o in outs],
        out_shape=[o[0] for o in outs],
        scratch_shapes=scratch,
        compiler_params=pltpu.CompilerParams(vmem_limit_bytes=62 * 2**20, **comm),
        name="backward_main",
    )(*[i[0] for i in ins])


def lane_row(small, row):
    return jnp.concatenate([small[q, row:row + 1, :] for q in range(small.shape[0])], axis=1)


def input_kernel(nseq, seqlen, qs, remote, gh, gu, gr, gsp, gv, w_a, tok, small, dft, xs_i, ks_i, *rest):
    rest = list(rest)

    def take(n):
        out = rest[:n]
        del rest[:n]
        return out

    if remote:
        piece1, sum2, sum3, keep4, give4, gain1, aff = take(7)
        dn_o, full1, full2, full3, full4, small_o = take(6)
    else:
        dn_o, dema_o, dgain_o = take(3)
    dsm, dn, xr, dyspec, dxspec, gspec, dkscr = take(7)
    step = pl.program_id(0)
    ng = dsm.shape[0]
    tiles = pl.num_programs(0) - ng
    nch = seqlen // CH
    rows = nseq * seqlen
    if remote:
        f1, s1, r1 = take(3)
        x2, z2, f2, s2, r2 = take(5)
        y3, x3, z3, f3, s3, r3 = take(6)
        core4, y4, x4, z4, f4, s4, r4 = take(7)
        sums, near, total, far, s5, r5 = take(6)
        one = Reduce(qs[0], s1, r1, full=f1)
        two = Reduce(qs[1], s2, r2, y_in=sum2, x_in=x2, z_in=z2, full=f2)
        three = Reduce(qs[2], s3, r3, core_in=sum3, y_in=y3, x_in=x3, z_in=z3, full=f3)
        four = Reduce(qs[3], s4, r4, keep=keep4, give=give4, core_in=core4, y_in=y4, x_in=x4, z_in=z4, full=f4)

    def slot(at, fn):
        if remote:
            pl.when(step == at)(fn)

    def back(chunk):
        chunk.full[chunk.own_piece(), :] = chunk.add_z()
        chunk.start("back_z")

    def widen(chunk):
        chunk.wait("back_z")
        chunk.start("back_x")

    def open_up():
        greet(fsdp_peers() + dp_peers())
        f1[one.own_piece(), :] = piece1[...]
        met(10)
        three.start("y")
        one.start("back_z")
        two.start("x")
        four.start("core")

    slot(0, open_up)

    def at_two():
        four.add_core()
        four.start("y")

    slot(2, at_two)

    def at_three():
        two.add_x()
        two.start("z")
        three.add_y()
        three.start("x")
        widen(one)

    slot(3, at_three)

    @pl.when(step < tiles)
    def _():
        w_z, w_r, w_u, w_h, w_v = split_pack(w_a)
        at = pl.ds(pl.multiple_of(step * RT, RT), RT)
        x = tok[...].astype(f32)
        n = (x * lax.rsqrt(jnp.mean(x * x, axis=-1, keepdims=True) + eps)).astype(bf)
        a = mm_nt(gv[...], w_v[...])
        b = mm_nt(gh[...], w_h[...]) + mm_nt(gu[...], w_u[...]) + mm_nt(gsp[...], w_z[...]) + mm_nt(gr[...], w_r[...])
        for q in range(ng):
            c = slice(q * LG, (q + 1) * LG)
            xr[q, at, :] = n[:, c]
            dn[q, at, :] = a[:, c].astype(bf)
            dsm[q, at, :] = b[:, c].astype(bf)

    @pl.when(step >= tiles)
    def _():
        g = step - tiles

        def d_first():
            back(four)
            two.wait("back_x")

        slot(tiles + 3, d_first)
        fwd = dft[:, CH:]
        for c in range(nseq * nch):
            dyspec[c] = mm(fwd, dsm[g, c * CH:(c + 1) * CH, :])

        def a_second():
            back(two)
            three.add_x()
            three.start("z")

        slot(tiles, a_second)

        def b_first():
            four.add_y()
            four.start("x")
            one.wait("back_x")

        slot(tiles + 1, b_first)

        def c_first():
            widen(two)
            back(three)
            four.add_x()
            four.start("z")

        slot(tiles + 2, c_first)

        def d_second():
            widen(three)

        slot(tiles + 3, d_second)

        def point(i, _):
            rc = pl.ds(pl.multiple_of(i * 16, 16), 16)
            rs = pl.ds(pl.multiple_of(CH + i * 16, 16), 16)
            kc = [ks_i[d, rc, :].astype(f32) for d in range(nch)]
            ks = [ks_i[d, rs, :].astype(f32) for d in range(nch)]
            gc = [0.] * nch
            gs = [0.] * nch
            for b in range(nseq):
                dc = [dyspec[b * nch + c, rc, :] for c in range(nch)]
                ds = [dyspec[b * nch + c, rs, :] for c in range(nch)]
                for c in range(nch):
                    oc = 0.
                    os = 0.
                    for d in range(nch - c):
                        oc = oc + kc[d] * dc[c + d] + ks[d] * ds[c + d]
                        os = os + kc[d] * ds[c + d] - ks[d] * dc[c + d]
                    dxspec[b * nch + c, rc, :] = oc.astype(bf)
                    dxspec[b * nch + c, rs, :] = os.astype(bf)
                for c in range(nch):
                    xc = xs_i[b * nch + c, rc, :].astype(f32)
                    xs = xs_i[b * nch + c, rs, :].astype(f32)
                    for d in range(nch - c):
                        gc[d] = gc[d] + xc * dc[c + d] + xs * ds[c + d]
                        gs[d] = gs[d] + xc * ds[c + d] - xs * dc[c + d]
            for d in range(nch):
                gspec[d, rc, :] = gc[d].astype(bf)
                gspec[d, rs, :] = gs[d].astype(bf)
            return 0

        lax.fori_loop(0, CH // 16, point, 0)
        dgain = 0.
        for c in range(nseq * nch):
            r = slice(c * CH, (c + 1) * CH)
            t = mm_tn(fwd, dxspec[c]) + dn[g, r, :].astype(f32)
            dn_o[0, r, :] = t.astype(bf)
            dgain = dgain + jnp.sum((t * xr[g, r, :].astype(f32)).reshape(CH // 8, 8, LG), axis=0)
        for d in range(nch):
            dk = mm_tn(fwd, gspec[d])
            if d + 1 < nch:
                dk = dk + mm_tn(dft[:, :CH], gspec[d + 1])
            dkscr[d * CH:(d + 1) * CH, :] = dk * (1.0 / CH)
        p = [small[g, i * NH:(i + 1) * NH, :] for i in range(4)]
        a, gg, ex, ro, keep = ema_rates(p)
        p8 = power_of(keep, 8)
        st = [jnp.broadcast_to(p8[h:h + 1, :], (8, LG)) for h in range(NH)]

        def horner(i, ab):
            A, B = ab
            v = dkscr[pl.ds(pl.multiple_of(seqlen - 8 - i * 8, 8), 8), :]
            B = tuple(B[h] * st[h] + A[h] for h in range(NH))
            A = tuple(A[h] * st[h] + v for h in range(NH))
            return (A, B)

        none = dkscr[0:8, :] * 0.0
        zero = (none,) * NH
        A, B = lax.fori_loop(0, seqlen // 8, horner, (zero, zero), unroll=2)
        rr = lax.broadcasted_iota(jnp.int32, (8, LG), 0).astype(f32)
        As = []
        Bs = []
        for h in range(NH):
            lad = ladder(keep[h:h + 1, :], 8)
            low = jnp.concatenate([jnp.zeros((1, LG), f32), lad[:7]], axis=0)
            As.append(jnp.sum(lad * A[h], axis=0, keepdims=True))
            Bs.append(jnp.sum(rr * low * A[h] + 8.0 * lad[7:8] * lad * B[h], axis=0, keepdims=True))
        As = jnp.concatenate(As, axis=0)
        Bs = jnp.concatenate(Bs, axis=0)
        dkeep = a * ex * ro * Bs
        da = ex * ro * As - gg * dkeep
        dg = -a * dkeep
        grads = (da * a * (1.0 - a), dg * gg * (1.0 - gg), a * ro * As, a * ex * As)
        for i, v in enumerate(grads):
            if remote:
                sums[g, i * NH:(i + 1) * NH, :] = v
            else:
                dema_o[i] = v
        if remote:
            sums[g, 4 * NH:, :] = jnp.concatenate(
                [jnp.sum(dgain, axis=0, keepdims=True), jnp.zeros((7, LG), f32)], axis=0)
        else:
            dgain_o[...] = dgain

    def close():
        fs = lax.axis_index("fsdp")

        def across(k, src, dst, peer):
            return pltpu.make_async_remote_copy(src_ref=src, dst_ref=dst, send_sem=s5.at[k], recv_sem=r5.at[k],
                                                device_id=peer, device_id_type=MESH)

        g1 = jnp.sum(gain1[...], axis=0, keepdims=True)
        cols = jnp.sum(aff[...], axis=1)
        for q in range(ng):
            sums[q, 4 * NH + 1:4 * NH + 6, :] = jnp.concatenate([g1[:, q * LG:(q + 1) * LG], cols], axis=0)
        first = [across(k, sums.at[peer[1]], near.at[k], peer) for k, peer in enumerate(fsdp_peers())]
        for c in first:
            c.start()
        widen(four)
        full1[...] = f1[...]
        full2[...] = f2[...]
        for c in first:
            c.wait()
        total[...] = sums[fs] + near[0] + near[1] + near[2]
        second = [across(3 + k, total, far.at[k], peer) for k, peer in enumerate(dp_peers())]
        for c in second:
            c.start()
        three.wait("back_x")
        full3[...] = f3[...]
        for c in second:
            c.wait()
        t = total[...]
        for k in range(7):
            t = t + far[k]
        small_o[...] = t
        four.wait("back_x")
        full4[...] = f4[...]

    slot(tiles + ng - 1, close)


def input_main(grads, w_a, tokens, small, dft, xspec, kspec, nseq, comm_in=None):
    rows, D = tokens.shape
    seqlen = rows // nseq
    nch = seqlen // CH
    ng = D // LG
    nchunks = nseq * nch
    tiles = rows // RT
    remote = comm_in is not None

    def early(a):
        return pl.BlockSpec((RT, a.shape[1]), lambda i: (jnp.minimum(i, tiles - 1), 0))

    def lanes(i):
        return jnp.maximum(i - tiles, 0)

    ins = [(a, early(a)) for a in grads] + [(w_a, const_spec(w_a)), (tokens, early(tokens)), (small, const_spec(small))]
    ins += [(dft, const_spec(dft)), (xspec, pl.BlockSpec((nchunks, 2 * CH, LG), lambda i: (0, 0, lanes(i)))),
            (kspec, pl.BlockSpec((nch, 2 * CH, LG), lambda i: (0, 0, lanes(i))))]
    outs = [(jax.ShapeDtypeStruct((ng, rows, LG), bf), pl.BlockSpec((1, rows, LG), lambda i: (lanes(i), 0, 0)))]
    scratch = [pltpu.VMEM((ng, rows, LG), bf)] * 3
    scratch += [pltpu.VMEM((nchunks, 2 * CH, LG), f32),
                pltpu.VMEM((nchunks, 2 * CH, LG), bf), pltpu.VMEM((nch, 2 * CH, LG), bf), pltpu.VMEM((seqlen, LG), f32)]
    params = {}
    qs = ()
    if remote:
        piece1, sum2, sum3, keep4, give4, gain1, aff = comm_in
        n = [piece1.shape[0] * 8, sum2.shape[0], sum3.shape[1], keep4.shape[1]]
        qs = [a // 8 for a in n]
        ins += [(a, const_spec(a)) for a in comm_in]
        fulls = [jax.ShapeDtypeStruct((a, LG), bf) for a in n]
        one = jax.ShapeDtypeStruct((SMALL, LG), f32)
        outs += [(a, const_spec(a)) for a in fulls + [one]]
        v = lambda *s: pltpu.VMEM(s + (LG,), bf)
        w = lambda *s: pltpu.VMEM(s + one.shape, f32)
        sem = pltpu.SemaphoreType.DMA((10,))
        scratch += [v(n[0]), sem, sem,
                    v(n[1] // 2), v(3, qs[1]), v(n[1]), sem, sem,
                    v(n[2]), v(n[2] // 2), v(3, qs[2]), v(n[2]), sem, sem,
                    v(2, n[3]), v(n[3]), v(n[3] // 2), v(3, qs[3]), v(n[3]), sem, sem,
                    w(4), w(3), w(), w(7), sem, sem]
        params = dict(collective_id=3, has_side_effects=True)
    else:
        outs += [(jax.ShapeDtypeStruct((4, NH, D), f32), pl.BlockSpec((4, NH, LG), lambda i: (0, 0, lanes(i)))),
                 (jax.ShapeDtypeStruct((8, D), f32), pl.BlockSpec((8, LG), lambda i: (0, lanes(i))))]
    return pl.pallas_call(
        functools.partial(input_kernel, nseq, seqlen, qs, remote),
        grid=(tiles + ng,),
        in_specs=[i[1] for i in ins],
        out_specs=[o[1] for o in outs],
        out_shape=[o[0] for o in outs],
        scratch_shapes=scratch,
        compiler_params=pltpu.CompilerParams(vmem_limit_bytes=62 * 2**20, **params),
        name="input_main",
    )(*[i[0] for i in ins])


def finish_kernel(groups, fs, tok, dxd, dn, small, *rest):
    n = len(groups)
    fulls, sums = rest[:n], rest[n:n + 1]
    outs = list(rest[n + 1:] if groups else rest)
    dtok_o = outs.pop(0)
    x = tok[...].astype(f32)
    inv = lax.rsqrt(jnp.mean(x * x, axis=-1, keepdims=True) + eps)
    d = jnp.concatenate([dn[q] for q in range(dn.shape[0])], axis=1).astype(f32) * lane_row(small, 4 * NH)
    xr = x * inv
    dtok_o[...] = (dxd[...].astype(f32) + inv * (d - xr * jnp.mean(d * xr, axis=-1, keepdims=True))).astype(bf)
    if groups:
        @pl.when(pl.program_id(0) == 0)
        def _():
            gain_o, ema_o, aff_o = outs[:3]
            t = sums[0]
            gain_o[...] = t[4 * NH:4 * NH + 2, :]
            for i in range(4):
                ema_o[i] = t[i * NH:(i + 1) * NH, :]
            width = aff_o.shape[1]
            mine = 0.
            for q in range(4):
                mine = mine + jnp.where(fs[0] == q, 1.0, 0.0) * t[4 * NH + 2:4 * NH + 6, q * width:(q + 1) * width]
            aff_o[...] = mine
            at = 3
            for full, count in zip(fulls, groups):
                unpack(full, outs[at:at + count])
                at += count


def finish_main(fs, tokens, dxd, dn, small, fulls=(), sums=None, groups=(), shapes=()):
    rows, D = tokens.shape
    ng = dn.shape[0]
    ds = row_spec(D)
    extra = list(fulls) + ([sums] if groups else [])
    outs = [jax.ShapeDtypeStruct(s, f32) for s in shapes]
    return pl.pallas_call(
        functools.partial(finish_kernel, groups),
        grid=(rows // RT,),
        in_specs=[SMEM, ds, ds, pl.BlockSpec((ng, RT, LG), lambda i: (0, i, 0))] + [const_spec(a) for a in [small] + extra],
        out_specs=[ds] + [const_spec(a) for a in outs],
        out_shape=[jax.ShapeDtypeStruct((rows, D), bf)] + outs,
        name="finish",
    )(fs, tokens, dxd, dn, small, *extra)


def local_step(tokens, lengths, cotangent, fs, plain=None, shards=None):
    nseq = lengths.shape[0]
    rows, D = tokens.shape
    dft = jnp.asarray(dft_tables(), bf)
    remote = shards is not None
    if remote:
        ema_t, norm_gains, qk_affine, w_z, w_r, w_u, w_h, w_v, u_h, w_in, w_out = shards
        normed, smooth, x_spec, k_spec, small, affine, w_a, u_full = ema_forward(
            tokens, dft, nseq, comm_in=(ema_t, norm_gains, qk_affine, w_z, w_r, w_u, w_h, w_v, u_h))
        *saved, in_full, out_full = forward_main(
            lengths, smooth, normed, tokens, affine, w_a, u_full, (w_in, w_out))
    else:
        small, affine, w_a, u_full, in_full, out_full = plain
        normed, smooth, x_spec, k_spec = ema_forward(tokens, dft, nseq, small)
        saved = forward_main(lengths, smooth, normed, tokens, affine, w_a, u_full)
    middle, *saved = saved
    output, dm, g_gain1, *first = ffn_main(fs, middle, cotangent, small, in_full, out_full, remote)
    dxd, gh, gu, gr, gv, gsp, g_aff, *second = backward_main(
        dm, saved, smooth, normed, affine, u_full, first if remote else None)
    shared = ((gh, gu, gr, gsp, gv), w_a, tokens, small, dft, x_spec, k_spec, nseq)
    if not remote:
        dn, g_ema, g_gain0 = input_main(*shared)
        grad_tokens, = finish_main(fs, tokens, dxd, dn, small)
        grad_gains = jnp.stack([jnp.sum(g_gain0, axis=0), jnp.sum(g_gain1, axis=0)])
        return output, grad_tokens, (grad_gains, jnp.swapaxes(g_ema, 1, 2), jnp.sum(g_aff, axis=1), *second, *first)
    dn, *fulls, sums = input_main(*shared, (*second, g_gain1, g_aff))
    shapes = [norm_gains.shape, ema_t.shape, qk_affine.shape]
    shapes += [w.shape for w in (w_in, w_out, w_h, u_h, w_u, w_r, w_v, w_z)]
    grad_tokens, g_gains, g_ema, g_aff, g_in, g_out, g_h, g_uh, g_u, g_r, g_v, g_z = finish_main(
        fs, tokens, dxd, dn, small, fulls, sums, (2, 3, 1, 2), shapes)
    return output, grad_tokens, (g_gains, jnp.swapaxes(g_ema, 1, 2), g_aff, g_z, g_v, g_r, g_u, g_h, g_uh, g_in, g_out)


def small_table(norm_gains, ema_params):
    d = norm_gains.shape[1]
    ema = jnp.swapaxes(ema_params, 1, 2).reshape(4 * NH, d)
    rows = jnp.concatenate([ema, norm_gains, jnp.zeros((SMALL - 4 * NH - 2, d), bf)], axis=0).astype(f32)
    return jnp.swapaxes(rows.reshape(SMALL, d // LG, LG), 0, 1)


def per_device(tokens, lengths, norm_gains, ema_params, qk_affine, w_z, w_v, w_r, w_u, w_h, u_h, w_in, w_out, cotangent):
    at = lax.axis_index("fsdp")
    parts = lax.axis_size("fsdp")
    fs = at.reshape(1)
    if parts == 4 and lax.axis_size("dp") == 8:
        shards = (jnp.swapaxes(ema_params, 1, 2), norm_gains, qk_affine, w_z, w_r, w_u, w_h, w_v, u_h, w_in, w_out)
        output, grad_tokens, pieces = local_step(tokens, lengths, cotangent, fs, shards=shards)
        return (output, grad_tokens) + pieces
    gather = lambda w, axis: lax.all_gather(w, "fsdp", axis=axis, tiled=True)
    w_a = gather(jnp.concatenate([w_z, w_r, w_u, w_h, w_v], axis=1), 0)
    plain = (small_table(gather(norm_gains, 1), gather(ema_params, 1)), gather(qk_affine, 1).astype(f32), w_a,
             gather(u_h, 0), gather(w_in, 0), gather(w_out, 0))
    output, grad_tokens, totals = local_step(tokens, lengths, cotangent, fs, plain)
    summed = lax.psum(totals, ("dp", "fsdp"))
    pieces = tuple(
        lax.dynamic_slice_in_dim(g, at * (g.shape[d] // parts), g.shape[d] // parts, d)
        for g, d in zip(summed, (1, 1, 1, 0, 0, 0, 0, 0, 0, 0, 0)))
    return (output, grad_tokens) + pieces


def solution(mesh):
    rows = P(("dp", "fsdp"), None)
    shard = P("fsdp", None)
    wide = P(None, "fsdp")
    deep = P(None, "fsdp", None)
    return jax.shard_map(
        per_device,
        mesh=mesh,
        in_specs=(rows, P(("dp", "fsdp")), wide, deep, wide) + (shard,) * 8 + (rows,),
        out_specs=(rows, rows, wide, deep, wide) + (shard,) * 8,
        check_vma=False,
    )
```

```python
import functools

import jax
import jax.numpy as jnp
import numpy as np
from jax import lax
from jax.experimental import pallas as pl
from jax.experimental.pallas import tpu as pltpu
from jax.sharding import PartitionSpec as P

bf = jnp.bfloat16
f32 = jnp.float32
SPAN = 128
CH = 256
NH = 16
LG = 128
eps = 1e-6


def dft_tables():
    f=np.arange(CH)[:,None]+0.5
    m=np.arange(-CH,CH)[None,:]
    ang=2*np.pi*f*m/(2*CH)
    both=np.concatenate([np.cos(ang),np.sin(ang)],axis=0)
    return np.concatenate([both,both.T],axis=0).astype(np.float32)

def mm(a,b): return jnp.dot(a,b,preferred_element_type=f32)
def mm_tn(a,b): return lax.dot_general(a,b,(((0,),(0,)),((),())),preferred_element_type=f32)
def mm_nt(a,b): return lax.dot_general(a,b,(((1,),(1,)),((),())),preferred_element_type=f32)

def ema_rates(p):
    a=jax.nn.sigmoid(p[0]); g=jax.nn.sigmoid(p[1])
    return a,g,p[2],p[3],1.0-a*g

def power_of(base, n):
    out=None
    sq=base
    while n:
        if n&1: out = sq if out is None else out*sq
        n>>=1
        if n: sq=sq*sq
    return out

def ladder(keep, width):
    r=lax.broadcasted_iota(jnp.int32,(width,keep.shape[-1]),0)
    acc=jnp.ones((width,keep.shape[-1]),f32)
    sq=keep
    bit=1
    while bit<width:
        acc=acc*jnp.where((r&bit)!=0, sq, 1.0)
        sq=sq*sq
        bit*=2
    return acc

MESH = pl.DeviceIdType.MESH


def flip(i, bit):
    return i + bit - 2 * bit * ((i // bit) % 2)


def const_spec(a):
    nd = len(a.shape)
    return pl.BlockSpec(a.shape, lambda i: (0,) * nd, pipeline_mode=pl.Buffered(1))


ANY = pl.BlockSpec(memory_space=pl.ANY)


class Gather:
    def __init__(self, shards, outs, pieces, send, recv, local):
        self.shards, self.outs, self.pieces = shards, outs, pieces
        self.send, self.recv, self.local = send, recv, local
        self.dp = lax.axis_index("dp")
        self.fs = lax.axis_index("fsdp")
        self.x = self.dp % 2
        self.z = (self.dp // 2) % 2
        self.core_peer = (self.dp, flip(self.fs, 1))
        self.y_peer = (self.dp, flip(self.fs, 2))
        self.x_peer = (flip(self.dp, 1), self.fs)
        self.z_peer = (flip(self.dp, 2), self.fs)

    def peers(self):
        return [self.core_peer, self.y_peer, self.x_peer, self.z_peer]

    def copy(self, p, k):
        a, col, width = self.pieces[p]
        shard, out = self.shards[a], self.outs[a]
        n = shard.shape[0]
        far = flip(self.fs, 2) * n
        cols = pl.ds(col, width)
        x, z = self.x, self.z

        def at(ref, base, zz, xx, half=None):
            r = n // 4 if half is None else n // 8
            row = base + (2 * zz + xx) * (n // 4) + (0 if half is None else half * r)
            return ref.at[pl.ds(pl.multiple_of(row, r), r), cols]

        src, dst, peer = (
            (at(shard, 0, z, x), at(out, self.fs * n, z, x), self.y_peer),
            (at(out, far, z, x),) * 2 + (self.x_peer,),
            (at(out, far, z, x),) * 2 + (self.z_peer,),
            (at(out, far, 1 - z, x, 0),) * 2 + (self.x_peer,),
            (at(out, far, z, 1 - x, 1),) * 2 + (self.z_peer,),
            (at(out, far, z, x),) * 2 + (self.core_peer,),
            (at(out, far, z, 1 - x),) * 2 + (self.core_peer,),
            (at(out, far, 1 - z, x),) * 2 + (self.core_peer,),
            (at(out, far, 1 - z, 1 - x),) * 2 + (self.core_peer,),
        )[k]
        return pltpu.make_async_remote_copy(
            src_ref=src, dst_ref=dst, send_sem=self.send.at[9 * p + k], recv_sem=self.recv.at[9 * p + k],
            device_id=peer, device_id_type=MESH)

    def whole(self, a):
        n = self.shards[a].shape[0]
        slot = 9 * len(self.pieces) + a
        return pltpu.make_async_remote_copy(
            src_ref=self.shards[a], dst_ref=self.outs[a].at[pl.ds(pl.multiple_of(self.fs * n, n), n)],
            send_sem=self.send.at[slot], recv_sem=self.recv.at[slot], device_id=self.core_peer, device_id_type=MESH)

    def own(self, a):
        n = self.shards[a].shape[0]
        mine = pl.ds(pl.multiple_of(self.fs * n, n), n)
        return pltpu.make_async_copy(self.shards[a], self.outs[a].at[mine], self.local.at[a])

    def begin(self):
        for p in range(len(self.pieces)):
            self.copy(p, 0).start()
        for a in range(len(self.shards)):
            self.whole(a).start()
            self.own(a).start()

    def relay(self, p):
        self.copy(p, 0).wait_recv()
        for k in (1, 2, 5):
            self.copy(p, k).start()

    def cross(self, p):
        self.copy(p, 2).wait_recv()
        self.copy(p, 3).start()
        self.copy(p, 7).start()
        self.copy(p, 1).wait_recv()
        self.copy(p, 4).start()
        self.copy(p, 6).start()

    def last(self, p):
        self.copy(p, 3).wait_recv()
        self.copy(p, 4).wait_recv()
        self.copy(p, 8).start()

    def finish(self):
        for p in range(len(self.pieces)):
            for k in range(9):
                self.copy(p, k).wait_send()
            for k in (5, 6, 7, 8):
                self.copy(p, k).wait_recv()
        for a in range(len(self.shards)):
            self.whole(a).wait()
            self.own(a).wait()


def gather_sems(arrays, pieces):
    sem = pltpu.SemaphoreType.DMA((9 * pieces + arrays,))
    return [sem, sem, pltpu.SemaphoreType.DMA((arrays,))]


SMALL = 4 * NH + 16
PIECES = 3


def ema_fwd_kernel(nseq, seqlen, remote, tok, dft, *rest):
    rest = list(rest)

    def take(n):
        out = rest[:n]
        del rest[:n]
        return out

    g = pl.program_id(0)
    nch = seqlen // CH
    rows = nseq * seqlen
    if remote:
        ema_i, gain_i, aff_i, *parts = take(9)
    else:
        small, = take(1)
    normed_o, smooth_o, xs_o, ks_o = take(4)
    if remote:
        small_o, aff_o, w_full, u_full = take(4)
    nscr, kscr, kspec, xspec, yspec = take(5)
    if remote:
        small, sent, own, s1, r1, *sems = take(8)
        fs = lax.axis_index("fsdp")
        gather = Gather((own, parts[5]), (w_full, u_full),
                        ((0, 0, 1664), (0, 1664, own.shape[1] - 1664), (1, 0, parts[5].shape[1])), *sems)
        across = [pltpu.make_async_remote_copy(
            src_ref=sent.at[fs], dst_ref=sent.at[fs], send_sem=s1.at[k], recv_sem=r1.at[k],
            device_id=peer, device_id_type=MESH) for k, peer in enumerate(fsdp_peers())]

    def slot(at, fn):
        if remote:
            pl.when(g == at)(fn)

    def open_up():
        greet(fsdp_peers() + [gather.x_peer, gather.z_peer])
        for i in range(4):
            sent[fs, i * NH:(i + 1) * NH, :] = ema_i[i]
        tail = [gain_i[...].astype(f32), jnp.concatenate([aff_i[...].astype(f32)] * 4, axis=1),
                jnp.zeros((SMALL - 4 * NH - 6, LG), f32)]
        sent[fs, 4 * NH:, :] = jnp.concatenate(tail, axis=0).astype(bf)
        at = 0
        for w in parts[:5]:
            own[:, at:at + w.shape[1]] = w[...]
            at += w.shape[1]
        met(5)
        for c in across:
            c.start()
        gather.begin()

    slot(0, open_up)

    @pl.when(g == 0)
    def _():
        def body(i, _):
            r = pl.ds(pl.multiple_of(i * 256, 256), 256)
            x = tok[r, :].astype(f32)
            n = x * lax.rsqrt(jnp.mean(x * x, axis=-1, keepdims=True) + eps)
            for q in range(x.shape[1] // LG):
                nscr[q, r, :] = n[:, q * LG:(q + 1) * LG]
            return 0
        lax.fori_loop(0, rows // 256, body, 0)

    def settle():
        for c in across:
            c.wait()
        for q in range(4):
            small[q] = sent[q].astype(f32)
        small_o[...] = small[...]
        for q in range(4):
            n = aff_i.shape[1]
            aff_o[:, q * n:(q + 1) * n] = small[q, 4 * NH + 2:4 * NH + 6, 0:n]

    slot(0, settle)

    slot(1, lambda: gather.relay(1))
    slot(2, lambda: gather.cross(1))

    def last_first():
        gather.last(0)
        gather.last(1)

    slot(3, last_first)
    p = [small[g, i * NH:(i + 1) * NH, :] for i in range(4)]
    normed = (nscr[g] * small[g, 4 * NH:4 * NH + 1, :]).astype(bf)
    normed_o[...] = normed
    a, gg, ex, ro, keep = ema_rates(p)
    w = a * ex * ro * (1.0 / CH)
    step = power_of(keep, 16)
    z0 = []
    st = []
    for h in range(NH):
        z0.append(ladder(keep[h:h + 1, :], 16) * w[h:h + 1, :])
        st.append(jnp.broadcast_to(step[h:h + 1, :], (8, LG)))

    def kgen(i, zs):
        acc = list(zs)
        while len(acc) > 1:
            acc = [acc[j] + acc[j + 1] for j in range(0, len(acc), 2)]
        acc = acc[0]
        kscr[pl.ds(pl.multiple_of(CH + i * 16, 16), 16), :] = acc.astype(bf)
        return tuple(jnp.concatenate([zs[h][:8] * st[h], zs[h][8:] * st[h]], axis=0) for h in range(NH))

    lax.fori_loop(0, seqlen // 16, kgen, tuple(z0), unroll=4)
    kscr[0:CH, :] = jnp.zeros((CH, LG), bf)
    both = dft[:2 * CH]
    fwd = dft[:2 * CH, CH:]
    inv = dft[3 * CH:]
    for d in range(0, nch, 2):
        kd = mm(both, jnp.concatenate([kscr[d * CH:(d + 2) * CH, :], kscr[(d + 1) * CH:(d + 3) * CH, :]], axis=1))
        for i in range(2):
            kspec[d + i] = kd[:, i * LG:(i + 1) * LG]
            ks_o[d + i] = kd[:, i * LG:(i + 1) * LG].astype(bf)
    for c in range(0, nseq * nch, 2):
        xd = mm(fwd, jnp.concatenate([normed[c * CH:(c + 1) * CH], normed[(c + 1) * CH:(c + 2) * CH]], axis=1))
        for i in range(2):
            xspec[c + i] = xd[:, i * LG:(i + 1) * LG]
            xs_o[c + i] = xd[:, i * LG:(i + 1) * LG].astype(bf)

    slot(1, lambda: gather.relay(2))
    slot(2, lambda: gather.cross(2))

    def point(i, _):
        rc = pl.ds(pl.multiple_of(i * 16, 16), 16)
        rs = pl.ds(pl.multiple_of(CH + i * 16, 16), 16)
        kc = [kspec[d, rc, :] for d in range(nch)]
        ks = [kspec[d, rs, :] for d in range(nch)]
        for b in range(nseq):
            xc = [xspec[b * nch + c, rc, :] for c in range(nch)]
            xs = [xspec[b * nch + c, rs, :] for c in range(nch)]
            for c in range(nch):
                yc = 0.
                ys = 0.
                for d in range(c + 1):
                    yc = yc + kc[d] * xc[c - d] - ks[d] * xs[c - d]
                    ys = ys + kc[d] * xs[c - d] + ks[d] * xc[c - d]
                yspec[b * nch + c, rc, :] = yc.astype(bf)
                yspec[b * nch + c, rs, :] = ys.astype(bf)
        return 0

    lax.fori_loop(0, CH // 16, point, 0)
    slot(0, lambda: gather.relay(0))
    slot(1, lambda: gather.cross(0))
    for c in range(0, nseq * nch, 2):
        y = mm(inv, jnp.concatenate([yspec[c], yspec[c + 1]], axis=1)).astype(bf)
        smooth_o[c * CH:(c + 1) * CH, :] = y[:, :LG]
        smooth_o[(c + 1) * CH:(c + 2) * CH, :] = y[:, LG:]

    def close():
        gather.last(2)
        gather.finish()

    slot(3, close)


def ema_forward(tokens, dft, nseq, small=None, comm_in=None):
    rows, D = tokens.shape
    seqlen = rows // nseq
    nch = seqlen // CH
    ng = D // LG
    nchunks = nseq * nch
    remote = comm_in is not None
    col = pl.BlockSpec((rows, LG), lambda g: (0, g))
    ins = [tokens, dft] + (list(comm_in) if remote else [small])
    wide = jax.ShapeDtypeStruct((rows, D), bf)
    outs = [(wide, col), (wide, col),
            (jax.ShapeDtypeStruct((nchunks, 2 * CH, D), bf), pl.BlockSpec((nchunks, 2 * CH, LG), lambda g: (0, 0, g))),
            (jax.ShapeDtypeStruct((nch, 2 * CH, D), bf), pl.BlockSpec((nch, 2 * CH, LG), lambda g: (0, 0, g)))]
    scratch = [pltpu.VMEM((ng, rows, LG), f32), pltpu.VMEM((seqlen + CH, LG), bf), pltpu.VMEM((nch, 2 * CH, LG), f32),
               pltpu.VMEM((nchunks, 2 * CH, LG), f32), pltpu.VMEM((nchunks, 2 * CH, LG), bf)]
    params = {}
    if remote:
        n = sum(w.shape[1] for w in comm_in[3:8])
        u = comm_in[8]
        a = jax.ShapeDtypeStruct((4, SMALL, LG), f32)
        b = jax.ShapeDtypeStruct((4, 4 * comm_in[2].shape[1]), f32)
        outs += [(a, const_spec(a)), (b, const_spec(b)), (jax.ShapeDtypeStruct((D, n), bf), ANY),
                 (jax.ShapeDtypeStruct((4 * u.shape[0], D), bf), ANY)]
        sem = pltpu.SemaphoreType.DMA((3,))
        scratch += [pltpu.VMEM(a.shape, f32), pltpu.VMEM(a.shape, bf), pltpu.VMEM((D // 4, n), bf), sem, sem] + gather_sems(2, PIECES)
        params = dict(collective_id=1, has_side_effects=True)
    return pl.pallas_call(
        functools.partial(ema_fwd_kernel, nseq, seqlen, remote),
        grid=(ng,),
        in_specs=[const_spec(a) for a in ins],
        out_specs=[o[1] for o in outs],
        out_shape=[o[0] for o in outs],
        scratch_shapes=scratch,
        compiler_params=pltpu.CompilerParams(vmem_limit_bytes=60 * 2**20, **params),
        name="ema_fwd",
    )(*ins)


class Reduce:
    def __init__(self, q, first, send, recv, **refs):
        self.q, self.first, self.send, self.recv = q, first, send, recv
        self.__dict__.update(refs)
        self.dp = lax.axis_index("dp")
        self.fs = lax.axis_index("fsdp")
        self.x = self.dp % 2
        self.z = self.dp // 2
        self.y = self.fs // 2

    def rows(self, at, count):
        return pl.ds(pl.multiple_of(at, self.q), count)

    def half(self, x):
        return self.rows(x * 4 * self.q, 4 * self.q)

    def remote(self, src, dst, slot, device):
        return pltpu.make_async_remote_copy(
            src_ref=src, dst_ref=dst, send_sem=self.send.at[slot], recv_sem=self.recv.at[slot],
            device_id=device, device_id_type=MESH)

    def line(self):
        for i, oz in enumerate((3, 2, 1)):
            dp = self.dp
            if oz & 1:
                dp = flip(dp, 2)
            if oz & 2:
                dp = flip(dp, 4)
            yield i, dp

    def copies(self, stage):
        q = self.q
        over_y = (self.dp, flip(self.fs, 2))
        over_x = (flip(self.dp, 1), self.fs)
        if stage == "core":
            return [self.remote(self.give, self.core_in, 0, (self.dp, flip(self.fs, 1)))]
        if stage == "near" and self.first == "y":
            return [self.remote(self.core_in.at[1 - self.y], self.near, 1, over_y)]
        if stage == "near":
            return [self.remote(self.core_in.at[y, self.half(1 - self.x)], self.near.at[y], 1 + y, over_x)
                    for y in range(2)]
        if stage == "next" and self.first == "y":
            return [self.remote(self.near.at[self.half(1 - self.x)], self.mid, 3, over_x)]
        if stage == "next":
            return [self.remote(self.near.at[1 - self.y], self.mid, 3, over_y)]
        if stage == "z":
            return [self.remote(self.mid.at[self.rows((dp // 2) * q, q)], self.z_in.at[i], 4 + i, (dp, self.fs))
                    for i, dp in self.line()]
        if stage == "back_z":
            mine = self.full.at[self.own_piece()]
            return [self.remote(mine, mine, 7 + i, (dp, self.fs)) for i, dp in self.line()]
        half = self.full.at[self.half(self.x)]
        return [self.remote(half, half, 10, over_x)]

    def start(self, stage):
        for c in self.copies(stage):
            c.start()

    def wait(self, stage):
        for c in self.copies(stage):
            c.wait()

    def add(self, dst, src, count):
        @pl.loop(0, 4)
        def _(i):
            r = self.rows(i * (count // 4), count // 4)
            dst[r, :] = (dst[r, :].astype(f32) + src[r, :].astype(f32)).astype(bf)

    def to_near(self):
        self.wait("core")
        for y in range(2):
            self.add(self.core_in.at[y], self.keep.at[y], 8 * self.q)
        self.start("near")

    def add_near(self):
        self.wait("near")
        if self.first == "y":
            self.add(self.near, self.core_in.at[self.y], 8 * self.q)
        else:
            for y in range(2):
                self.add(self.near.at[y], self.core_in.at[y, self.half(self.x)], 4 * self.q)

    def to_next(self):
        self.add_near()
        self.start("next")

    def to_z(self):
        self.wait("next")
        src = self.near.at[self.half(self.x)] if self.first == "y" else self.near.at[self.y]
        self.add(self.mid, src, 4 * self.q)
        self.start("z")

    def add_z(self):
        self.wait("z")
        total = self.mid[self.rows(self.z * self.q, self.q), :].astype(f32)
        for i in range(3):
            total += self.z_in[i].astype(f32)
        return total.astype(bf)

    def back(self):
        self.full[self.own_piece(), :] = self.add_z()
        self.start("back_z")

    def widen(self):
        self.wait("back_z")
        self.start("back_x")

    def own_piece(self):
        return self.rows((self.x * 4 + self.z) * self.q, self.q)


def greet(peers):
    sem = pltpu.get_barrier_semaphore()
    for peer in peers:
        pl.semaphore_signal(sem, inc=1, device_id=peer, device_id_type=MESH)


def met(count):
    pl.semaphore_wait(pltpu.get_barrier_semaphore(), count)


def dp_peers():
    dp, fs = lax.axis_index("dp"), lax.axis_index("fsdp")
    out = []
    for k in range(1, 8):
        d = dp
        for bit in (1, 2, 4):
            if k & bit:
                d = flip(d, bit)
        out.append((d, fs))
    return out


def fsdp_peers():
    dp, fs = lax.axis_index("dp"), lax.axis_index("fsdp")
    return [(dp, flip(fs, 1)), (dp, flip(fs, 2)), (dp, flip(flip(fs, 1), 2))]


def blocks(accs, shard):
    at = 0
    for acc in accs:
        n = acc.shape[0] // 4
        rows = pl.ds(pl.multiple_of(shard * n, n), n)
        for j in range(acc.shape[1] // LG):
            yield at, n, acc[rows, j * LG:(j + 1) * LG]
            at += n


def pack(accs, dst, core):
    for y in range(2):
        for at, n, block in blocks(accs, 2 * y + core):
            dst[y, at:at + n, :] = block.astype(bf)


def pack_add(accs, dst, core):
    for y in range(2):
        for at, n, block in blocks(accs, 2 * y + core):
            dst[y, at:at + n, :] = (block + dst[y, at:at + n, :].astype(f32)).astype(bf)


def unpack(full, outs):
    at = 0
    for out in outs:
        n = out.shape[0]
        for j in range(out.shape[1] // LG):
            out[:, j * LG:(j + 1) * LG] = full[at:at + n, :].astype(f32)
            at += n


RT = 512
TT = 1024


def sigm(v):
    return 0.5 * jnp.tanh(0.5 * v) + 0.5


def tile_valid(lens, step, seqlen):
    row0 = step * RT
    seq = row0 // seqlen
    return row0 - seq * seqlen, lens[seq]


def split_pack(w_a):
    zd = SPAN
    d = w_a.shape[0]
    vd = (w_a.shape[1] - zd - 2 * d) // 2
    cuts = [0, zd, zd + vd, zd + vd + d, zd + vd + 2 * d, zd + 2 * vd + 2 * d]
    return [w_a.at[:, lo:hi] for lo, hi in zip(cuts, cuts[1:])]


def forward_kernel(seqlen, remote, lens, sm, nm, tok, aff, w_a, u_h, *rest):
    shards, rest = (rest[:2], rest[2:]) if remote else ((), rest)
    middle_o, upd_o, u2_o, uh_o, val_o, vsl_o, gat_o, rv_o, a2_o, pr_o, qk_o = rest[:11]
    rest = rest[11:]
    if remote:
        gather = Gather(shards, rest[:2], tuple((a, 0, w.shape[1]) for a, w in enumerate(shards)), *rest[3:])
        rest = rest[2:]
    gscr = rest[0]

    def slot(at, fn):
        if remote:
            pl.when(pl.program_id(0) == at)(fn)

    slot(0, lambda: greet(gather.peers()))

    w_z, w_r, w_u, w_h, w_v = split_pack(w_a)
    base, length = tile_valid(lens, pl.program_id(0), seqlen)
    zd = w_z.shape[1]
    vd = w_v.shape[1]
    s = sm[...]
    n = nm[...]
    scale = zd ** -0.5
    zp = mm(s, w_z[...])
    sg = sigm(zp)
    sh = zp * sg
    ssl = sg + sh * (1.0 - sg)
    q = (sh * aff[0:1, :] + aff[1:2, :]).astype(bf)
    k = (sh * aff[2:3, :] + aff[3:4, :]).astype(bf)
    qk_o[0] = q
    qk_o[1] = k
    qk_o[2] = sh.astype(bf)
    qk_o[3] = ssl.astype(bf)
    probs = []
    for b in range(RT // SPAN):
        r = slice(b * SPAN, (b + 1) * SPAN)
        sc = mm_nt(q[r], k[r]) * scale
        keys = base + b * SPAN + lax.broadcasted_iota(jnp.int32, (1, SPAN), 1)
        sc = jnp.where(keys < length, sc, -1e9)
        e = jnp.exp(sc - jnp.max(sc, axis=-1, keepdims=True))
        p = (e / jnp.sum(e, axis=-1, keepdims=True)).astype(bf)
        pr_o[r, :] = p
        probs.append(p)

    def begin():
        met(4)
        gather.begin()

    slot(0, begin)

    def relay():
        gather.relay(0)
        gather.relay(1)

    slot(1, relay)

    def cross():
        gather.cross(0)
        gather.cross(1)

    slot(2, cross)

    def last():
        gather.last(0)
        gather.last(1)

    slot(3, last)
    rows = base + lax.broadcasted_iota(jnp.int32, (RT, 1), 0)
    live = (rows < length).astype(f32)
    for j in range(vd // 256):
        c = slice(j * 256, (j + 1) * 256)
        vp = mm(n, w_v[:, c])
        sg = sigm(vp)
        v = vp * sg
        vl = v.astype(bf)
        val_o[:, c] = vl
        vsl_o[:, c] = (sg + v - v * sg).astype(bf)
        att = jnp.concatenate(
            [mm(probs[b], vl[b * SPAN:(b + 1) * SPAN]) for b in range(RT // SPAN)], axis=0)
        rp = mm(s, w_r[:, c])
        sg = sigm(rp)
        re = rp * sg
        att = att * live
        ga = (re * att).astype(bf)
        gat_o[:, c] = ga
        gscr[:, c] = ga
        rv_o[:, c] = (re * live).astype(bf)
        a2_o[:, c] = (att * (sg + re - re * sg)).astype(bf)
    for j in range(w_h.shape[1] // 256):
        c = slice(j * 256, (j + 1) * 256)
        hp = mm(s, w_h[:, c]) + mm(gscr[...], u_h[:, c])
        up = sigm(mm(s, w_u[:, c]))
        x = tok[:, c].astype(f32)
        sg = sigm(hp)
        cand = hp * sg
        diff = cand - x
        ud = up * diff
        middle_o[:, c] = (x + ud).astype(bf)
        upd_o[:, c] = up.astype(bf)
        u2_o[:, c] = (ud - ud * up).astype(bf)
        uh_o[:, c] = (up * (sg + cand - cand * sg)).astype(bf)


    slot(3, lambda: gather.finish())


def row_spec(width):
    return pl.BlockSpec((RT, width), lambda i: (i, 0))


SMEM = pl.BlockSpec(memory_space=pltpu.SMEM)


def forward_main(lengths, smooth, normed, tokens, affine, w_a, u_h, shards=()):
    rows, D = tokens.shape
    nseq = lengths.shape[0]
    vd = u_h.shape[0]
    zd = affine.shape[1]
    d_out = jax.ShapeDtypeStruct((rows, D), bf)
    v_out = jax.ShapeDtypeStruct((rows, vd), bf)
    ds, vs = row_spec(D), row_spec(vd)
    ws = (affine, w_a, u_h)
    remote = len(shards) > 0
    params = dict(collective_id=4, has_side_effects=True) if remote else {}
    fulls = [jax.ShapeDtypeStruct((4 * w.shape[0], w.shape[1]), bf) for w in shards]
    return pl.pallas_call(
        functools.partial(forward_kernel, rows // nseq, remote),
        grid=(rows // RT,),
        in_specs=[SMEM, ds, ds, ds] + [const_spec(w) for w in (*ws, *shards)],
        out_specs=[ds] * 4 + [vs] * 5 + [row_spec(SPAN), pl.BlockSpec((4, RT, zd), lambda i: (0, i, 0))]
        + [ANY] * len(shards),
        out_shape=[d_out] * 4 + [v_out] * 5
        + [jax.ShapeDtypeStruct((rows, SPAN), bf), jax.ShapeDtypeStruct((4, rows, zd), bf)] + fulls,
        scratch_shapes=[pltpu.VMEM((RT, vd), bf)] + (gather_sems(2, 2) if remote else []),
        compiler_params=pltpu.CompilerParams(vmem_limit_bytes=60 * 2**20, **params),
        name="forward_main",
    )(lengths, smooth, normed, tokens, *ws, *shards)


def ffn_kernel(packed, fs, middle, cot, gain, w_in, w_out, out_o, dm_o, dg_o, *rest):
    if packed:
        keep_a, give_a, keep_b, give_b, gwi, gwo, ascr, gscr = rest
    else:
        gwi, gwo, ascr, gscr = rest

    @pl.when(pl.program_id(0) == 0)
    def _():
        gwi[...] = jnp.zeros_like(gwi)
        gwo[...] = jnp.zeros_like(gwo)
        dg_o[...] = jnp.zeros_like(dg_o)

    m = middle[...].astype(f32)
    inv = lax.rsqrt(jnp.mean(m * m, axis=-1, keepdims=True) + eps)
    gn = lane_row(gain, 4 * NH + 1)
    mr = m * inv
    y = (mr * gn).astype(bf)
    cl = cot[...]
    for j in range(w_in.shape[1] // 256):
        c = slice(j * 256, (j + 1) * 256)
        pre = mm(y, w_in[:, c])
        sg = sigm(pre)
        act = pre * sg
        al = act.astype(bf)
        ascr[:, c] = al
        ga = mm_nt(cl, w_out[c, :])
        gf = (ga * (sg + act - act * sg)).astype(bf)
        gscr[:, c] = gf
        gwo[c, :] += mm_tn(al, cl)
        gwi[:, c] += mm_tn(y, gf)
    out_o[...] = (m + mm(ascr[...], w_out[...])).astype(bf)
    dy = mm_nt(gscr[...], w_in[...])
    dg_o[...] += jnp.sum((dy * mr).reshape(TT // 8, 8, m.shape[1]), axis=0)
    dyg = dy * gn
    inner = jnp.mean(dyg * mr, axis=-1, keepdims=True)
    dm_o[...] = (cl.astype(f32) + inv * (dyg - mr * inner)).astype(bf)
    if packed:
        @pl.when(pl.program_id(0) == pl.num_programs(0) - 1)
        def _():
            core = fs[0] % 2
            pack((gwo,), give_a, 1 - core)
            pack((gwo,), keep_a, core)
            pack((gwi,), give_b, 1 - core)
            pack((gwi,), keep_b, core)


def ffn_main(fs, middle, cot, gains, w_in, w_out, packed):
    rows, D = middle.shape
    ff = w_in.shape[1]
    ds = pl.BlockSpec((TT, D), lambda i: (i, 0))
    accs = [(D, ff), (ff, D)]
    pair = [jax.ShapeDtypeStruct((2, D * ff // 4 // LG, LG), bf)] * 4
    extra = pair if packed else [jax.ShapeDtypeStruct(s, f32) for s in accs]
    gain = jax.ShapeDtypeStruct((8, D), f32)
    return pl.pallas_call(
        functools.partial(ffn_kernel, packed),
        grid=(rows // TT,),
        in_specs=[SMEM, ds, ds] + [const_spec(w) for w in (gains, w_in, w_out)],
        out_specs=[ds, ds] + [const_spec(a) for a in [gain] + extra],
        out_shape=[jax.ShapeDtypeStruct((rows, D), bf)] * 2 + [gain] + extra,
        scratch_shapes=([pltpu.VMEM(s, f32) for s in accs] if packed else [])
        + [pltpu.VMEM((TT, ff), bf), pltpu.VMEM((TT, ff), bf)],
        compiler_params=pltpu.CompilerParams(vmem_limit_bytes=60 * 2**20),
        name="ffn_main",
    )(fs, middle, cot, gains, w_in, w_out)


def backward_kernel(qs, remote, dm, upd, u2, uh, gat, rv, a2, sm, val, vsl, pr, qk, nm, aff, u_h, *rest):
    rest = list(rest)

    def take(n):
        out = rest[:n]
        del rest[:n]
        return out

    if remote:
        keep_a, give_a, keep_b, give_b = take(4)
    dxd_o, gh_o, gu_o, gr_o, gv_o, gsp_o, ga_o = take(7)
    if remote:
        half_a_o, piece_b_o, near_c_o, near_d_o, keep_e_o, give_e_o = take(6)
    gz, gv, gr, gu, gh_w, guh = take(6)
    ascr, = take(1)
    step = pl.program_id(0)
    tiles = pl.num_programs(0) // 2
    if remote:
        core1, near1, mid1, z1, f1, s1, r1 = take(7)
        core2, near2, mid2, z2, s2, r2 = take(6)
        give3, core3, near3, s3, r3 = take(5)
        give4, core4, near4, s4, r4 = take(5)
        a = Reduce(qs[0], "y", s1, r1, keep=keep_a, give=give_a, core_in=core1, near=near1, mid=mid1, z_in=z1, full=f1)
        b = Reduce(qs[1], "x", s2, r2, keep=keep_b, give=give_b, core_in=core2, near=near2, mid=mid2, z_in=z2)
        c = Reduce(qs[2], "y", s3, r3, give=give3, core_in=core3, near=near3)
        d = Reduce(qs[3], "x", s4, r4, give=give4, core_in=core4, near=near4)
        core = a.fs % 2
        ra, rb, rd = a, b, d

    def slot(at, fn):
        if remote:
            pl.when(step == at)(fn)

    @pl.when(step == 0)
    def _():
        for o in (gz, gv, gr, gu, gh_w, guh, ga_o):
            o[...] = jnp.zeros_like(o)

    def open_up():
        greet(fsdp_peers()[:2] + dp_peers())
        met(9)
        a.start("core")
        b.start("core")

    slot(0, open_up)

    def at_one():
        a.to_near()
        b.to_near()

    slot(1, at_one)

    def send_core(chunk, accs):
        pack(accs, chunk.give, 1 - core)
        chunk.start("core")

    def send_near(chunk, accs):
        chunk.wait("core")
        pack_add(accs, chunk.core_in, core)
        chunk.start("near")

    def at_four():
        send_core(c, (gr, gh_w))
        send_core(d, (guh, gu))

    slot(tiles, at_four)
    slot(tiles + 1, lambda: send_near(c, (gr, gh_w)))
    slot(tiles + 3, lambda: a.back())

    @pl.when(step < tiles)
    def _():
        vd = u_h.shape[0]
        d = dm[...].astype(f32)
        gh = (d * uh[...].astype(f32)).astype(bf)
        gu_l = (d * u2[...].astype(f32)).astype(bf)
        gh_o[...] = gh
        gu_o[...] = gu_l
        dxd_o[...] = (d - d * upd[...].astype(f32)).astype(bf)
        s = sm[...]
        gh_w[...] += mm_tn(s, gh)
        gu[...] += mm_tn(s, gu_l)

        def onward():
            ra.to_next()
            rb.to_next()

        slot(3, onward)
        at = pl.ds(pl.multiple_of(step * RT, RT), RT)
        for j in range(vd // 256):
            c = slice(j * 256, (j + 1) * 256)
            dg = mm_nt(gh, u_h[c, :])
            gr_l = (dg * a2[:, c].astype(f32)).astype(bf)
            gr_o[:, c] = gr_l
            ascr[at, c] = (dg * rv[:, c].astype(f32)).astype(bf)
            guh[c, :] += mm_tn(gat[:, c], gh)
            gr[:, c] += mm_tn(s, gr_l)

    @pl.when(step >= tiles)
    def _():
        vd = u_h.shape[0]
        zd = aff.shape[1]
        scale = zd ** -0.5
        gsp = []
        sums = [0.0] * 4
        for b in range(RT // SPAN):
            r = slice(b * SPAN, (b + 1) * SPAN)
            p = pr[r, :]
            pf = p.astype(f32)
            ga = ascr[pl.ds(pl.multiple_of((step - tiles) * RT + b * SPAN, SPAN), SPAN), :]
            dp = mm_nt(ga, val[r, :])
            inner = jnp.sum(dp * pf, axis=-1, keepdims=True)
            gs = (pf * (dp - inner)).astype(bf)
            dq = mm(gs, qk[1, r, :]) * scale
            dk = mm_tn(gs, qk[0, r, :]) * scale
            sh = qk[2, r, :].astype(f32)
            for i, t in enumerate((dq * sh, dq, dk * sh, dk)):
                sums[i] = sums[i] + jnp.sum(t.reshape(SPAN // 8, 8, zd), axis=0)
            gsp.append(((dq * aff[0:1, :] + dk * aff[2:3, :]) * qk[3, r, :].astype(f32)).astype(bf))
            dv = mm_tn(p, ga)
            gv_o[r, :] = (dv * vsl[r, :].astype(f32)).astype(bf)
        for i in range(4):
            ga_o[i] += sums[i]
        gsp = jnp.concatenate(gsp, axis=0)

        def middle():
            ra.to_z()
            rb.to_z()

        slot(tiles, middle)
        slot(tiles + 1, lambda: send_near(rd, (guh, gu)))
        gsp_o[...] = gsp
        gz[...] += mm_tn(sm[...], gsp)
        n = nm[...]
        for j in range(vd // 256):
            c = slice(j * 256, (j + 1) * 256)
            gv[:, c] += mm_tn(n, gv_o[:, c])

    def close():
        pack((gv, gz), give_e_o, 1 - core)
        pack((gv, gz), keep_e_o, core)
        c.add_near()
        near_c_o[...] = near3[...]
        d.add_near()
        near_d_o[...] = near4[...]
        a.wait("back_z")
        half_a_o[...] = f1[a.half(a.x), :]
        piece_b_o[...] = b.add_z()

    slot(2 * tiles - 1, close)


def backward_main(dm, saved, smooth, normed, affine, u_h, chunks=None):
    rows, D = dm.shape
    vd = u_h.shape[0]
    zd = affine.shape[1]
    remote = chunks is not None
    tiles = rows // RT
    upd, u2, uh, val, vsl, gat, rv, a2, pr, qk = saved

    def early(width):
        return pl.BlockSpec((RT, width), lambda i: (jnp.minimum(i, tiles - 1), 0))

    def late(width):
        return pl.BlockSpec((RT, width), lambda i: (jnp.maximum(i - tiles, 0), 0))

    de, ve, vl, dl = early(D), early(vd), late(vd), late(D)
    accs = [(D, zd), (D, vd), (D, vd), (D, D), (D, D), (vd, D)]
    ga = jax.ShapeDtypeStruct((4, 8, zd), f32)
    both = pl.BlockSpec((RT, D), lambda i: (i % tiles, 0))
    ins = [(dm, de), (upd, de), (u2, de), (uh, de), (gat, ve), (rv, ve), (a2, ve), (smooth, both),
           (val, vl), (vsl, vl), (pr, late(SPAN)),
           (qk, pl.BlockSpec((4, RT, zd), lambda i: (0, jnp.maximum(i - tiles, 0), 0))), (normed, dl),
           (affine, const_spec(affine)), (u_h, const_spec(u_h))]
    wide = lambda n: jax.ShapeDtypeStruct((rows, n), bf)
    outs = [(wide(D), de), (wide(D), de), (wide(D), de), (wide(vd), ve), (wide(vd), vl), (wide(zd), late(zd)),
            (ga, const_spec(ga))]
    scratch = [pltpu.VMEM((rows, vd), bf)]
    comm = {}
    qs = ()
    if remote:
        n = [chunks[0].shape[1], chunks[2].shape[1], (D * vd + D * D) // 4 // LG, (vd * D + D * D) // 4 // LG,
             (D * vd + D * zd) // 4 // LG]
        qs = [a // 8 for a in n]
        ins += [(c, const_spec(c)) for c in chunks]
        buf = lambda *s: jax.ShapeDtypeStruct(s + (LG,), bf)
        outs += [(s, const_spec(s)) for s in (buf(n[0] // 2), buf(qs[1]), buf(n[2]), buf(2, n[3] // 2), buf(2, n[4]),
                                              buf(2, n[4]))]
        v = lambda *s: pltpu.VMEM(s + (LG,), bf)
        sem = pltpu.SemaphoreType.DMA((11,))
        scratch = [pltpu.VMEM(a, f32) for a in accs] + scratch
        scratch += [v(2, n[0]), v(n[0]), v(n[0] // 2), v(3, qs[0]), v(n[0]), sem, sem,
                    v(2, n[1]), v(2, n[1] // 2), v(n[1] // 2), v(3, qs[1]), sem, sem,
                    v(2, n[2]), v(2, n[2]), v(n[2]), sem, sem,
                    v(2, n[3]), v(2, n[3]), v(2, n[3] // 2), sem, sem]
        comm = dict(collective_id=2, has_side_effects=True)
    else:
        outs += [(s, const_spec(s)) for s in (jax.ShapeDtypeStruct(a, f32) for a in accs)]
    return pl.pallas_call(
        functools.partial(backward_kernel, qs, remote),
        grid=(2 * tiles,),
        in_specs=[i[1] for i in ins],
        out_specs=[o[1] for o in outs],
        out_shape=[o[0] for o in outs],
        scratch_shapes=scratch,
        compiler_params=pltpu.CompilerParams(vmem_limit_bytes=62 * 2**20, **comm),
        name="backward_main",
    )(*[i[0] for i in ins])


def lane_row(small, row):
    return jnp.concatenate([small[q, row:row + 1, :] for q in range(small.shape[0])], axis=1)


def input_kernel(nseq, seqlen, qs, remote, gh, gu, gr, gsp, gv, w_a, tok, small, dft, xs_i, ks_i, *rest):
    rest = list(rest)

    def take(n):
        out = rest[:n]
        del rest[:n]
        return out

    if remote:
        half_a, piece_b, near_c, near_d, keep_e, give_e, gain1, aff = take(8)
        dn_o, full_a, full_b, full_c, full_d, full_e, small_o = take(7)
    else:
        dn_o, dema_o, dgain_o = take(3)
    dsm, dn, xr, dyspec, dxspec, gspec, dkscr = take(7)
    step = pl.program_id(0)
    ng = dsm.shape[0]
    tiles = pl.num_programs(0) - ng
    nch = seqlen // CH
    rows = nseq * seqlen
    if remote:
        f0, s0, r0 = take(3)
        f1, s1, r1 = take(3)
        mid2, z2, f2, s2, r2 = take(5)
        mid3, z3, f3, s3, r3 = take(5)
        core4, near4, mid4, z4, f4, s4, r4 = take(7)
        sums, near, total, far, s5, r5, gains = take(7)
        a_ = Reduce(qs[0], "y", s0, r0, full=f0)
        b_ = Reduce(qs[1], "x", s1, r1, full=f1)
        c_ = Reduce(qs[2], "y", s2, r2, near=near_c, mid=mid2, z_in=z2, full=f2)
        d_ = Reduce(qs[3], "x", s3, r3, near=near_d, mid=mid3, z_in=z3, full=f3)
        e_ = Reduce(qs[4], "y", s4, r4, keep=keep_e, give=give_e, core_in=core4, near=near4, mid=mid4, z_in=z4, full=f4)

    def slot(at, fn):
        if remote:
            pl.when(step == at)(fn)

    def open_up():
        greet(fsdp_peers() + dp_peers())
        f0[a_.half(a_.x), :] = half_a[...]
        f1[b_.own_piece(), :] = piece_b[...]
        met(10)
        c_.start("next")
        d_.start("next")
        e_.start("core")
        b_.start("back_z")

    slot(0, open_up)

    def at_one():
        e_.to_near()
        a_.start("back_x")

    slot(1, at_one)

    def at_two():
        c_.to_z()

    slot(2, at_two)
    def at_three():
        d_.to_z()
        b_.widen()

    slot(3, at_three)

    @pl.when(step < tiles)
    def _():
        w_z, w_r, w_u, w_h, w_v = split_pack(w_a)
        at = pl.ds(pl.multiple_of(step * RT, RT), RT)
        x = tok[...].astype(f32)
        n = (x * lax.rsqrt(jnp.mean(x * x, axis=-1, keepdims=True) + eps)).astype(bf)
        a = mm_nt(gv[...], w_v[...])
        b = mm_nt(gh[...], w_h[...]) + mm_nt(gu[...], w_u[...]) + mm_nt(gsp[...], w_z[...]) + mm_nt(gr[...], w_r[...])
        for q in range(ng):
            c = slice(q * LG, (q + 1) * LG)
            xr[q, at, :] = n[:, c]
            dn[q, at, :] = a[:, c].astype(bf)
            dsm[q, at, :] = b[:, c].astype(bf)

    @pl.when(step >= tiles)
    def _():
        g = step - tiles

        slot(tiles + 1, lambda: e_.to_z())
        slot(tiles + 2, lambda: c_.widen())
        slot(tiles + 3, lambda: d_.widen())
        fwd = dft[:2 * CH, CH:]
        inv = dft[3 * CH:]
        for c in range(0, nseq * nch, 2):
            dy = mm(fwd, jnp.concatenate([dsm[g, c * CH:(c + 1) * CH, :], dsm[g, (c + 1) * CH:(c + 2) * CH, :]], axis=1))
            dyspec[c] = dy[:, :LG]
            dyspec[c + 1] = dy[:, LG:]

        def a_second():
            e_.to_next()
            a_.wait("back_x")
            full_a[...] = f0[...]
            b_.wait("back_x")
            full_b[...] = f1[...]
            c_.back()

        slot(tiles, a_second)
        slot(tiles + 1, lambda: d_.back())
        slot(tiles + 2, lambda: e_.back())
        slot(tiles + 3, lambda: e_.widen())

        def point(i, _):
            rc = pl.ds(pl.multiple_of(i * 16, 16), 16)
            rs = pl.ds(pl.multiple_of(CH + i * 16, 16), 16)
            kc = [ks_i[d, rc, :].astype(f32) for d in range(nch)]
            ks = [ks_i[d, rs, :].astype(f32) for d in range(nch)]
            gc = [0.] * nch
            gs = [0.] * nch
            for b in range(nseq):
                dc = [dyspec[b * nch + c, rc, :] for c in range(nch)]
                ds = [dyspec[b * nch + c, rs, :] for c in range(nch)]
                for c in range(nch):
                    oc = 0.
                    os = 0.
                    for d in range(nch - c):
                        oc = oc + kc[d] * dc[c + d] + ks[d] * ds[c + d]
                        os = os + kc[d] * ds[c + d] - ks[d] * dc[c + d]
                    dxspec[b * nch + c, rc, :] = oc.astype(bf)
                    dxspec[b * nch + c, rs, :] = os.astype(bf)
                for c in range(nch):
                    xc = xs_i[b * nch + c, rc, :].astype(f32)
                    xs = xs_i[b * nch + c, rs, :].astype(f32)
                    for d in range(nch - c):
                        gc[d] = gc[d] + xc * dc[c + d] + xs * ds[c + d]
                        gs[d] = gs[d] + xc * ds[c + d] - xs * dc[c + d]
            for d in range(nch):
                gspec[d, rc, :] = gc[d].astype(bf)
                gspec[d, rs, :] = gs[d].astype(bf)
            return 0

        lax.fori_loop(0, CH // 16, point, 0)
        dgain = 0.
        for c in range(0, nseq * nch, 2):
            both = mm(inv, jnp.concatenate([dxspec[c], dxspec[c + 1]], axis=1))
            for i in range(2):
                r = slice((c + i) * CH, (c + i + 1) * CH)
                t = both[:, i * LG:(i + 1) * LG] + dn[g, r, :].astype(f32)
                dn_o[0, r, :] = t.astype(bf)
                dgain = dgain + jnp.sum((t * xr[g, r, :].astype(f32)).reshape(CH // 8, 8, LG), axis=0)
        whole = dft[2 * CH:]
        for d in range(0, nch, 2):
            dk = mm(whole, jnp.concatenate([gspec[d], gspec[d + 1]], axis=1)) * (1.0 / CH)
            if d:
                dkscr[(d - 1) * CH:d * CH, :] += dk[:CH, :LG]
            dkscr[d * CH:(d + 1) * CH, :] = dk[CH:, :LG] + dk[:CH, LG:]
            dkscr[(d + 1) * CH:(d + 2) * CH, :] = dk[CH:, LG:]
        p = [small[g, i * NH:(i + 1) * NH, :] for i in range(4)]
        a, gg, ex, ro, keep = ema_rates(p)
        p8 = power_of(keep, 8)
        st = [jnp.broadcast_to(p8[h:h + 1, :], (8, LG)) for h in range(NH)]

        def horner(i, ab):
            A, B = ab
            v = dkscr[pl.ds(pl.multiple_of(seqlen - 8 - i * 8, 8), 8), :]
            B = tuple(B[h] * st[h] + A[h] for h in range(NH))
            A = tuple(A[h] * st[h] + v for h in range(NH))
            return (A, B)

        none = dkscr[0:8, :] * 0.0
        zero = (none,) * NH
        A, B = lax.fori_loop(0, seqlen // 8, horner, (zero, zero), unroll=8)
        rr = lax.broadcasted_iota(jnp.int32, (8, LG), 0).astype(f32)
        As = []
        Bs = []
        for h in range(NH):
            lad = ladder(keep[h:h + 1, :], 8)
            low = jnp.concatenate([jnp.zeros((1, LG), f32), lad[:7]], axis=0)
            As.append(jnp.sum(lad * A[h], axis=0, keepdims=True))
            Bs.append(jnp.sum(rr * low * A[h] + 8.0 * lad[7:8] * lad * B[h], axis=0, keepdims=True))
        As = jnp.concatenate(As, axis=0)
        Bs = jnp.concatenate(Bs, axis=0)
        dkeep = a * ex * ro * Bs
        da = ex * ro * As - gg * dkeep
        dg = -a * dkeep
        grads = (da * a * (1.0 - a), dg * gg * (1.0 - gg), a * ro * As, a * ex * As)
        for i, v in enumerate(grads):
            if remote:
                sums[g, i * NH:(i + 1) * NH, :] = v.astype(bf)
            else:
                dema_o[i] = v
        if remote:
            gains[g, 0:1, :] = jnp.sum(dgain, axis=0, keepdims=True)
        else:
            dgain_o[...] = dgain

    def close():
        fs = lax.axis_index("fsdp")

        def across(k, src, dst, peer):
            return pltpu.make_async_remote_copy(src_ref=src, dst_ref=dst, send_sem=s5.at[k], recv_sem=r5.at[k],
                                                device_id=peer, device_id_type=MESH)

        g1 = jnp.sum(gain1[...], axis=0, keepdims=True)
        cols = jnp.sum(aff[...], axis=1)
        for q in range(ng):
            sums[q, 4 * NH:, :] = jnp.concatenate(
                [gains[q, 0:1, :], g1[:, q * LG:(q + 1) * LG], cols, jnp.zeros((SMALL - 4 * NH - 6, LG), f32)],
                axis=0).astype(bf)
        first = [across(k, sums.at[peer[1]], near.at[k], peer) for k, peer in enumerate(fsdp_peers())]
        for c in first:
            c.start()
        for c in first:
            c.wait()
        t = sums[fs].astype(f32)
        for k in range(3):
            t = t + near[k].astype(f32)
        total[...] = t.astype(bf)
        second = [across(3 + k, total, far.at[k], peer) for k, peer in enumerate(dp_peers())]
        for c in second:
            c.start()
        c_.wait("back_x")
        full_c[...] = f2[...]
        d_.wait("back_x")
        full_d[...] = f3[...]
        for c in second:
            c.wait()
        for k in range(7):
            t = t + far[k].astype(f32)
        small_o[...] = t
        e_.wait("back_x")
        full_e[...] = f4[...]

    slot(tiles + ng - 1, close)


def input_main(grads, w_a, tokens, small, dft, xspec, kspec, nseq, comm_in=None):
    rows, D = tokens.shape
    seqlen = rows // nseq
    nch = seqlen // CH
    ng = D // LG
    nchunks = nseq * nch
    tiles = rows // RT
    remote = comm_in is not None

    def early(a):
        return pl.BlockSpec((RT, a.shape[1]), lambda i: (jnp.minimum(i, tiles - 1), 0))

    def lanes(i):
        return jnp.maximum(i - tiles, 0)

    ins = [(a, early(a)) for a in grads] + [(w_a, const_spec(w_a)), (tokens, early(tokens)), (small, const_spec(small))]
    ins += [(dft, const_spec(dft)), (xspec, pl.BlockSpec((nchunks, 2 * CH, LG), lambda i: (0, 0, lanes(i)))),
            (kspec, pl.BlockSpec((nch, 2 * CH, LG), lambda i: (0, 0, lanes(i))))]
    outs = [(jax.ShapeDtypeStruct((ng, rows, LG), bf), pl.BlockSpec((1, rows, LG), lambda i: (lanes(i), 0, 0)))]
    scratch = [pltpu.VMEM((ng, rows, LG), bf)] * 3
    scratch += [pltpu.VMEM((nchunks, 2 * CH, LG), f32),
                pltpu.VMEM((nchunks, 2 * CH, LG), bf), pltpu.VMEM((nch, 2 * CH, LG), bf), pltpu.VMEM((seqlen, LG), f32)]
    params = {}
    qs = ()
    if remote:
        half_a, piece_b, near_c, near_d, keep_e, *_ = comm_in
        n = [half_a.shape[0] * 2, piece_b.shape[0] * 8, near_c.shape[0], near_d.shape[1] * 2, keep_e.shape[1]]
        qs = [a // 8 for a in n]
        ins += [(a, const_spec(a)) for a in comm_in]
        fulls = [jax.ShapeDtypeStruct((a, LG), bf) for a in n]
        one = jax.ShapeDtypeStruct((SMALL, LG), bf)
        outs += [(a, const_spec(a)) for a in fulls + [jax.ShapeDtypeStruct(one.shape, f32)]]
        v = lambda *s: pltpu.VMEM(s + (LG,), bf)
        w = lambda *s: pltpu.VMEM(s + one.shape, bf)
        sem = pltpu.SemaphoreType.DMA((11,))
        scratch += [v(n[0]), sem, sem, v(n[1]), sem, sem,
                    v(n[2] // 2), v(3, qs[2]), v(n[2]), sem, sem,
                    v(n[3] // 2), v(3, qs[3]), v(n[3]), sem, sem,
                    v(2, n[4]), v(n[4]), v(n[4] // 2), v(3, qs[4]), v(n[4]), sem, sem,
                    w(4), w(3), w(), w(7), sem, sem, pltpu.VMEM((ng, 8, LG), f32)]
        params = dict(collective_id=3, has_side_effects=True)
    else:
        outs += [(jax.ShapeDtypeStruct((4, NH, D), f32), pl.BlockSpec((4, NH, LG), lambda i: (0, 0, lanes(i)))),
                 (jax.ShapeDtypeStruct((8, D), f32), pl.BlockSpec((8, LG), lambda i: (0, lanes(i))))]
    return pl.pallas_call(
        functools.partial(input_kernel, nseq, seqlen, qs, remote),
        grid=(tiles + ng,),
        in_specs=[i[1] for i in ins],
        out_specs=[o[1] for o in outs],
        out_shape=[o[0] for o in outs],
        scratch_shapes=scratch,
        compiler_params=pltpu.CompilerParams(vmem_limit_bytes=62 * 2**20, **params),
        name="input_main",
    )(*[i[0] for i in ins])


def finish_kernel(groups, fs, tok, dxd, dn, small, *rest):
    n = len(groups)
    fulls, sums = rest[:n], rest[n:n + 1]
    outs = list(rest[n + 1:] if groups else rest)
    dtok_o = outs.pop(0)
    x = tok[...].astype(f32)
    inv = lax.rsqrt(jnp.mean(x * x, axis=-1, keepdims=True) + eps)
    d = jnp.concatenate([dn[q] for q in range(dn.shape[0])], axis=1).astype(f32) * lane_row(small, 4 * NH)
    xr = x * inv
    dtok_o[...] = (dxd[...].astype(f32) + inv * (d - xr * jnp.mean(d * xr, axis=-1, keepdims=True))).astype(bf)
    if groups:
        @pl.when(pl.program_id(0) == 0)
        def _():
            gain_o, ema_o, aff_o = outs[:3]
            t = sums[0]
            gain_o[...] = t[4 * NH:4 * NH + 2, :]
            for i in range(4):
                ema_o[i] = t[i * NH:(i + 1) * NH, :]
            width = aff_o.shape[1]
            mine = 0.
            for q in range(4):
                mine = mine + jnp.where(fs[0] == q, 1.0, 0.0) * t[4 * NH + 2:4 * NH + 6, q * width:(q + 1) * width]
            aff_o[...] = mine

        at = 3
        for i, (full, count) in enumerate(zip(fulls, groups)):
            @pl.when(pl.program_id(0) == i % 2)
            def _(full=full, at=at, count=count):
                unpack(full, outs[at:at + count])
            at += count


def finish_main(fs, tokens, dxd, dn, small, fulls=(), sums=None, groups=(), shapes=()):
    rows, D = tokens.shape
    ng = dn.shape[0]
    tile = min(2 * RT, rows)
    ds = pl.BlockSpec((tile, D), lambda i: (i, 0))
    extra = list(fulls) + ([sums] if groups else [])
    outs = [jax.ShapeDtypeStruct(s, f32) for s in shapes]
    return pl.pallas_call(
        functools.partial(finish_kernel, groups),
        grid=(rows // tile,),
        in_specs=[SMEM, ds, ds, pl.BlockSpec((ng, tile, LG), lambda i: (0, i, 0))] + [const_spec(a) for a in [small] + extra],
        out_specs=[ds] + [const_spec(a) for a in outs],
        out_shape=[jax.ShapeDtypeStruct((rows, D), bf)] + outs,
        compiler_params=pltpu.CompilerParams(vmem_limit_bytes=60 * 2**20),
        name="finish",
    )(fs, tokens, dxd, dn, small, *extra)


def local_step(tokens, lengths, cotangent, fs, plain=None, shards=None):
    nseq = lengths.shape[0]
    rows, D = tokens.shape
    dft = jnp.asarray(dft_tables(), bf)
    remote = shards is not None
    if remote:
        ema_t, norm_gains, qk_affine, w_z, w_r, w_u, w_h, w_v, u_h, w_in, w_out = shards
        normed, smooth, x_spec, k_spec, small, affine, w_a, u_full = ema_forward(
            tokens, dft, nseq, comm_in=(ema_t, norm_gains, qk_affine, w_z, w_r, w_u, w_h, w_v, u_h))
        *saved, in_full, out_full = forward_main(
            lengths, smooth, normed, tokens, affine, w_a, u_full, (w_in, w_out))
    else:
        small, affine, w_a, u_full, in_full, out_full = plain
        normed, smooth, x_spec, k_spec = ema_forward(tokens, dft, nseq, small)
        saved = forward_main(lengths, smooth, normed, tokens, affine, w_a, u_full)
    middle, *saved = saved
    output, dm, g_gain1, *first = ffn_main(fs, middle, cotangent, small, in_full, out_full, remote)
    dxd, gh, gu, gr, gv, gsp, g_aff, *second = backward_main(
        dm, saved, smooth, normed, affine, u_full, first if remote else None)
    shared = ((gh, gu, gr, gsp, gv), w_a, tokens, small, dft, x_spec, k_spec, nseq)
    if not remote:
        dn, g_ema, g_gain0 = input_main(*shared)
        grad_tokens, = finish_main(fs, tokens, dxd, dn, small)
        grad_gains = jnp.stack([jnp.sum(g_gain0, axis=0), jnp.sum(g_gain1, axis=0)])
        return output, grad_tokens, (grad_gains, jnp.swapaxes(g_ema, 1, 2), jnp.sum(g_aff, axis=1), *second, *first)
    dn, *fulls, sums = input_main(*shared, (*second, g_gain1, g_aff))
    shapes = [norm_gains.shape, ema_t.shape, qk_affine.shape]
    shapes += [w.shape for w in (w_out, w_in, w_r, w_h, u_h, w_u, w_v, w_z)]
    grad_tokens, g_gains, g_ema, g_aff, g_out, g_in, g_r, g_h, g_uh, g_u, g_v, g_z = finish_main(
        fs, tokens, dxd, dn, small, fulls, sums, (1, 1, 2, 2, 2), shapes)
    return output, grad_tokens, (g_gains, jnp.swapaxes(g_ema, 1, 2), g_aff, g_z, g_v, g_r, g_u, g_h, g_uh, g_in, g_out)


def small_table(norm_gains, ema_params):
    d = norm_gains.shape[1]
    ema = jnp.swapaxes(ema_params, 1, 2).reshape(4 * NH, d)
    rows = jnp.concatenate([ema, norm_gains, jnp.zeros((SMALL - 4 * NH - 2, d), bf)], axis=0).astype(f32)
    return jnp.swapaxes(rows.reshape(SMALL, d // LG, LG), 0, 1)


def per_device(tokens, lengths, norm_gains, ema_params, qk_affine, w_z, w_v, w_r, w_u, w_h, u_h, w_in, w_out, cotangent):
    at = lax.axis_index("fsdp")
    parts = lax.axis_size("fsdp")
    fs = at.reshape(1)
    if parts == 4 and lax.axis_size("dp") == 8:
        shards = (jnp.swapaxes(ema_params, 1, 2), norm_gains, qk_affine, w_z, w_r, w_u, w_h, w_v, u_h, w_in, w_out)
        output, grad_tokens, pieces = local_step(tokens, lengths, cotangent, fs, shards=shards)
        return (output, grad_tokens) + pieces
    gather = lambda w, axis: lax.all_gather(w, "fsdp", axis=axis, tiled=True)
    w_a = gather(jnp.concatenate([w_z, w_r, w_u, w_h, w_v], axis=1), 0)
    plain = (small_table(gather(norm_gains, 1), gather(ema_params, 1)), gather(qk_affine, 1).astype(f32), w_a,
             gather(u_h, 0), gather(w_in, 0), gather(w_out, 0))
    output, grad_tokens, totals = local_step(tokens, lengths, cotangent, fs, plain)
    summed = lax.psum(totals, ("dp", "fsdp"))
    pieces = tuple(
        lax.dynamic_slice_in_dim(g, at * (g.shape[d] // parts), g.shape[d] // parts, d)
        for g, d in zip(summed, (1, 1, 1, 0, 0, 0, 0, 0, 0, 0, 0)))
    return (output, grad_tokens) + pieces


def solution(mesh):
    rows = P(("dp", "fsdp"), None)
    shard = P("fsdp", None)
    wide = P(None, "fsdp")
    deep = P(None, "fsdp", None)
    return jax.shard_map(
        per_device,
        mesh=mesh,
        in_specs=(rows, P(("dp", "fsdp")), wide, deep, wide) + (shard,) * 8 + (rows,),
        out_specs=(rows, rows, wide, deep, wide) + (shard,) * 8,
        check_vma=False,
    )
```

```python
import functools

import jax
import jax.numpy as jnp
import numpy as np
from jax import lax
from jax.experimental import pallas as pl
from jax.experimental.pallas import tpu as pltpu
from jax.sharding import PartitionSpec as P

bf = jnp.bfloat16
f32 = jnp.float32
SPAN = 128
CH = 256
NH = 16
LG = 128
eps = 1e-6


def dft_tables():
    f=np.arange(CH)[:,None]+0.5
    m=np.arange(-CH,CH)[None,:]
    ang=2*np.pi*f*m/(2*CH)
    both=np.concatenate([np.cos(ang),np.sin(ang)],axis=0)
    return np.concatenate([both,both.T],axis=0).astype(np.float32)

def mm(a,b): return jnp.dot(a,b,preferred_element_type=f32)
def mm_tn(a,b): return lax.dot_general(a,b,(((0,),(0,)),((),())),preferred_element_type=f32)
def mm_nt(a,b): return lax.dot_general(a,b,(((1,),(1,)),((),())),preferred_element_type=f32)

def ema_rates(p):
    a=jax.nn.sigmoid(p[0]); g=jax.nn.sigmoid(p[1])
    return a,g,p[2],p[3],1.0-a*g

def power_of(base, n):
    out=None
    sq=base
    while n:
        if n&1: out = sq if out is None else out*sq
        n>>=1
        if n: sq=sq*sq
    return out

def ladder(keep, width):
    r=lax.broadcasted_iota(jnp.int32,(width,keep.shape[-1]),0)
    acc=jnp.ones((width,keep.shape[-1]),f32)
    sq=keep
    bit=1
    while bit<width:
        acc=acc*jnp.where((r&bit)!=0, sq, 1.0)
        sq=sq*sq
        bit*=2
    return acc

MESH = pl.DeviceIdType.MESH


def flip(i, bit):
    return i + bit - 2 * bit * ((i // bit) % 2)


def const_spec(a):
    nd = len(a.shape)
    return pl.BlockSpec(a.shape, lambda i: (0,) * nd, pipeline_mode=pl.Buffered(1))


ANY = pl.BlockSpec(memory_space=pl.ANY)


class Gather:
    def __init__(self, shards, outs, pieces, send, recv, local):
        self.shards, self.outs, self.pieces = shards, outs, pieces
        self.send, self.recv, self.local = send, recv, local
        self.dp = lax.axis_index("dp")
        self.fs = lax.axis_index("fsdp")
        self.x = self.dp % 2
        self.z = (self.dp // 2) % 2
        self.core_peer = (self.dp, flip(self.fs, 1))
        self.y_peer = (self.dp, flip(self.fs, 2))
        self.x_peer = (flip(self.dp, 1), self.fs)
        self.z_peer = (flip(self.dp, 2), self.fs)

    def peers(self):
        return [self.core_peer, self.y_peer, self.x_peer, self.z_peer]

    def copy(self, p, k):
        a, col, width = self.pieces[p]
        shard, out = self.shards[a], self.outs[a]
        n = shard.shape[0]
        far = flip(self.fs, 2) * n
        cols = pl.ds(col, width)
        x, z = self.x, self.z

        def at(ref, base, zz, xx, half=None):
            r = n // 4 if half is None else n // 8
            row = base + (2 * zz + xx) * (n // 4) + (0 if half is None else half * r)
            return ref.at[pl.ds(pl.multiple_of(row, r), r), cols]

        src, dst, peer = (
            (at(shard, 0, z, x), at(out, self.fs * n, z, x), self.y_peer),
            (at(out, far, z, x),) * 2 + (self.x_peer,),
            (at(out, far, z, x),) * 2 + (self.z_peer,),
            (at(out, far, 1 - z, x, 0),) * 2 + (self.x_peer,),
            (at(out, far, z, 1 - x, 1),) * 2 + (self.z_peer,),
            (at(out, far, z, x),) * 2 + (self.core_peer,),
            (at(out, far, z, 1 - x),) * 2 + (self.core_peer,),
            (at(out, far, 1 - z, x),) * 2 + (self.core_peer,),
            (at(out, far, 1 - z, 1 - x),) * 2 + (self.core_peer,),
        )[k]
        return pltpu.make_async_remote_copy(
            src_ref=src, dst_ref=dst, send_sem=self.send.at[9 * p + k], recv_sem=self.recv.at[9 * p + k],
            device_id=peer, device_id_type=MESH)

    def whole(self, a):
        n = self.shards[a].shape[0]
        slot = 9 * len(self.pieces) + a
        return pltpu.make_async_remote_copy(
            src_ref=self.shards[a], dst_ref=self.outs[a].at[pl.ds(pl.multiple_of(self.fs * n, n), n)],
            send_sem=self.send.at[slot], recv_sem=self.recv.at[slot], device_id=self.core_peer, device_id_type=MESH)

    def own(self, a):
        n = self.shards[a].shape[0]
        mine = pl.ds(pl.multiple_of(self.fs * n, n), n)
        return pltpu.make_async_copy(self.shards[a], self.outs[a].at[mine], self.local.at[a])

    def begin(self):
        for p in range(len(self.pieces)):
            self.copy(p, 0).start()
        for a in range(len(self.shards)):
            self.whole(a).start()
            self.own(a).start()

    def relay(self, p):
        self.copy(p, 0).wait_recv()
        for k in (1, 2, 5):
            self.copy(p, k).start()

    def cross(self, p):
        self.copy(p, 2).wait_recv()
        self.copy(p, 3).start()
        self.copy(p, 7).start()
        self.copy(p, 1).wait_recv()
        self.copy(p, 4).start()
        self.copy(p, 6).start()

    def last(self, p):
        self.copy(p, 3).wait_recv()
        self.copy(p, 4).wait_recv()
        self.copy(p, 8).start()

    def finish(self):
        for p in range(len(self.pieces)):
            for k in range(9):
                self.copy(p, k).wait_send()
            for k in (5, 6, 7, 8):
                self.copy(p, k).wait_recv()
        for a in range(len(self.shards)):
            self.whole(a).wait()
            self.own(a).wait()


def gather_sems(arrays, pieces):
    sem = pltpu.SemaphoreType.DMA((9 * pieces + arrays,))
    return [sem, sem, pltpu.SemaphoreType.DMA((arrays,))]


SMALL = 4 * NH + 16
PIECES = 3


def ema_fwd_kernel(nseq, seqlen, remote, tok, dft, *rest):
    rest = list(rest)

    def take(n):
        out = rest[:n]
        del rest[:n]
        return out

    g = pl.program_id(0)
    nch = seqlen // CH
    rows = nseq * seqlen
    if remote:
        ema_i, gain_i, aff_i, *parts = take(9)
    else:
        small, = take(1)
    normed_o, smooth_o, xs_o, ks_o = take(4)
    if remote:
        small_o, aff_o, w_full, u_full = take(4)
    nscr, kscr, kspec, xspec, yspec = take(5)
    if remote:
        small, sent, own, s1, r1, *sems = take(8)
        fs = lax.axis_index("fsdp")
        gather = Gather((own, parts[5]), (w_full, u_full),
                        ((0, 0, 1664), (0, 1664, own.shape[1] - 1664), (1, 0, parts[5].shape[1])), *sems)
        across = [pltpu.make_async_remote_copy(
            src_ref=sent.at[fs], dst_ref=sent.at[fs], send_sem=s1.at[k], recv_sem=r1.at[k],
            device_id=peer, device_id_type=MESH) for k, peer in enumerate(fsdp_peers())]

    def slot(at, fn):
        if remote:
            pl.when(g == at)(fn)

    def open_up():
        greet(fsdp_peers() + [gather.x_peer, gather.z_peer])
        for i in range(4):
            sent[fs, i * NH:(i + 1) * NH, :] = ema_i[i]
        tail = [gain_i[...].astype(f32), jnp.concatenate([aff_i[...].astype(f32)] * 4, axis=1),
                jnp.zeros((SMALL - 4 * NH - 6, LG), f32)]
        sent[fs, 4 * NH:, :] = jnp.concatenate(tail, axis=0).astype(bf)
        at = 0
        for w in parts[:5]:
            own[:, at:at + w.shape[1]] = w[...]
            at += w.shape[1]
        met(5)
        for c in across:
            c.start()
        gather.begin()

    slot(0, open_up)

    @pl.when(g == 0)
    def _():
        def body(i, _):
            r = pl.ds(pl.multiple_of(i * 256, 256), 256)
            x = tok[r, :].astype(f32)
            n = x * lax.rsqrt(jnp.mean(x * x, axis=-1, keepdims=True) + eps)
            for q in range(x.shape[1] // LG):
                nscr[q, r, :] = n[:, q * LG:(q + 1) * LG]
            return 0
        lax.fori_loop(0, rows // 256, body, 0)

    def settle():
        for c in across:
            c.wait()
        for q in range(4):
            small[q] = sent[q].astype(f32)
        small_o[...] = small[...]
        for q in range(4):
            n = aff_i.shape[1]
            aff_o[:, q * n:(q + 1) * n] = small[q, 4 * NH + 2:4 * NH + 6, 0:n]

    slot(0, settle)

    slot(1, lambda: gather.relay(1))
    slot(2, lambda: gather.cross(0))
    p = [small[g, i * NH:(i + 1) * NH, :] for i in range(4)]
    normed = (nscr[g] * small[g, 4 * NH:4 * NH + 1, :]).astype(bf)
    normed_o[...] = normed
    a, gg, ex, ro, keep = ema_rates(p)
    w = a * ex * ro * (1.0 / CH)
    step = power_of(keep, 16)
    z0 = []
    st = []
    for h in range(NH):
        z0.append(ladder(keep[h:h + 1, :], 16) * w[h:h + 1, :])
        st.append(jnp.broadcast_to(step[h:h + 1, :], (8, LG)))

    def kgen(i, zs):
        acc = list(zs)
        while len(acc) > 1:
            acc = [acc[j] + acc[j + 1] for j in range(0, len(acc), 2)]
        acc = acc[0]
        kscr[pl.ds(pl.multiple_of(CH + i * 16, 16), 16), :] = acc.astype(bf)
        return tuple(jnp.concatenate([zs[h][:8] * st[h], zs[h][8:] * st[h]], axis=0) for h in range(NH))

    lax.fori_loop(0, seqlen // 16, kgen, tuple(z0), unroll=4)
    kscr[0:CH, :] = jnp.zeros((CH, LG), bf)
    both = dft[:2 * CH]
    fwd = dft[:2 * CH, CH:]
    inv = dft[3 * CH:]
    for d in range(0, nch, 2):
        kd = mm(both, jnp.concatenate([kscr[d * CH:(d + 2) * CH, :], kscr[(d + 1) * CH:(d + 3) * CH, :]], axis=1))
        for i in range(2):
            kspec[d + i] = kd[:, i * LG:(i + 1) * LG]
            ks_o[d + i] = kd[:, i * LG:(i + 1) * LG].astype(bf)
    for c in range(0, nseq * nch, 2):
        xd = mm(fwd, jnp.concatenate([normed[c * CH:(c + 1) * CH], normed[(c + 1) * CH:(c + 2) * CH]], axis=1))
        for i in range(2):
            xspec[c + i] = xd[:, i * LG:(i + 1) * LG]
            xs_o[c + i] = xd[:, i * LG:(i + 1) * LG].astype(bf)

    slot(1, lambda: gather.relay(2))
    slot(2, lambda: gather.cross(1))
    slot(3, lambda: gather.last(0))

    def point(i, _):
        rc = pl.ds(pl.multiple_of(i * 16, 16), 16)
        rs = pl.ds(pl.multiple_of(CH + i * 16, 16), 16)
        kc = [kspec[d, rc, :] for d in range(nch)]
        ks = [kspec[d, rs, :] for d in range(nch)]
        for b in range(nseq):
            xc = [xspec[b * nch + c, rc, :] for c in range(nch)]
            xs = [xspec[b * nch + c, rs, :] for c in range(nch)]
            for c in range(nch):
                yc = 0.
                ys = 0.
                for d in range(c + 1):
                    yc = yc + kc[d] * xc[c - d] - ks[d] * xs[c - d]
                    ys = ys + kc[d] * xs[c - d] + ks[d] * xc[c - d]
                yspec[b * nch + c, rc, :] = yc.astype(bf)
                yspec[b * nch + c, rs, :] = ys.astype(bf)
        return 0

    lax.fori_loop(0, CH // 16, point, 0)
    slot(0, lambda: gather.relay(0))
    slot(2, lambda: gather.cross(2))
    slot(3, lambda: gather.last(1))
    for c in range(0, nseq * nch, 2):
        y = mm(inv, jnp.concatenate([yspec[c], yspec[c + 1]], axis=1)).astype(bf)
        smooth_o[c * CH:(c + 1) * CH, :] = y[:, :LG]
        smooth_o[(c + 1) * CH:(c + 2) * CH, :] = y[:, LG:]

    def close():
        gather.last(2)
        gather.finish()

    slot(3, close)


def ema_forward(tokens, dft, nseq, small=None, comm_in=None):
    rows, D = tokens.shape
    seqlen = rows // nseq
    nch = seqlen // CH
    ng = D // LG
    nchunks = nseq * nch
    remote = comm_in is not None
    col = pl.BlockSpec((rows, LG), lambda g: (0, g))
    ins = [tokens, dft] + (list(comm_in) if remote else [small])
    wide = jax.ShapeDtypeStruct((rows, D), bf)
    outs = [(wide, col), (wide, col),
            (jax.ShapeDtypeStruct((nchunks, 2 * CH, D), bf), pl.BlockSpec((nchunks, 2 * CH, LG), lambda g: (0, 0, g))),
            (jax.ShapeDtypeStruct((nch, 2 * CH, D), bf), pl.BlockSpec((nch, 2 * CH, LG), lambda g: (0, 0, g)))]
    scratch = [pltpu.VMEM((ng, rows, LG), f32), pltpu.VMEM((seqlen + CH, LG), bf), pltpu.VMEM((nch, 2 * CH, LG), f32),
               pltpu.VMEM((nchunks, 2 * CH, LG), f32), pltpu.VMEM((nchunks, 2 * CH, LG), bf)]
    params = {}
    if remote:
        n = sum(w.shape[1] for w in comm_in[3:8])
        u = comm_in[8]
        a = jax.ShapeDtypeStruct((4, SMALL, LG), f32)
        b = jax.ShapeDtypeStruct((4, 4 * comm_in[2].shape[1]), f32)
        outs += [(a, const_spec(a)), (b, const_spec(b)), (jax.ShapeDtypeStruct((D, n), bf), ANY),
                 (jax.ShapeDtypeStruct((4 * u.shape[0], D), bf), ANY)]
        sem = pltpu.SemaphoreType.DMA((3,))
        scratch += [pltpu.VMEM(a.shape, f32), pltpu.VMEM(a.shape, bf), pltpu.VMEM((D // 4, n), bf), sem, sem] + gather_sems(2, PIECES)
        params = dict(collective_id=1, has_side_effects=True)
    return pl.pallas_call(
        functools.partial(ema_fwd_kernel, nseq, seqlen, remote),
        grid=(ng,),
        in_specs=[const_spec(a) for a in ins],
        out_specs=[o[1] for o in outs],
        out_shape=[o[0] for o in outs],
        scratch_shapes=scratch,
        compiler_params=pltpu.CompilerParams(vmem_limit_bytes=60 * 2**20, **params),
        name="ema_fwd",
    )(*ins)


class Reduce:
    def __init__(self, q, first, send, recv, **refs):
        self.q, self.first, self.send, self.recv = q, first, send, recv
        self.__dict__.update(refs)
        self.dp = lax.axis_index("dp")
        self.fs = lax.axis_index("fsdp")
        self.x = self.dp % 2
        self.z = self.dp // 2
        self.y = self.fs // 2

    def rows(self, at, count):
        return pl.ds(pl.multiple_of(at, self.q), count)

    def half(self, x):
        return self.rows(x * 4 * self.q, 4 * self.q)

    def remote(self, src, dst, slot, device):
        return pltpu.make_async_remote_copy(
            src_ref=src, dst_ref=dst, send_sem=self.send.at[slot], recv_sem=self.recv.at[slot],
            device_id=device, device_id_type=MESH)

    def line(self):
        for i, oz in enumerate((3, 2, 1)):
            dp = self.dp
            if oz & 1:
                dp = flip(dp, 2)
            if oz & 2:
                dp = flip(dp, 4)
            yield i, dp

    def copies(self, stage):
        q = self.q
        over_y = (self.dp, flip(self.fs, 2))
        over_x = (flip(self.dp, 1), self.fs)
        if stage == "core":
            return [self.remote(self.give, self.core_in, 0, (self.dp, flip(self.fs, 1)))]
        if stage == "near" and self.first == "y":
            return [self.remote(self.core_in.at[1 - self.y], self.near, 1, over_y)]
        if stage == "near":
            return [self.remote(self.core_in.at[y, self.half(1 - self.x)], self.near.at[y], 1 + y, over_x)
                    for y in range(2)]
        if stage == "next" and self.first == "y":
            return [self.remote(self.near.at[self.half(1 - self.x)], self.mid, 3, over_x)]
        if stage == "next":
            return [self.remote(self.near.at[1 - self.y], self.mid, 3, over_y)]
        if stage == "z":
            return [self.remote(self.mid.at[self.rows((dp // 2) * q, q)], self.z_in.at[i], 4 + i, (dp, self.fs))
                    for i, dp in self.line()]
        if stage == "back_z":
            mine = self.full.at[self.own_piece()]
            return [self.remote(mine, mine, 7 + i, (dp, self.fs)) for i, dp in self.line()]
        half = self.full.at[self.half(self.x)]
        return [self.remote(half, half, 10, over_x)]

    def start(self, stage):
        for c in self.copies(stage):
            c.start()

    def wait(self, stage):
        for c in self.copies(stage):
            c.wait()

    def add(self, dst, src, count):
        @pl.loop(0, 4)
        def _(i):
            r = self.rows(i * (count // 4), count // 4)
            dst[r, :] = (dst[r, :].astype(f32) + src[r, :].astype(f32)).astype(bf)

    def to_near(self):
        self.wait("core")
        for y in range(2):
            self.add(self.core_in.at[y], self.keep.at[y], 8 * self.q)
        self.start("near")

    def add_near(self):
        self.wait("near")
        if self.first == "y":
            self.add(self.near, self.core_in.at[self.y], 8 * self.q)
        else:
            for y in range(2):
                self.add(self.near.at[y], self.core_in.at[y, self.half(self.x)], 4 * self.q)

    def to_next(self):
        self.add_near()
        self.start("next")

    def add_next(self):
        self.wait("next")
        src = self.near.at[self.half(self.x)] if self.first == "y" else self.near.at[self.y]
        self.add(self.mid, src, 4 * self.q)

    def to_z(self):
        self.add_next()
        self.start("z")

    def add_z(self):
        self.wait("z")
        total = self.mid[self.rows(self.z * self.q, self.q), :].astype(f32)
        for i in range(3):
            total += self.z_in[i].astype(f32)
        return total.astype(bf)

    def back(self):
        self.full[self.own_piece(), :] = self.add_z()
        self.start("back_z")

    def widen(self):
        self.wait("back_z")
        self.start("back_x")

    def own_piece(self):
        return self.rows((self.x * 4 + self.z) * self.q, self.q)


def greet(peers):
    sem = pltpu.get_barrier_semaphore()
    for peer in peers:
        pl.semaphore_signal(sem, inc=1, device_id=peer, device_id_type=MESH)


def met(count):
    pl.semaphore_wait(pltpu.get_barrier_semaphore(), count)


def dp_peers():
    dp, fs = lax.axis_index("dp"), lax.axis_index("fsdp")
    out = []
    for k in range(1, 8):
        d = dp
        for bit in (1, 2, 4):
            if k & bit:
                d = flip(d, bit)
        out.append((d, fs))
    return out


def fsdp_peers():
    dp, fs = lax.axis_index("dp"), lax.axis_index("fsdp")
    return [(dp, flip(fs, 1)), (dp, flip(fs, 2)), (dp, flip(flip(fs, 1), 2))]


def blocks(accs, shard):
    at = 0
    for acc in accs:
        n = acc.shape[0] // 4
        rows = pl.ds(pl.multiple_of(shard * n, n), n)
        for j in range(acc.shape[1] // LG):
            yield at, n, acc[rows, j * LG:(j + 1) * LG]
            at += n


def pack(accs, dst, core):
    for y in range(2):
        for at, n, block in blocks(accs, 2 * y + core):
            dst[y, at:at + n, :] = block.astype(bf)


def pack_add(accs, dst, core):
    for y in range(2):
        for at, n, block in blocks(accs, 2 * y + core):
            dst[y, at:at + n, :] = (block + dst[y, at:at + n, :].astype(f32)).astype(bf)


def unpack(full, outs):
    at = 0
    for out in outs:
        n = out.shape[0]
        for j in range(out.shape[1] // LG):
            out[:, j * LG:(j + 1) * LG] = full[at:at + n, :].astype(f32)
            at += n


RT = 512
TT = 1024


def sigm(v):
    return 0.5 * jnp.tanh(0.5 * v) + 0.5


def tile_valid(lens, step, seqlen):
    row0 = step * RT
    seq = row0 // seqlen
    return row0 - seq * seqlen, lens[seq]


def split_pack(w_a):
    zd = SPAN
    d = w_a.shape[0]
    vd = (w_a.shape[1] - zd - 2 * d) // 2
    cuts = [0, zd, zd + vd, zd + vd + d, zd + vd + 2 * d, zd + 2 * vd + 2 * d]
    return [w_a.at[:, lo:hi] for lo, hi in zip(cuts, cuts[1:])]


def forward_kernel(seqlen, remote, lens, sm, nm, tok, aff, w_a, u_h, *rest):
    shards, rest = (rest[:2], rest[2:]) if remote else ((), rest)
    middle_o, upd_o, u2_o, uh_o, val_o, vsl_o, gat_o, rv_o, a2_o, pr_o, qk_o = rest[:11]
    rest = rest[11:]
    if remote:
        gather = Gather(shards, rest[:2], tuple((a, 0, w.shape[1]) for a, w in enumerate(shards)), *rest[3:])
        rest = rest[2:]
    gscr = rest[0]

    def slot(at, fn):
        if remote:
            pl.when(pl.program_id(0) == at)(fn)

    slot(0, lambda: greet(gather.peers()))

    w_z, w_r, w_u, w_h, w_v = split_pack(w_a)
    base, length = tile_valid(lens, pl.program_id(0), seqlen)
    zd = w_z.shape[1]
    vd = w_v.shape[1]
    s = sm[...]
    n = nm[...]
    scale = zd ** -0.5
    zp = mm(s, w_z[...])
    sg = sigm(zp)
    sh = zp * sg
    ssl = sg + sh * (1.0 - sg)
    q = (sh * aff[0:1, :] + aff[1:2, :]).astype(bf)
    k = (sh * aff[2:3, :] + aff[3:4, :]).astype(bf)
    qk_o[0] = q
    qk_o[1] = k
    qk_o[2] = sh.astype(bf)
    qk_o[3] = ssl.astype(bf)
    probs = []
    for b in range(RT // SPAN):
        r = slice(b * SPAN, (b + 1) * SPAN)
        sc = mm_nt(q[r], k[r]) * scale
        keys = base + b * SPAN + lax.broadcasted_iota(jnp.int32, (1, SPAN), 1)
        sc = jnp.where(keys < length, sc, -1e9)
        e = jnp.exp(sc - jnp.max(sc, axis=-1, keepdims=True))
        p = (e / jnp.sum(e, axis=-1, keepdims=True)).astype(bf)
        pr_o[r, :] = p
        probs.append(p)

    def begin():
        met(4)
        gather.begin()

    slot(0, begin)

    def relay():
        gather.relay(0)
        gather.relay(1)

    slot(1, relay)

    def cross():
        gather.cross(0)
        gather.cross(1)

    slot(2, cross)

    def last():
        gather.last(0)
        gather.last(1)

    slot(3, last)
    rows = base + lax.broadcasted_iota(jnp.int32, (RT, 1), 0)
    live = (rows < length).astype(f32)
    for j in range(vd // 256):
        c = slice(j * 256, (j + 1) * 256)
        vp = mm(n, w_v[:, c])
        sg = sigm(vp)
        v = vp * sg
        vl = v.astype(bf)
        val_o[:, c] = vl
        vsl_o[:, c] = (sg + v - v * sg).astype(bf)
        att = jnp.concatenate(
            [mm(probs[b], vl[b * SPAN:(b + 1) * SPAN]) for b in range(RT // SPAN)], axis=0)
        rp = mm(s, w_r[:, c])
        sg = sigm(rp)
        re = rp * sg
        att = att * live
        ga = (re * att).astype(bf)
        gat_o[:, c] = ga
        gscr[:, c] = ga
        rv_o[:, c] = (re * live).astype(bf)
        a2_o[:, c] = (att * (sg + re - re * sg)).astype(bf)
    for j in range(w_h.shape[1] // 256):
        c = slice(j * 256, (j + 1) * 256)
        hp = mm(s, w_h[:, c]) + mm(gscr[...], u_h[:, c])
        up = sigm(mm(s, w_u[:, c]))
        x = tok[:, c].astype(f32)
        sg = sigm(hp)
        cand = hp * sg
        diff = cand - x
        ud = up * diff
        middle_o[:, c] = (x + ud).astype(bf)
        upd_o[:, c] = up.astype(bf)
        u2_o[:, c] = (ud - ud * up).astype(bf)
        uh_o[:, c] = (up * (sg + cand - cand * sg)).astype(bf)


    slot(3, lambda: gather.finish())


def row_spec(width):
    return pl.BlockSpec((RT, width), lambda i: (i, 0))


SMEM = pl.BlockSpec(memory_space=pltpu.SMEM)


def forward_main(lengths, smooth, normed, tokens, affine, w_a, u_h, shards=()):
    rows, D = tokens.shape
    nseq = lengths.shape[0]
    vd = u_h.shape[0]
    zd = affine.shape[1]
    d_out = jax.ShapeDtypeStruct((rows, D), bf)
    v_out = jax.ShapeDtypeStruct((rows, vd), bf)
    ds, vs = row_spec(D), row_spec(vd)
    ws = (affine, w_a, u_h)
    remote = len(shards) > 0
    params = dict(collective_id=4, has_side_effects=True) if remote else {}
    fulls = [jax.ShapeDtypeStruct((4 * w.shape[0], w.shape[1]), bf) for w in shards]
    return pl.pallas_call(
        functools.partial(forward_kernel, rows // nseq, remote),
        grid=(rows // RT,),
        in_specs=[SMEM, ds, ds, ds] + [const_spec(w) for w in (*ws, *shards)],
        out_specs=[ds] * 4 + [vs] * 5 + [row_spec(SPAN), pl.BlockSpec((4, RT, zd), lambda i: (0, i, 0))]
        + [ANY] * len(shards),
        out_shape=[d_out] * 4 + [v_out] * 5
        + [jax.ShapeDtypeStruct((rows, SPAN), bf), jax.ShapeDtypeStruct((4, rows, zd), bf)] + fulls,
        scratch_shapes=[pltpu.VMEM((RT, vd), bf)] + (gather_sems(2, 2) if remote else []),
        compiler_params=pltpu.CompilerParams(vmem_limit_bytes=60 * 2**20, **params),
        name="forward_main",
    )(lengths, smooth, normed, tokens, *ws, *shards)


def ffn_kernel(packed, fs, middle, cot, gain, w_in, w_out, out_o, dm_o, dg_o, *rest):
    if packed:
        keep_a, give_a, keep_b, give_b, gwi, gwo, ascr, gscr = rest
    else:
        gwi, gwo, ascr, gscr = rest

    @pl.when(pl.program_id(0) == 0)
    def _():
        gwi[...] = jnp.zeros_like(gwi)
        gwo[...] = jnp.zeros_like(gwo)
        dg_o[...] = jnp.zeros_like(dg_o)

    m = middle[...].astype(f32)
    inv = lax.rsqrt(jnp.mean(m * m, axis=-1, keepdims=True) + eps)
    gn = lane_row(gain, 4 * NH + 1)
    mr = m * inv
    y = (mr * gn).astype(bf)
    cl = cot[...]
    for j in range(w_in.shape[1] // 256):
        c = slice(j * 256, (j + 1) * 256)
        pre = mm(y, w_in[:, c])
        sg = sigm(pre)
        act = pre * sg
        al = act.astype(bf)
        ascr[:, c] = al
        ga = mm_nt(cl, w_out[c, :])
        gf = (ga * (sg + act - act * sg)).astype(bf)
        gscr[:, c] = gf
        gwo[c, :] += mm_tn(al, cl)
        gwi[:, c] += mm_tn(y, gf)
    out_o[...] = (m + mm(ascr[...], w_out[...])).astype(bf)
    dy = mm_nt(gscr[...], w_in[...])
    part = jnp.sum((dy * mr).reshape(TT // 8, 8, m.shape[1]), axis=0)
    for j in range(m.shape[1] // LG):
        dg_o[j] += part[:, j * LG:(j + 1) * LG]
    dyg = dy * gn
    inner = jnp.mean(dyg * mr, axis=-1, keepdims=True)
    dm_o[...] = (cl.astype(f32) + inv * (dyg - mr * inner)).astype(bf)
    if packed:
        @pl.when(pl.program_id(0) == pl.num_programs(0) - 1)
        def _():
            core = fs[0] % 2
            pack((gwo,), give_a, 1 - core)
            pack((gwo,), keep_a, core)
            pack((gwi,), give_b, 1 - core)
            pack((gwi,), keep_b, core)


def ffn_main(fs, middle, cot, gains, w_in, w_out, packed):
    rows, D = middle.shape
    ff = w_in.shape[1]
    ds = pl.BlockSpec((TT, D), lambda i: (i, 0))
    accs = [(D, ff), (ff, D)]
    pair = [jax.ShapeDtypeStruct((2, D * ff // 4 // LG, LG), bf)] * 4
    extra = pair if packed else [jax.ShapeDtypeStruct(s, f32) for s in accs]
    gain = jax.ShapeDtypeStruct((D // LG, 8, LG), f32)
    return pl.pallas_call(
        functools.partial(ffn_kernel, packed),
        grid=(rows // TT,),
        in_specs=[SMEM, ds, ds] + [const_spec(w) for w in (gains, w_in, w_out)],
        out_specs=[ds, ds] + [const_spec(a) for a in [gain] + extra],
        out_shape=[jax.ShapeDtypeStruct((rows, D), bf)] * 2 + [gain] + extra,
        scratch_shapes=([pltpu.VMEM(s, f32) for s in accs] if packed else [])
        + [pltpu.VMEM((TT, ff), bf), pltpu.VMEM((TT, ff), bf)],
        compiler_params=pltpu.CompilerParams(vmem_limit_bytes=60 * 2**20),
        name="ffn_main",
    )(fs, middle, cot, gains, w_in, w_out)


def backward_kernel(qs, remote, dm, upd, u2, uh, gat, rv, a2, sm, val, vsl, pr, qk, nm, aff, u_h, *rest):
    rest = list(rest)

    def take(n):
        out = rest[:n]
        del rest[:n]
        return out

    if remote:
        keep_a, give_a, keep_b, give_b = take(4)
    dxd_o, gh_o, gu_o, gr_o, gv_o, gsp_o, ga_o = take(7)
    if remote:
        half_a_o, piece_b_o, near_c_o, near_d_o, keep_e_o, give_e_o = take(6)
    gz, gv, gr, gu, gh_w, guh = take(6)
    ascr, = take(1)
    step = pl.program_id(0)
    tiles = pl.num_programs(0) // 2
    if remote:
        core1, near1, mid1, z1, f1, s1, r1 = take(7)
        core2, near2, mid2, z2, s2, r2 = take(6)
        give3, core3, near3, s3, r3 = take(5)
        give4, core4, near4, s4, r4 = take(5)
        a = Reduce(qs[0], "y", s1, r1, keep=keep_a, give=give_a, core_in=core1, near=near1, mid=mid1, z_in=z1, full=f1)
        b = Reduce(qs[1], "x", s2, r2, keep=keep_b, give=give_b, core_in=core2, near=near2, mid=mid2, z_in=z2)
        c = Reduce(qs[2], "y", s3, r3, give=give3, core_in=core3, near=near3)
        d = Reduce(qs[3], "x", s4, r4, give=give4, core_in=core4, near=near4)
        core = a.fs % 2
        ra, rb, rd = a, b, d

    def slot(at, fn):
        if remote:
            pl.when(step == at)(fn)

    @pl.when(step == 0)
    def _():
        for o in (gz, gv, gr, gu, gh_w, guh, ga_o):
            o[...] = jnp.zeros_like(o)

    def open_up():
        greet(fsdp_peers()[:2] + dp_peers())
        met(9)
        a.start("core")
        b.start("core")

    slot(0, open_up)

    def at_one():
        a.to_near()
        b.to_near()

    slot(1, at_one)

    def send_core(chunk, accs):
        pack(accs, chunk.give, 1 - core)
        chunk.start("core")

    def send_near(chunk, accs):
        chunk.wait("core")
        pack_add(accs, chunk.core_in, core)
        chunk.start("near")

    def at_four():
        send_core(c, (gr, gh_w))
        send_core(d, (guh, gu))

    slot(tiles, at_four)
    slot(tiles + 1, lambda: send_near(c, (gr, gh_w)))
    slot(tiles + 3, lambda: a.back())

    @pl.when(step < tiles)
    def _():
        vd = u_h.shape[0]
        d = dm[...].astype(f32)
        gh = (d * uh[...].astype(f32)).astype(bf)
        gu_l = (d * u2[...].astype(f32)).astype(bf)
        gh_o[...] = gh
        gu_o[...] = gu_l
        dxd_o[...] = (d - d * upd[...].astype(f32)).astype(bf)
        s = sm[...]
        gh_w[...] += mm_tn(s, gh)
        gu[...] += mm_tn(s, gu_l)

        def onward():
            ra.to_next()
            rb.to_next()

        slot(3, onward)
        at = pl.ds(pl.multiple_of(step * RT, RT), RT)
        for j in range(vd // 256):
            c = slice(j * 256, (j + 1) * 256)
            dg = mm_nt(gh, u_h[c, :])
            gr_l = (dg * a2[:, c].astype(f32)).astype(bf)
            gr_o[:, c] = gr_l
            ascr[at, c] = (dg * rv[:, c].astype(f32)).astype(bf)
            guh[c, :] += mm_tn(gat[:, c], gh)
            gr[:, c] += mm_tn(s, gr_l)

    @pl.when(step >= tiles)
    def _():
        vd = u_h.shape[0]
        zd = aff.shape[1]
        scale = zd ** -0.5
        gsp = []
        sums = [0.0] * 4
        for b in range(RT // SPAN):
            r = slice(b * SPAN, (b + 1) * SPAN)
            p = pr[r, :]
            pf = p.astype(f32)
            ga = ascr[pl.ds(pl.multiple_of((step - tiles) * RT + b * SPAN, SPAN), SPAN), :]
            dp = mm_nt(ga, val[r, :])
            inner = jnp.sum(dp * pf, axis=-1, keepdims=True)
            gs = (pf * (dp - inner)).astype(bf)
            dq = mm(gs, qk[1, r, :]) * scale
            dk = mm_tn(gs, qk[0, r, :]) * scale
            sh = qk[2, r, :].astype(f32)
            for i, t in enumerate((dq * sh, dq, dk * sh, dk)):
                sums[i] = sums[i] + jnp.sum(t.reshape(SPAN // 8, 8, zd), axis=0)
            gsp.append(((dq * aff[0:1, :] + dk * aff[2:3, :]) * qk[3, r, :].astype(f32)).astype(bf))
            dv = mm_tn(p, ga)
            gv_o[r, :] = (dv * vsl[r, :].astype(f32)).astype(bf)
        for i in range(4):
            ga_o[i] += sums[i]
        gsp = jnp.concatenate(gsp, axis=0)

        def middle():
            ra.to_z()
            rb.to_z()

        slot(tiles, middle)
        slot(tiles + 1, lambda: send_near(rd, (guh, gu)))
        gsp_o[...] = gsp
        gz[...] += mm_tn(sm[...], gsp)
        n = nm[...]
        for j in range(vd // 256):
            c = slice(j * 256, (j + 1) * 256)
            gv[:, c] += mm_tn(n, gv_o[:, c])

    def close():
        pack((gv, gz), give_e_o, 1 - core)
        pack((gv, gz), keep_e_o, core)
        c.add_near()
        near_c_o[...] = near3[...]
        d.add_near()
        near_d_o[...] = near4[...]
        a.wait("back_z")
        half_a_o[...] = f1[a.half(a.x), :]
        piece_b_o[...] = b.add_z()

    slot(2 * tiles - 1, close)


def backward_main(dm, saved, smooth, normed, affine, u_h, chunks=None):
    rows, D = dm.shape
    vd = u_h.shape[0]
    zd = affine.shape[1]
    remote = chunks is not None
    tiles = rows // RT
    upd, u2, uh, val, vsl, gat, rv, a2, pr, qk = saved

    def early(width):
        return pl.BlockSpec((RT, width), lambda i: (jnp.minimum(i, tiles - 1), 0))

    def late(width):
        return pl.BlockSpec((RT, width), lambda i: (jnp.maximum(i - tiles, 0), 0))

    de, ve, vl, dl = early(D), early(vd), late(vd), late(D)
    accs = [(D, zd), (D, vd), (D, vd), (D, D), (D, D), (vd, D)]
    ga = jax.ShapeDtypeStruct((4, 8, zd), f32)
    both = pl.BlockSpec((RT, D), lambda i: (i % tiles, 0))
    ins = [(dm, de), (upd, de), (u2, de), (uh, de), (gat, ve), (rv, ve), (a2, ve), (smooth, both),
           (val, vl), (vsl, vl), (pr, late(SPAN)),
           (qk, pl.BlockSpec((4, RT, zd), lambda i: (0, jnp.maximum(i - tiles, 0), 0))), (normed, dl),
           (affine, const_spec(affine)), (u_h, const_spec(u_h))]
    wide = lambda n: jax.ShapeDtypeStruct((rows, n), bf)
    outs = [(wide(D), de), (wide(D), de), (wide(D), de), (wide(vd), ve), (wide(vd), vl), (wide(zd), late(zd)),
            (ga, const_spec(ga))]
    scratch = [pltpu.VMEM((rows, vd), bf)]
    comm = {}
    qs = ()
    if remote:
        n = [chunks[0].shape[1], chunks[2].shape[1], (D * vd + D * D) // 4 // LG, (vd * D + D * D) // 4 // LG,
             (D * vd + D * zd) // 4 // LG]
        qs = [a // 8 for a in n]
        ins += [(c, const_spec(c)) for c in chunks]
        buf = lambda *s: jax.ShapeDtypeStruct(s + (LG,), bf)
        outs += [(s, const_spec(s)) for s in (buf(n[0] // 2), buf(qs[1]), buf(n[2]), buf(2, n[3] // 2), buf(2, n[4]),
                                              buf(2, n[4]))]
        v = lambda *s: pltpu.VMEM(s + (LG,), bf)
        sem = pltpu.SemaphoreType.DMA((11,))
        scratch = [pltpu.VMEM(a, f32) for a in accs] + scratch
        scratch += [v(2, n[0]), v(n[0]), v(n[0] // 2), v(3, qs[0]), v(n[0]), sem, sem,
                    v(2, n[1]), v(2, n[1] // 2), v(n[1] // 2), v(3, qs[1]), sem, sem,
                    v(2, n[2]), v(2, n[2]), v(n[2]), sem, sem,
                    v(2, n[3]), v(2, n[3]), v(2, n[3] // 2), sem, sem]
        comm = dict(collective_id=2, has_side_effects=True)
    else:
        outs += [(s, const_spec(s)) for s in (jax.ShapeDtypeStruct(a, f32) for a in accs)]
    return pl.pallas_call(
        functools.partial(backward_kernel, qs, remote),
        grid=(2 * tiles,),
        in_specs=[i[1] for i in ins],
        out_specs=[o[1] for o in outs],
        out_shape=[o[0] for o in outs],
        scratch_shapes=scratch,
        compiler_params=pltpu.CompilerParams(vmem_limit_bytes=62 * 2**20, **comm),
        name="backward_main",
    )(*[i[0] for i in ins])


def lane_row(small, row):
    return jnp.concatenate([small[q, row:row + 1, :] for q in range(small.shape[0])], axis=1)


def input_kernel(nseq, seqlen, qs, remote, gh, gu, gr, gsp, gv, w_a, tok, small, dft, xs_i, ks_i, *rest):
    rest = list(rest)

    def take(n):
        out = rest[:n]
        del rest[:n]
        return out

    if remote:
        half_a, piece_b, near_c, near_d, keep_e, give_e, gain1, aff = take(8)
        dn_o, full_a, full_b, full_c, full_d, full_e, small_o = take(7)
    else:
        dn_o, dema_o, dgain_o = take(3)
    dsm, dn, xr, dyspec, dxspec, gspec, dkscr = take(7)
    step = pl.program_id(0)
    ng = dsm.shape[0]
    tiles = pl.num_programs(0) - ng
    nch = seqlen // CH
    rows = nseq * seqlen
    if remote:
        f0, s0, r0 = take(3)
        f1, s1, r1 = take(3)
        mid2, z2, f2, s2, r2 = take(5)
        mid3, z3, f3, s3, r3 = take(5)
        core4, near4, mid4, z4, f4, s4, r4 = take(7)
        sums, near, total, far, s5, r5 = take(6)
        a_ = Reduce(qs[0], "y", s0, r0, full=f0)
        b_ = Reduce(qs[1], "x", s1, r1, full=f1)
        c_ = Reduce(qs[2], "y", s2, r2, near=near_c, mid=mid2, z_in=z2, full=f2)
        d_ = Reduce(qs[3], "x", s3, r3, near=near_d, mid=mid3, z_in=z3, full=f3)
        e_ = Reduce(qs[4], "y", s4, r4, keep=keep_e, give=give_e, core_in=core4, near=near4, mid=mid4, z_in=z4, full=f4)

    def slot(at, fn):
        if remote:
            pl.when(step == at)(fn)

    if remote:
        fs = lax.axis_index("fsdp")

    def across(k, src, dst, peer):
        return pltpu.make_async_remote_copy(src_ref=src, dst_ref=dst, send_sem=s5.at[k], recv_sem=r5.at[k],
                                            device_id=peer, device_id_type=MESH)

    def gathered():
        return [across(k, sums.at[peer[1]], near.at[k], peer) for k, peer in enumerate(fsdp_peers())]

    def hand_over(block):
        for copy, peer in zip(gathered(), fsdp_peers()):
            pl.when(peer[1] == block)(copy.start)

    def open_up():
        greet(fsdp_peers() + dp_peers())
        f0[a_.half(a_.x), :] = half_a[...]
        f1[b_.own_piece(), :] = piece_b[...]
        met(10)
        c_.start("next")
        d_.start("next")
        e_.start("core")
        b_.start("back_z")

    slot(0, open_up)

    def at_one():
        e_.to_near()
        a_.start("back_x")

    slot(1, at_one)

    def at_three():
        c_.to_z()
        d_.to_z()
        b_.widen()

    slot(3, at_three)

    @pl.when(step < tiles)
    def _():
        w_z, w_r, w_u, w_h, w_v = split_pack(w_a)
        at = pl.ds(pl.multiple_of(step * RT, RT), RT)
        x = tok[...].astype(f32)
        n = (x * lax.rsqrt(jnp.mean(x * x, axis=-1, keepdims=True) + eps)).astype(bf)
        a = mm_nt(gv[...], w_v[...])
        b = mm_nt(gh[...], w_h[...]) + mm_nt(gu[...], w_u[...]) + mm_nt(gsp[...], w_z[...]) + mm_nt(gr[...], w_r[...])
        for q in range(ng):
            c = slice(q * LG, (q + 1) * LG)
            xr[q, at, :] = n[:, c]
            dn[q, at, :] = a[:, c].astype(bf)
            dsm[q, at, :] = b[:, c].astype(bf)

    @pl.when(step >= tiles)
    def _():
        g = lax.rem(step - tiles + 1 + fs, ng) if remote else step - tiles

        if remote:
            @pl.when(step > tiles)
            def _():
                hand_over(lax.rem(step - tiles + fs, ng))


        slot(tiles, lambda: e_.to_next())
        slot(tiles + 2, lambda: d_.back())
        slot(tiles + 3, lambda: c_.widen())
        fwd = dft[:2 * CH, CH:]
        inv = dft[3 * CH:]
        for c in range(0, nseq * nch, 2):
            dy = mm(fwd, jnp.concatenate([dsm[g, c * CH:(c + 1) * CH, :], dsm[g, (c + 1) * CH:(c + 2) * CH, :]], axis=1))
            dyspec[c] = dy[:, :LG]
            dyspec[c + 1] = dy[:, LG:]

        def a_second():
            a_.wait("back_x")
            full_a[...] = f0[...]

        slot(tiles, a_second)

        def b_second():
            c_.back()
            e_.to_z()
            b_.wait("back_x")
            full_b[...] = f1[...]

        slot(tiles + 1, b_second)
        slot(tiles + 3, lambda: e_.back())

        def point(i, _):
            rc = pl.ds(pl.multiple_of(i * 16, 16), 16)
            rs = pl.ds(pl.multiple_of(CH + i * 16, 16), 16)
            kc = [ks_i[d, rc, :].astype(f32) for d in range(nch)]
            ks = [ks_i[d, rs, :].astype(f32) for d in range(nch)]
            gc = [0.] * nch
            gs = [0.] * nch
            for b in range(nseq):
                dc = [dyspec[b * nch + c, rc, :] for c in range(nch)]
                ds = [dyspec[b * nch + c, rs, :] for c in range(nch)]
                for c in range(nch):
                    oc = 0.
                    os = 0.
                    for d in range(nch - c):
                        oc = oc + kc[d] * dc[c + d] + ks[d] * ds[c + d]
                        os = os + kc[d] * ds[c + d] - ks[d] * dc[c + d]
                    dxspec[b * nch + c, rc, :] = oc.astype(bf)
                    dxspec[b * nch + c, rs, :] = os.astype(bf)
                for c in range(nch):
                    xc = xs_i[b * nch + c, rc, :].astype(f32)
                    xs = xs_i[b * nch + c, rs, :].astype(f32)
                    for d in range(nch - c):
                        gc[d] = gc[d] + xc * dc[c + d] + xs * ds[c + d]
                        gs[d] = gs[d] + xc * ds[c + d] - xs * dc[c + d]
            for d in range(nch):
                gspec[d, rc, :] = gc[d].astype(bf)
                gspec[d, rs, :] = gs[d].astype(bf)
            return 0

        lax.fori_loop(0, CH // 16, point, 0)
        dgain = 0.
        for c in range(0, nseq * nch, 2):
            both = mm(inv, jnp.concatenate([dxspec[c], dxspec[c + 1]], axis=1))
            for i in range(2):
                r = slice((c + i) * CH, (c + i + 1) * CH)
                t = both[:, i * LG:(i + 1) * LG] + dn[g, r, :].astype(f32)
                dn_o[0, r, :] = t.astype(bf)
                dgain = dgain + jnp.sum((t * xr[g, r, :].astype(f32)).reshape(CH // 8, 8, LG), axis=0)
        whole = dft[2 * CH:]
        for d in range(0, nch, 2):
            dk = mm(whole, jnp.concatenate([gspec[d], gspec[d + 1]], axis=1)) * (1.0 / CH)
            if d:
                dkscr[(d - 1) * CH:d * CH, :] += dk[:CH, :LG]
            dkscr[d * CH:(d + 1) * CH, :] = dk[CH:, :LG] + dk[:CH, LG:]
            dkscr[(d + 1) * CH:(d + 2) * CH, :] = dk[CH:, LG:]
        p = [small[g, i * NH:(i + 1) * NH, :] for i in range(4)]
        a, gg, ex, ro, keep = ema_rates(p)
        p8 = power_of(keep, 8)
        st = [jnp.broadcast_to(p8[h:h + 1, :], (8, LG)) for h in range(NH)]

        def horner(i, ab):
            A, B = ab
            v = dkscr[pl.ds(pl.multiple_of(seqlen - 8 - i * 8, 8), 8), :]
            B = tuple(B[h] * st[h] + A[h] for h in range(NH))
            A = tuple(A[h] * st[h] + v for h in range(NH))
            return (A, B)

        none = dkscr[0:8, :] * 0.0
        zero = (none,) * NH
        A, B = lax.fori_loop(0, seqlen // 8, horner, (zero, zero), unroll=8)
        rr = lax.broadcasted_iota(jnp.int32, (8, LG), 0).astype(f32)
        As = []
        Bs = []
        for h in range(NH):
            lad = ladder(keep[h:h + 1, :], 8)
            low = jnp.concatenate([jnp.zeros((1, LG), f32), lad[:7]], axis=0)
            As.append(jnp.sum(lad * A[h], axis=0, keepdims=True))
            Bs.append(jnp.sum(rr * low * A[h] + 8.0 * lad[7:8] * lad * B[h], axis=0, keepdims=True))
        As = jnp.concatenate(As, axis=0)
        Bs = jnp.concatenate(Bs, axis=0)
        dkeep = a * ex * ro * Bs
        da = ex * ro * As - gg * dkeep
        dg = -a * dkeep
        grads = (da * a * (1.0 - a), dg * gg * (1.0 - gg), a * ro * As, a * ex * As)
        for i, v in enumerate(grads):
            if remote:
                sums[g, i * NH:(i + 1) * NH, :] = v.astype(bf)
            else:
                dema_o[i] = v
        if remote:
            lead = [jnp.sum(dgain, axis=0, keepdims=True), jnp.sum(gain1[g], axis=0, keepdims=True)]
            pad = jnp.zeros((SMALL - 4 * NH - 6, LG), f32)
            sums[g, 4 * NH:, :] = jnp.concatenate(lead + [jnp.sum(aff[...], axis=1), pad], axis=0).astype(bf)
        else:
            dgain_o[...] = dgain

    def close():
        d_.widen()
        for c in gathered():
            c.wait()
        t = sums[fs].astype(f32)
        for k in range(3):
            t = t + near[k].astype(f32)
        total[...] = t.astype(bf)
        second = [across(3 + k, total, far.at[k], peer) for k, peer in enumerate(dp_peers())]
        for c in second:
            c.start()
        e_.widen()
        c_.wait("back_x")
        full_c[...] = f2[...]
        for c in second:
            c.wait()
        for k in range(7):
            t = t + far[k].astype(f32)
        small_o[...] = t
        d_.wait("back_x")
        full_d[...] = f3[...]
        e_.wait("back_x")
        full_e[...] = f4[...]

    slot(tiles + ng - 1, close)


def input_main(grads, w_a, tokens, small, dft, xspec, kspec, nseq, comm_in=None):
    rows, D = tokens.shape
    seqlen = rows // nseq
    nch = seqlen // CH
    ng = D // LG
    nchunks = nseq * nch
    tiles = rows // RT
    remote = comm_in is not None

    def early(a):
        return pl.BlockSpec((RT, a.shape[1]), lambda i: (jnp.minimum(i, tiles - 1), 0))

    def lanes(i):
        at = jnp.maximum(i - tiles, 0)
        return lax.rem(at + 1 + lax.axis_index("fsdp"), ng) if remote else at

    ins = [(a, early(a)) for a in grads] + [(w_a, const_spec(w_a)), (tokens, early(tokens)), (small, const_spec(small))]
    ins += [(dft, const_spec(dft)), (xspec, pl.BlockSpec((nchunks, 2 * CH, LG), lambda i: (0, 0, lanes(i)))),
            (kspec, pl.BlockSpec((nch, 2 * CH, LG), lambda i: (0, 0, lanes(i))))]
    outs = [(jax.ShapeDtypeStruct((ng, rows, LG), bf), pl.BlockSpec((1, rows, LG), lambda i: (lanes(i), 0, 0)))]
    scratch = [pltpu.VMEM((ng, rows, LG), bf)] * 3
    scratch += [pltpu.VMEM((nchunks, 2 * CH, LG), f32),
                pltpu.VMEM((nchunks, 2 * CH, LG), bf), pltpu.VMEM((nch, 2 * CH, LG), bf), pltpu.VMEM((seqlen, LG), f32)]
    params = {}
    qs = ()
    if remote:
        half_a, piece_b, near_c, near_d, keep_e, *_ = comm_in
        n = [half_a.shape[0] * 2, piece_b.shape[0] * 8, near_c.shape[0], near_d.shape[1] * 2, keep_e.shape[1]]
        qs = [a // 8 for a in n]
        ins += [(a, const_spec(a)) for a in comm_in]
        fulls = [jax.ShapeDtypeStruct((a, LG), bf) for a in n]
        one = jax.ShapeDtypeStruct((SMALL, LG), bf)
        outs += [(a, const_spec(a)) for a in fulls + [jax.ShapeDtypeStruct(one.shape, f32)]]
        v = lambda *s: pltpu.VMEM(s + (LG,), bf)
        w = lambda *s: pltpu.VMEM(s + one.shape, bf)
        sem = pltpu.SemaphoreType.DMA((11,))
        scratch += [v(n[0]), sem, sem, v(n[1]), sem, sem,
                    v(n[2] // 2), v(3, qs[2]), v(n[2]), sem, sem,
                    v(n[3] // 2), v(3, qs[3]), v(n[3]), sem, sem,
                    v(2, n[4]), v(n[4]), v(n[4] // 2), v(3, qs[4]), v(n[4]), sem, sem,
                    w(4), w(3), w(), w(7), sem, sem]
        params = dict(collective_id=3, has_side_effects=True)
    else:
        outs += [(jax.ShapeDtypeStruct((4, NH, D), f32), pl.BlockSpec((4, NH, LG), lambda i: (0, 0, lanes(i)))),
                 (jax.ShapeDtypeStruct((8, D), f32), pl.BlockSpec((8, LG), lambda i: (0, lanes(i))))]
    return pl.pallas_call(
        functools.partial(input_kernel, nseq, seqlen, qs, remote),
        grid=(tiles + ng,),
        in_specs=[i[1] for i in ins],
        out_specs=[o[1] for o in outs],
        out_shape=[o[0] for o in outs],
        scratch_shapes=scratch,
        compiler_params=pltpu.CompilerParams(vmem_limit_bytes=62 * 2**20, **params),
        name="input_main",
    )(*[i[0] for i in ins])


def finish_kernel(groups, fs, tok, dxd, dn, small, *rest):
    n = len(groups)
    fulls, sums = rest[:n], rest[n:n + 1]
    outs = list(rest[n + 1:] if groups else rest)
    dtok_o = outs.pop(0)
    x = tok[...].astype(f32)
    inv = lax.rsqrt(jnp.mean(x * x, axis=-1, keepdims=True) + eps)
    d = jnp.concatenate([dn[q] for q in range(dn.shape[0])], axis=1).astype(f32) * lane_row(small, 4 * NH)
    xr = x * inv
    dtok_o[...] = (dxd[...].astype(f32) + inv * (d - xr * jnp.mean(d * xr, axis=-1, keepdims=True))).astype(bf)
    if groups:
        @pl.when(pl.program_id(0) == 0)
        def _():
            gain_o, ema_o, aff_o = outs[:3]
            t = sums[0]
            gain_o[...] = t[4 * NH:4 * NH + 2, :]
            for i in range(4):
                ema_o[i] = t[i * NH:(i + 1) * NH, :]
            width = aff_o.shape[1]
            mine = 0.
            for q in range(4):
                mine = mine + jnp.where(fs[0] == q, 1.0, 0.0) * t[4 * NH + 2:4 * NH + 6, q * width:(q + 1) * width]
            aff_o[...] = mine

        at = 3
        for i, (full, count) in enumerate(zip(fulls, groups)):
            @pl.when(pl.program_id(0) == i % 2)
            def _(full=full, at=at, count=count):
                unpack(full, outs[at:at + count])
            at += count


def finish_main(fs, tokens, dxd, dn, small, fulls=(), sums=None, groups=(), shapes=()):
    rows, D = tokens.shape
    ng = dn.shape[0]
    tile = min(2 * RT, rows)
    ds = pl.BlockSpec((tile, D), lambda i: (i, 0))
    extra = list(fulls) + ([sums] if groups else [])
    outs = [jax.ShapeDtypeStruct(s, f32) for s in shapes]
    return pl.pallas_call(
        functools.partial(finish_kernel, groups),
        grid=(rows // tile,),
        in_specs=[SMEM, ds, ds, pl.BlockSpec((ng, tile, LG), lambda i: (0, i, 0))] + [const_spec(a) for a in [small] + extra],
        out_specs=[ds] + [const_spec(a) for a in outs],
        out_shape=[jax.ShapeDtypeStruct((rows, D), bf)] + outs,
        compiler_params=pltpu.CompilerParams(vmem_limit_bytes=60 * 2**20),
        name="finish",
    )(fs, tokens, dxd, dn, small, *extra)


def local_step(tokens, lengths, cotangent, fs, plain=None, shards=None):
    nseq = lengths.shape[0]
    rows, D = tokens.shape
    dft = jnp.asarray(dft_tables(), bf)
    remote = shards is not None
    if remote:
        ema_t, norm_gains, qk_affine, w_z, w_r, w_u, w_h, w_v, u_h, w_in, w_out = shards
        normed, smooth, x_spec, k_spec, small, affine, w_a, u_full = ema_forward(
            tokens, dft, nseq, comm_in=(ema_t, norm_gains, qk_affine, w_z, w_r, w_u, w_h, w_v, u_h))
        *saved, in_full, out_full = forward_main(
            lengths, smooth, normed, tokens, affine, w_a, u_full, (w_in, w_out))
    else:
        small, affine, w_a, u_full, in_full, out_full = plain
        normed, smooth, x_spec, k_spec = ema_forward(tokens, dft, nseq, small)
        saved = forward_main(lengths, smooth, normed, tokens, affine, w_a, u_full)
    middle, *saved = saved
    output, dm, g_gain1, *first = ffn_main(fs, middle, cotangent, small, in_full, out_full, remote)
    dxd, gh, gu, gr, gv, gsp, g_aff, *second = backward_main(
        dm, saved, smooth, normed, affine, u_full, first if remote else None)
    shared = ((gh, gu, gr, gsp, gv), w_a, tokens, small, dft, x_spec, k_spec, nseq)
    if not remote:
        dn, g_ema, g_gain0 = input_main(*shared)
        grad_tokens, = finish_main(fs, tokens, dxd, dn, small)
        grad_gains = jnp.stack([jnp.sum(g_gain0, axis=0), jnp.sum(g_gain1, axis=1).reshape(D)])
        return output, grad_tokens, (grad_gains, jnp.swapaxes(g_ema, 1, 2), jnp.sum(g_aff, axis=1), *second, *first)
    dn, *fulls, sums = input_main(*shared, (*second, g_gain1, g_aff))
    shapes = [norm_gains.shape, ema_t.shape, qk_affine.shape]
    shapes += [w.shape for w in (w_out, w_in, w_r, w_h, u_h, w_u, w_v, w_z)]
    grad_tokens, g_gains, g_ema, g_aff, g_out, g_in, g_r, g_h, g_uh, g_u, g_v, g_z = finish_main(
        fs, tokens, dxd, dn, small, fulls, sums, (1, 1, 2, 2, 2), shapes)
    return output, grad_tokens, (g_gains, jnp.swapaxes(g_ema, 1, 2), g_aff, g_z, g_v, g_r, g_u, g_h, g_uh, g_in, g_out)


def small_table(norm_gains, ema_params):
    d = norm_gains.shape[1]
    ema = jnp.swapaxes(ema_params, 1, 2).reshape(4 * NH, d)
    rows = jnp.concatenate([ema, norm_gains, jnp.zeros((SMALL - 4 * NH - 2, d), bf)], axis=0).astype(f32)
    return jnp.swapaxes(rows.reshape(SMALL, d // LG, LG), 0, 1)


def per_device(tokens, lengths, norm_gains, ema_params, qk_affine, w_z, w_v, w_r, w_u, w_h, u_h, w_in, w_out, cotangent):
    at = lax.axis_index("fsdp")
    parts = lax.axis_size("fsdp")
    fs = at.reshape(1)
    if parts == 4 and lax.axis_size("dp") == 8:
        shards = (jnp.swapaxes(ema_params, 1, 2), norm_gains, qk_affine, w_z, w_r, w_u, w_h, w_v, u_h, w_in, w_out)
        output, grad_tokens, pieces = local_step(tokens, lengths, cotangent, fs, shards=shards)
        return (output, grad_tokens) + pieces
    gather = lambda w, axis: lax.all_gather(w, "fsdp", axis=axis, tiled=True)
    w_a = gather(jnp.concatenate([w_z, w_r, w_u, w_h, w_v], axis=1), 0)
    plain = (small_table(gather(norm_gains, 1), gather(ema_params, 1)), gather(qk_affine, 1).astype(f32), w_a,
             gather(u_h, 0), gather(w_in, 0), gather(w_out, 0))
    output, grad_tokens, totals = local_step(tokens, lengths, cotangent, fs, plain)
    summed = lax.psum(totals, ("dp", "fsdp"))
    pieces = tuple(
        lax.dynamic_slice_in_dim(g, at * (g.shape[d] // parts), g.shape[d] // parts, d)
        for g, d in zip(summed, (1, 1, 1, 0, 0, 0, 0, 0, 0, 0, 0)))
    return (output, grad_tokens) + pieces


def solution(mesh):
    rows = P(("dp", "fsdp"), None)
    shard = P("fsdp", None)
    wide = P(None, "fsdp")
    deep = P(None, "fsdp", None)
    return jax.shard_map(
        per_device,
        mesh=mesh,
        in_specs=(rows, P(("dp", "fsdp")), wide, deep, wide) + (shard,) * 8 + (rows,),
        out_specs=(rows, rows, wide, deep, wide) + (shard,) * 8,
        check_vma=False,
    )
```

```python
import functools

import jax
import jax.numpy as jnp
import numpy as np
from jax import lax
from jax.experimental import pallas as pl
from jax.experimental.pallas import tpu as pltpu
from jax.sharding import PartitionSpec as P

bf = jnp.bfloat16
f32 = jnp.float32
SPAN = 128
CH = 256
NH = 16
LG = 128
eps = 1e-6


def dft_tables():
    f=np.arange(CH)[:,None]+0.5
    m=np.arange(-CH,CH)[None,:]
    ang=2*np.pi*f*m/(2*CH)
    both=np.concatenate([np.cos(ang),np.sin(ang)],axis=0)
    return np.concatenate([both,both.T],axis=0).astype(np.float32)

def mm(a,b): return jnp.dot(a,b,preferred_element_type=f32)
def mm_tn(a,b): return lax.dot_general(a,b,(((0,),(0,)),((),())),preferred_element_type=f32)
def mm_nt(a,b): return lax.dot_general(a,b,(((1,),(1,)),((),())),preferred_element_type=f32)

def ema_rates(p):
    a=jax.nn.sigmoid(p[0]); g=jax.nn.sigmoid(p[1])
    return a,g,p[2],p[3],1.0-a*g

def power_of(base, n):
    out=None
    sq=base
    while n:
        if n&1: out = sq if out is None else out*sq
        n>>=1
        if n: sq=sq*sq
    return out

def ladder(keep, width):
    r=lax.broadcasted_iota(jnp.int32,(width,keep.shape[-1]),0)
    acc=jnp.ones((width,keep.shape[-1]),f32)
    sq=keep
    bit=1
    while bit<width:
        acc=acc*jnp.where((r&bit)!=0, sq, 1.0)
        sq=sq*sq
        bit*=2
    return acc

MESH = pl.DeviceIdType.MESH


def flip(i, bit):
    return i + bit - 2 * bit * ((i // bit) % 2)


def const_spec(a):
    nd = len(a.shape)
    return pl.BlockSpec(a.shape, lambda i: (0,) * nd, pipeline_mode=pl.Buffered(1))


ANY = pl.BlockSpec(memory_space=pl.ANY)


class Gather:
    def __init__(self, shards, outs, pieces, send, recv, local, straight=()):
        self.shards, self.outs, self.pieces = shards, outs, pieces
        self.send, self.recv, self.local, self.straight = send, recv, local, straight
        self.dp = lax.axis_index("dp")
        self.fs = lax.axis_index("fsdp")
        self.x = self.dp % 2
        self.z = (self.dp // 2) % 2
        self.core_peer = (self.dp, flip(self.fs, 1))
        self.y_peer = (self.dp, flip(self.fs, 2))
        self.x_peer = (flip(self.dp, 1), self.fs)
        self.z_peer = (flip(self.dp, 2), self.fs)

        self.x_across = (self.x_peer[0], self.core_peer[1])
        self.z_across = (self.z_peer[0], self.core_peer[1])

    def peers(self):
        return [self.core_peer, self.y_peer, self.x_peer, self.z_peer]

    def copy(self, p, k):
        a, col, width = self.pieces[p]
        shard, out = self.shards[a], self.outs[a]
        n = shard.shape[0]
        far = flip(self.fs, 2) * n
        cols = pl.ds(col, width)
        x, z = self.x, self.z

        def at(ref, base, zz, xx, half=None):
            r = n // 4 if half is None else n // 8
            row = base + (2 * zz + xx) * (n // 4) + (0 if half is None else half * r)
            return ref.at[pl.ds(pl.multiple_of(row, r), r), cols]

        src, dst, peer = (
            (at(shard, 0, z, x), at(out, self.fs * n, z, x), self.y_peer),
            (at(out, far, z, x),) * 2 + (self.x_peer,),
            (at(out, far, z, x),) * 2 + (self.z_peer,),
            (at(out, far, 1 - z, x, 0),) * 2 + (self.x_peer,),
            (at(out, far, z, 1 - x, 1),) * 2 + (self.z_peer,),
            (at(out, far, z, x),) * 2 + (self.core_peer,),
            (at(out, far, z, 1 - x),) * 2 + (self.core_peer,),
            (at(out, far, 1 - z, x),) * 2 + (self.core_peer,),
            (at(out, far, 1 - z, 1 - x),) * 2 + (self.core_peer,),
            (at(out, far, 1 - z, x, 0),) * 2 + (self.x_across,),
            (at(out, far, z, 1 - x, 1),) * 2 + (self.z_across,),
        )[k]
        return pltpu.make_async_remote_copy(
            src_ref=src, dst_ref=dst, send_sem=self.send.at[11 * p + k], recv_sem=self.recv.at[11 * p + k],
            device_id=peer, device_id_type=MESH)

    def whole(self, a):
        n = self.shards[a].shape[0]
        slot = 11 * len(self.pieces) + a
        return pltpu.make_async_remote_copy(
            src_ref=self.shards[a], dst_ref=self.outs[a].at[pl.ds(pl.multiple_of(self.fs * n, n), n)],
            send_sem=self.send.at[slot], recv_sem=self.recv.at[slot], device_id=self.core_peer, device_id_type=MESH)

    def own(self, a):
        n = self.shards[a].shape[0]
        mine = pl.ds(pl.multiple_of(self.fs * n, n), n)
        return pltpu.make_async_copy(self.shards[a], self.outs[a].at[mine], self.local.at[a])

    def begin(self):
        for p in range(len(self.pieces)):
            self.copy(p, 0).start()
        for a in range(len(self.shards)):
            self.whole(a).start()
            self.own(a).start()

    def relay(self, p):
        self.copy(p, 0).wait_recv()
        for k in (1, 2, 5):
            self.copy(p, k).start()

    def cross(self, p):
        straight = p in self.straight
        self.copy(p, 2).wait_recv()
        for k in (3, 9, 7) if straight else (3, 7):
            self.copy(p, k).start()
        self.copy(p, 1).wait_recv()
        for k in (4, 10, 6) if straight else (4, 6):
            self.copy(p, k).start()

    def last(self, p):
        self.copy(p, 3).wait_recv()
        self.copy(p, 4).wait_recv()
        if p not in self.straight:
            self.copy(p, 8).start()

    def finish(self):
        for p in range(len(self.pieces)):
            ends = (9, 10) if p in self.straight else (8,)
            for k in (0, 1, 2, 3, 4, 5, 6, 7) + ends:
                self.copy(p, k).wait_send()
            for k in (5, 6, 7) + ends:
                self.copy(p, k).wait_recv()
        for a in range(len(self.shards)):
            self.whole(a).wait()
            self.own(a).wait()


def gather_sems(arrays, pieces):
    sem = pltpu.SemaphoreType.DMA((11 * pieces + arrays,))
    return [sem, sem, pltpu.SemaphoreType.DMA((arrays,))]


SMALL = 4 * NH + 16
PIECES = 3


def ema_fwd_kernel(nseq, seqlen, remote, tok, dft, *rest):
    rest = list(rest)

    def take(n):
        out = rest[:n]
        del rest[:n]
        return out

    g = pl.program_id(0)
    nch = seqlen // CH
    rows = nseq * seqlen
    if remote:
        ema_i, gain_i, aff_i, *parts = take(9)
    else:
        small, = take(1)
    normed_o, smooth_o, xs_o, ks_o = take(4)
    if remote:
        small_o, aff_o, w_full, u_full = take(4)
    nscr, kscr, kspec, xspec, yspec = take(5)
    if remote:
        small, sent, own, s1, r1, *sems = take(8)
        fs = lax.axis_index("fsdp")
        gather = Gather((own, parts[5]), (w_full, u_full),
                        ((0, 0, 1664), (0, 1664, own.shape[1] - 1664), (1, 0, parts[5].shape[1])), *sems, (2,))
        across = [pltpu.make_async_remote_copy(
            src_ref=sent.at[fs], dst_ref=sent.at[fs], send_sem=s1.at[k], recv_sem=r1.at[k],
            device_id=peer, device_id_type=MESH) for k, peer in enumerate(fsdp_peers())]

    def slot(at, fn):
        if remote:
            pl.when(g == at)(fn)

    def open_up():
        greet(fsdp_peers() + [gather.x_peer, gather.z_peer, gather.x_across, gather.z_across])
        for i in range(4):
            sent[fs, i * NH:(i + 1) * NH, :] = ema_i[i]
        tail = [gain_i[...].astype(f32), jnp.concatenate([aff_i[...].astype(f32)] * 4, axis=1),
                jnp.zeros((SMALL - 4 * NH - 6, LG), f32)]
        sent[fs, 4 * NH:, :] = jnp.concatenate(tail, axis=0).astype(bf)
        at = 0
        for w in parts[:5]:
            own[:, at:at + w.shape[1]] = w[...]
            at += w.shape[1]
        met(7)
        for c in across:
            c.start()
        gather.begin()

    slot(0, open_up)

    @pl.when(g == 0)
    def _():
        def body(i, _):
            r = pl.ds(pl.multiple_of(i * 256, 256), 256)
            x = tok[r, :].astype(f32)
            n = x * lax.rsqrt(jnp.mean(x * x, axis=-1, keepdims=True) + eps)
            for q in range(x.shape[1] // LG):
                nscr[q, r, :] = n[:, q * LG:(q + 1) * LG]
            return 0
        lax.fori_loop(0, rows // 256, body, 0)

    def settle():
        for c in across:
            c.wait()
        for q in range(4):
            small[q] = sent[q].astype(f32)
        small_o[...] = small[...]
        for q in range(4):
            n = aff_i.shape[1]
            aff_o[:, q * n:(q + 1) * n] = small[q, 4 * NH + 2:4 * NH + 6, 0:n]

    slot(0, settle)

    p = [small[g, i * NH:(i + 1) * NH, :] for i in range(4)]
    normed = (nscr[g] * small[g, 4 * NH:4 * NH + 1, :]).astype(bf)
    normed_o[...] = normed
    a, gg, ex, ro, keep = ema_rates(p)
    w = a * ex * ro * (1.0 / CH)
    step = power_of(keep, 16)
    z0 = []
    st = []
    for h in range(NH):
        z0.append(ladder(keep[h:h + 1, :], 16) * w[h:h + 1, :])
        st.append(jnp.broadcast_to(step[h:h + 1, :], (8, LG)))

    def kgen(i, zs):
        acc = list(zs)
        while len(acc) > 1:
            acc = [acc[j] + acc[j + 1] for j in range(0, len(acc), 2)]
        acc = acc[0]
        kscr[pl.ds(pl.multiple_of(CH + i * 16, 16), 16), :] = acc.astype(bf)
        return tuple(jnp.concatenate([zs[h][:8] * st[h], zs[h][8:] * st[h]], axis=0) for h in range(NH))

    lax.fori_loop(0, seqlen // 16, kgen, tuple(z0), unroll=4)
    kscr[0:CH, :] = jnp.zeros((CH, LG), bf)
    slot(1, lambda: gather.relay(1))
    slot(2, lambda: gather.cross(0))
    slot(3, lambda: gather.cross(2))
    both = dft[:2 * CH]
    fwd = dft[:2 * CH, CH:]
    inv = dft[3 * CH:]
    for d in range(0, nch, 2):
        kd = mm(both, jnp.concatenate([kscr[d * CH:(d + 2) * CH, :], kscr[(d + 1) * CH:(d + 3) * CH, :]], axis=1))
        for i in range(2):
            kspec[d + i] = kd[:, i * LG:(i + 1) * LG]
            ks_o[d + i] = kd[:, i * LG:(i + 1) * LG].astype(bf)
    for c in range(0, nseq * nch, 2):
        xd = mm(fwd, jnp.concatenate([normed[c * CH:(c + 1) * CH], normed[(c + 1) * CH:(c + 2) * CH]], axis=1))
        for i in range(2):
            xspec[c + i] = xd[:, i * LG:(i + 1) * LG]
            xs_o[c + i] = xd[:, i * LG:(i + 1) * LG].astype(bf)

    slot(1, lambda: gather.relay(2))
    slot(3, lambda: gather.last(0))

    def point(i, _):
        rc = pl.ds(pl.multiple_of(i * 16, 16), 16)
        rs = pl.ds(pl.multiple_of(CH + i * 16, 16), 16)
        kc = [kspec[d, rc, :] for d in range(nch)]
        ks = [kspec[d, rs, :] for d in range(nch)]
        for b in range(nseq):
            xc = [xspec[b * nch + c, rc, :] for c in range(nch)]
            xs = [xspec[b * nch + c, rs, :] for c in range(nch)]
            for c in range(nch):
                yc = 0.
                ys = 0.
                for d in range(c + 1):
                    yc = yc + kc[d] * xc[c - d] - ks[d] * xs[c - d]
                    ys = ys + kc[d] * xs[c - d] + ks[d] * xc[c - d]
                yspec[b * nch + c, rc, :] = yc.astype(bf)
                yspec[b * nch + c, rs, :] = ys.astype(bf)
        return 0

    lax.fori_loop(0, CH // 16, point, 0)
    slot(0, lambda: gather.relay(0))
    slot(2, lambda: gather.cross(1))
    slot(3, lambda: gather.last(1))
    for c in range(0, nseq * nch, 2):
        y = mm(inv, jnp.concatenate([yspec[c], yspec[c + 1]], axis=1)).astype(bf)
        smooth_o[c * CH:(c + 1) * CH, :] = y[:, :LG]
        smooth_o[(c + 1) * CH:(c + 2) * CH, :] = y[:, LG:]

    def close():
        gather.last(2)
        gather.finish()

    slot(3, close)


def ema_forward(tokens, dft, nseq, small=None, comm_in=None):
    rows, D = tokens.shape
    seqlen = rows // nseq
    nch = seqlen // CH
    ng = D // LG
    nchunks = nseq * nch
    remote = comm_in is not None
    col = pl.BlockSpec((rows, LG), lambda g: (0, g))
    ins = [tokens, dft] + (list(comm_in) if remote else [small])
    wide = jax.ShapeDtypeStruct((rows, D), bf)
    outs = [(wide, col), (wide, col),
            (jax.ShapeDtypeStruct((nchunks, 2 * CH, D), bf), pl.BlockSpec((nchunks, 2 * CH, LG), lambda g: (0, 0, g))),
            (jax.ShapeDtypeStruct((nch, 2 * CH, D), bf), pl.BlockSpec((nch, 2 * CH, LG), lambda g: (0, 0, g)))]
    scratch = [pltpu.VMEM((ng, rows, LG), f32), pltpu.VMEM((seqlen + CH, LG), bf), pltpu.VMEM((nch, 2 * CH, LG), f32),
               pltpu.VMEM((nchunks, 2 * CH, LG), f32), pltpu.VMEM((nchunks, 2 * CH, LG), bf)]
    params = {}
    if remote:
        n = sum(w.shape[1] for w in comm_in[3:8])
        u = comm_in[8]
        a = jax.ShapeDtypeStruct((4, SMALL, LG), f32)
        b = jax.ShapeDtypeStruct((4, 4 * comm_in[2].shape[1]), f32)
        outs += [(a, const_spec(a)), (b, const_spec(b)), (jax.ShapeDtypeStruct((D, n), bf), ANY),
                 (jax.ShapeDtypeStruct((4 * u.shape[0], D), bf), ANY)]
        sem = pltpu.SemaphoreType.DMA((3,))
        scratch += [pltpu.VMEM(a.shape, f32), pltpu.VMEM(a.shape, bf), pltpu.VMEM((D // 4, n), bf), sem, sem] + gather_sems(2, PIECES)
        params = dict(collective_id=1, has_side_effects=True)
    return pl.pallas_call(
        functools.partial(ema_fwd_kernel, nseq, seqlen, remote),
        grid=(ng,),
        in_specs=[const_spec(a) for a in ins],
        out_specs=[o[1] for o in outs],
        out_shape=[o[0] for o in outs],
        scratch_shapes=scratch,
        compiler_params=pltpu.CompilerParams(vmem_limit_bytes=60 * 2**20, **params),
        name="ema_fwd",
    )(*ins)


class Reduce:
    def __init__(self, q, first, send, recv, **refs):
        self.q, self.first, self.send, self.recv = q, first, send, recv
        self.__dict__.update(refs)
        self.dp = lax.axis_index("dp")
        self.fs = lax.axis_index("fsdp")
        self.x = self.dp % 2
        self.z = self.dp // 2
        self.y = self.fs // 2

    def rows(self, at, count):
        return pl.ds(pl.multiple_of(at, self.q), count)

    def half(self, x):
        return self.rows(x * 4 * self.q, 4 * self.q)

    def remote(self, src, dst, slot, device):
        return pltpu.make_async_remote_copy(
            src_ref=src, dst_ref=dst, send_sem=self.send.at[slot], recv_sem=self.recv.at[slot],
            device_id=device, device_id_type=MESH)

    def line(self):
        for i, oz in enumerate((3, 2, 1)):
            dp = self.dp
            if oz & 1:
                dp = flip(dp, 2)
            if oz & 2:
                dp = flip(dp, 4)
            yield i, dp

    def copies(self, stage):
        q = self.q
        over_y = (self.dp, flip(self.fs, 2))
        over_x = (flip(self.dp, 1), self.fs)
        if stage == "core":
            return [self.remote(self.give, self.core_in, 0, (self.dp, flip(self.fs, 1)))]
        if stage == "near" and self.first == "y":
            return [self.remote(self.core_in.at[1 - self.y], self.near, 1, over_y)]
        if stage == "near":
            return [self.remote(self.core_in.at[y, self.half(1 - self.x)], self.near.at[y], 1 + y, over_x)
                    for y in range(2)]
        if stage == "next" and self.first == "y":
            return [self.remote(self.near.at[self.half(1 - self.x)], self.mid, 3, over_x)]
        if stage == "next":
            return [self.remote(self.near.at[1 - self.y], self.mid, 3, over_y)]
        if stage == "z":
            return [self.remote(self.mid.at[self.rows((dp // 2) * q, q)], self.z_in.at[i], 4 + i, (dp, self.fs))
                    for i, dp in self.line()]
        if stage == "back_z":
            mine = self.full.at[self.own_piece()]
            return [self.remote(mine, mine, 7 + i, (dp, self.fs)) for i, dp in self.line()]
        half = self.full.at[self.half(self.x)]
        return [self.remote(half, half, 10, over_x)]

    def start(self, stage):
        for c in self.copies(stage):
            c.start()

    def wait(self, stage):
        for c in self.copies(stage):
            c.wait()

    def add(self, dst, src, count):
        @pl.loop(0, 4)
        def _(i):
            r = self.rows(i * (count // 4), count // 4)
            dst[r, :] = (dst[r, :].astype(f32) + src[r, :].astype(f32)).astype(bf)

    def to_near(self):
        self.wait("core")
        for y in range(2):
            self.add(self.core_in.at[y], self.keep.at[y], 8 * self.q)
        self.start("near")

    def add_near(self):
        self.wait("near")
        if self.first == "y":
            self.add(self.near, self.core_in.at[self.y], 8 * self.q)
        else:
            for y in range(2):
                self.add(self.near.at[y], self.core_in.at[y, self.half(self.x)], 4 * self.q)

    def to_next(self):
        self.add_near()
        self.start("next")

    def add_next(self):
        self.wait("next")
        src = self.near.at[self.half(self.x)] if self.first == "y" else self.near.at[self.y]
        self.add(self.mid, src, 4 * self.q)

    def to_z(self):
        self.add_next()
        self.start("z")

    def add_z(self):
        self.wait("z")
        total = self.mid[self.rows(self.z * self.q, self.q), :].astype(f32)
        for i in range(3):
            total += self.z_in[i].astype(f32)
        return total.astype(bf)

    def back(self):
        self.full[self.own_piece(), :] = self.add_z()
        self.start("back_z")

    def widen(self):
        self.wait("back_z")
        self.start("back_x")

    def own_piece(self):
        return self.rows((self.x * 4 + self.z) * self.q, self.q)


def greet(peers):
    sem = pltpu.get_barrier_semaphore()
    for peer in peers:
        pl.semaphore_signal(sem, inc=1, device_id=peer, device_id_type=MESH)


def met(count):
    pl.semaphore_wait(pltpu.get_barrier_semaphore(), count)


def dp_peers():
    dp, fs = lax.axis_index("dp"), lax.axis_index("fsdp")
    out = []
    for k in range(1, 8):
        d = dp
        for bit in (1, 2, 4):
            if k & bit:
                d = flip(d, bit)
        out.append((d, fs))
    return out


def fsdp_peers():
    dp, fs = lax.axis_index("dp"), lax.axis_index("fsdp")
    return [(dp, flip(fs, 1)), (dp, flip(fs, 2)), (dp, flip(flip(fs, 1), 2))]


def blocks(accs, shard):
    at = 0
    for acc in accs:
        n = acc.shape[0] // 4
        rows = pl.ds(pl.multiple_of(shard * n, n), n)
        for j in range(acc.shape[1] // LG):
            yield at, n, acc[rows, j * LG:(j + 1) * LG]
            at += n


def pack(accs, dst, core):
    for y in range(2):
        for at, n, block in blocks(accs, 2 * y + core):
            dst[y, at:at + n, :] = block.astype(bf)


def pack_add(accs, dst, core):
    for y in range(2):
        for at, n, block in blocks(accs, 2 * y + core):
            dst[y, at:at + n, :] = (block + dst[y, at:at + n, :].astype(f32)).astype(bf)


def unpack(full, outs):
    at = 0
    for out in outs:
        n = out.shape[0]
        for j in range(out.shape[1] // LG):
            out[:, j * LG:(j + 1) * LG] = full[at:at + n, :].astype(f32)
            at += n


RT = 512
TT = 1024


def sigm(v):
    return 0.5 * jnp.tanh(0.5 * v) + 0.5


def tile_valid(lens, step, seqlen):
    row0 = step * RT
    seq = row0 // seqlen
    return row0 - seq * seqlen, lens[seq]


def split_pack(w_a):
    zd = SPAN
    d = w_a.shape[0]
    vd = (w_a.shape[1] - zd - 2 * d) // 2
    cuts = [0, zd, zd + vd, zd + vd + d, zd + vd + 2 * d, zd + 2 * vd + 2 * d]
    return [w_a.at[:, lo:hi] for lo, hi in zip(cuts, cuts[1:])]


def forward_kernel(seqlen, remote, lens, sm, nm, tok, aff, w_a, u_h, *rest):
    shards, rest = (rest[:2], rest[2:]) if remote else ((), rest)
    middle_o, upd_o, u2_o, uh_o, val_o, vsl_o, gat_o, rv_o, a2_o, pr_o, qk_o = rest[:11]
    rest = rest[11:]
    if remote:
        gather = Gather(shards, rest[:2], tuple((a, 0, w.shape[1]) for a, w in enumerate(shards)), *rest[3:])
        rest = rest[2:]
    gscr = rest[0]

    def slot(at, fn):
        if remote:
            pl.when(pl.program_id(0) == at)(fn)

    slot(0, lambda: greet(gather.peers()))

    w_z, w_r, w_u, w_h, w_v = split_pack(w_a)
    base, length = tile_valid(lens, pl.program_id(0), seqlen)
    zd = w_z.shape[1]
    vd = w_v.shape[1]
    s = sm[...]
    n = nm[...]
    scale = zd ** -0.5
    zp = mm(s, w_z[...])
    sg = sigm(zp)
    sh = zp * sg
    ssl = sg + sh * (1.0 - sg)
    q = (sh * aff[0:1, :] + aff[1:2, :]).astype(bf)
    k = (sh * aff[2:3, :] + aff[3:4, :]).astype(bf)
    qk_o[0] = q
    qk_o[1] = k
    qk_o[2] = sh.astype(bf)
    qk_o[3] = ssl.astype(bf)
    probs = []
    for b in range(RT // SPAN):
        r = slice(b * SPAN, (b + 1) * SPAN)
        sc = mm_nt(q[r], k[r]) * scale
        keys = base + b * SPAN + lax.broadcasted_iota(jnp.int32, (1, SPAN), 1)
        sc = jnp.where(keys < length, sc, -1e9)
        e = jnp.exp(sc - jnp.max(sc, axis=-1, keepdims=True))
        p = (e / jnp.sum(e, axis=-1, keepdims=True)).astype(bf)
        pr_o[r, :] = p
        probs.append(p)

    def begin():
        met(4)
        gather.begin()

    slot(0, begin)

    def relay():
        gather.relay(0)
        gather.relay(1)

    slot(1, relay)

    def cross():
        gather.cross(0)
        gather.cross(1)

    slot(2, cross)

    def last():
        gather.last(0)
        gather.last(1)

    slot(3, last)
    rows = base + lax.broadcasted_iota(jnp.int32, (RT, 1), 0)
    live = (rows < length).astype(f32)
    for j in range(vd // 256):
        c = slice(j * 256, (j + 1) * 256)
        vp = mm(n, w_v[:, c])
        sg = sigm(vp)
        v = vp * sg
        vl = v.astype(bf)
        val_o[:, c] = vl
        vsl_o[:, c] = (sg + v - v * sg).astype(bf)
        att = jnp.concatenate(
            [mm(probs[b], vl[b * SPAN:(b + 1) * SPAN]) for b in range(RT // SPAN)], axis=0)
        rp = mm(s, w_r[:, c])
        sg = sigm(rp)
        re = rp * sg
        att = att * live
        ga = (re * att).astype(bf)
        gat_o[:, c] = ga
        gscr[:, c] = ga
        rv_o[:, c] = (re * live).astype(bf)
        a2_o[:, c] = (att * (sg + re - re * sg)).astype(bf)
    for j in range(w_h.shape[1] // 256):
        c = slice(j * 256, (j + 1) * 256)
        hp = mm(s, w_h[:, c]) + mm(gscr[...], u_h[:, c])
        up = sigm(mm(s, w_u[:, c]))
        x = tok[:, c].astype(f32)
        sg = sigm(hp)
        cand = hp * sg
        diff = cand - x
        ud = up * diff
        middle_o[:, c] = (x + ud).astype(bf)
        upd_o[:, c] = up.astype(bf)
        u2_o[:, c] = (ud - ud * up).astype(bf)
        uh_o[:, c] = (up * (sg + cand - cand * sg)).astype(bf)


    slot(3, lambda: gather.finish())


def row_spec(width):
    return pl.BlockSpec((RT, width), lambda i: (i, 0))


SMEM = pl.BlockSpec(memory_space=pltpu.SMEM)


def forward_main(lengths, smooth, normed, tokens, affine, w_a, u_h, shards=()):
    rows, D = tokens.shape
    nseq = lengths.shape[0]
    vd = u_h.shape[0]
    zd = affine.shape[1]
    d_out = jax.ShapeDtypeStruct((rows, D), bf)
    v_out = jax.ShapeDtypeStruct((rows, vd), bf)
    ds, vs = row_spec(D), row_spec(vd)
    ws = (affine, w_a, u_h)
    remote = len(shards) > 0
    params = dict(collective_id=4, has_side_effects=True) if remote else {}
    fulls = [jax.ShapeDtypeStruct((4 * w.shape[0], w.shape[1]), bf) for w in shards]
    return pl.pallas_call(
        functools.partial(forward_kernel, rows // nseq, remote),
        grid=(rows // RT,),
        in_specs=[SMEM, ds, ds, ds] + [const_spec(w) for w in (*ws, *shards)],
        out_specs=[ds] * 4 + [vs] * 5 + [row_spec(SPAN), pl.BlockSpec((4, RT, zd), lambda i: (0, i, 0))]
        + [ANY] * len(shards),
        out_shape=[d_out] * 4 + [v_out] * 5
        + [jax.ShapeDtypeStruct((rows, SPAN), bf), jax.ShapeDtypeStruct((4, rows, zd), bf)] + fulls,
        scratch_shapes=[pltpu.VMEM((RT, vd), bf)] + (gather_sems(2, 2) if remote else []),
        compiler_params=pltpu.CompilerParams(vmem_limit_bytes=60 * 2**20, **params),
        name="forward_main",
    )(lengths, smooth, normed, tokens, *ws, *shards)


def ffn_kernel(packed, fs, middle, cot, gain, w_in, w_out, out_o, dm_o, dg_o, *rest):
    if packed:
        keep_a, give_a, keep_b, give_b, gwi, gwo, ascr, gscr = rest
    else:
        gwi, gwo, ascr, gscr = rest

    @pl.when(pl.program_id(0) == 0)
    def _():
        gwi[...] = jnp.zeros_like(gwi)
        gwo[...] = jnp.zeros_like(gwo)
        dg_o[...] = jnp.zeros_like(dg_o)

    m = middle[...].astype(f32)
    inv = lax.rsqrt(jnp.mean(m * m, axis=-1, keepdims=True) + eps)
    gn = lane_row(gain, 4 * NH + 1)
    mr = m * inv
    y = (mr * gn).astype(bf)
    cl = cot[...]
    for j in range(w_in.shape[1] // 256):
        c = slice(j * 256, (j + 1) * 256)
        pre = mm(y, w_in[:, c])
        sg = sigm(pre)
        act = pre * sg
        al = act.astype(bf)
        ascr[:, c] = al
        ga = mm_nt(cl, w_out[c, :])
        gf = (ga * (sg + act - act * sg)).astype(bf)
        gscr[:, c] = gf
        gwo[c, :] += mm_tn(al, cl)
        gwi[:, c] += mm_tn(y, gf)
    out_o[...] = (m + mm(ascr[...], w_out[...])).astype(bf)
    dy = mm_nt(gscr[...], w_in[...])
    part = jnp.sum((dy * mr).reshape(TT // 8, 8, m.shape[1]), axis=0)
    for j in range(m.shape[1] // LG):
        dg_o[j] += part[:, j * LG:(j + 1) * LG]
    dyg = dy * gn
    inner = jnp.mean(dyg * mr, axis=-1, keepdims=True)
    dm_o[...] = (cl.astype(f32) + inv * (dyg - mr * inner)).astype(bf)
    if packed:
        @pl.when(pl.program_id(0) == pl.num_programs(0) - 1)
        def _():
            core = fs[0] % 2
            pack((gwo,), give_a, 1 - core)
            pack((gwo,), keep_a, core)
            pack((gwi,), give_b, 1 - core)
            pack((gwi,), keep_b, core)


def ffn_main(fs, middle, cot, gains, w_in, w_out, packed):
    rows, D = middle.shape
    ff = w_in.shape[1]
    ds = pl.BlockSpec((TT, D), lambda i: (i, 0))
    accs = [(D, ff), (ff, D)]
    pair = [jax.ShapeDtypeStruct((2, D * ff // 4 // LG, LG), bf)] * 4
    extra = pair if packed else [jax.ShapeDtypeStruct(s, f32) for s in accs]
    gain = jax.ShapeDtypeStruct((D // LG, 8, LG), f32)
    return pl.pallas_call(
        functools.partial(ffn_kernel, packed),
        grid=(rows // TT,),
        in_specs=[SMEM, ds, ds] + [const_spec(w) for w in (gains, w_in, w_out)],
        out_specs=[ds, ds] + [const_spec(a) for a in [gain] + extra],
        out_shape=[jax.ShapeDtypeStruct((rows, D), bf)] * 2 + [gain] + extra,
        scratch_shapes=([pltpu.VMEM(s, f32) for s in accs] if packed else [])
        + [pltpu.VMEM((TT, ff), bf), pltpu.VMEM((TT, ff), bf)],
        compiler_params=pltpu.CompilerParams(vmem_limit_bytes=60 * 2**20),
        name="ffn_main",
    )(fs, middle, cot, gains, w_in, w_out)


def backward_kernel(qs, remote, dm, upd, u2, uh, gat, rv, a2, sm, val, vsl, pr, qk, nm, aff, u_h, *rest):
    rest = list(rest)

    def take(n):
        out = rest[:n]
        del rest[:n]
        return out

    if remote:
        keep_a, give_a, keep_b, give_b = take(4)
    dxd_o, gh_o, gu_o, gr_o, gv_o, gsp_o, ga_o = take(7)
    if remote:
        half_a_o, piece_b_o, near_c_o, near_d_o, keep_e_o, give_e_o = take(6)
    gz, gv, gr, gu, gh_w, guh = take(6)
    ascr, = take(1)
    step = pl.program_id(0)
    tiles = pl.num_programs(0) // 2
    if remote:
        core1, near1, mid1, z1, f1, s1, r1 = take(7)
        core2, near2, mid2, z2, s2, r2 = take(6)
        give3, core3, near3, s3, r3 = take(5)
        give4, core4, near4, s4, r4 = take(5)
        a = Reduce(qs[0], "y", s1, r1, keep=keep_a, give=give_a, core_in=core1, near=near1, mid=mid1, z_in=z1, full=f1)
        b = Reduce(qs[1], "x", s2, r2, keep=keep_b, give=give_b, core_in=core2, near=near2, mid=mid2, z_in=z2)
        c = Reduce(qs[2], "y", s3, r3, give=give3, core_in=core3, near=near3)
        d = Reduce(qs[3], "x", s4, r4, give=give4, core_in=core4, near=near4)
        core = a.fs % 2
        ra, rb, rd = a, b, d

    def slot(at, fn):
        if remote:
            pl.when(step == at)(fn)

    @pl.when(step == 0)
    def _():
        for o in (gz, gv, gr, gu, gh_w, guh, ga_o):
            o[...] = jnp.zeros_like(o)

    def open_up():
        greet(fsdp_peers()[:2] + dp_peers())
        met(9)
        a.start("core")
        b.start("core")

    slot(0, open_up)

    def at_one():
        a.to_near()
        b.to_near()

    slot(1, at_one)

    def send_core(chunk, accs):
        pack(accs, chunk.give, 1 - core)
        chunk.start("core")

    def send_near(chunk, accs):
        chunk.wait("core")
        pack_add(accs, chunk.core_in, core)
        chunk.start("near")

    def at_four():
        send_core(c, (gr, gh_w))
        send_core(d, (guh, gu))

    slot(tiles, at_four)
    slot(tiles + 1, lambda: send_near(c, (gr, gh_w)))
    slot(tiles + 3, lambda: a.back())

    @pl.when(step < tiles)
    def _():
        vd = u_h.shape[0]
        d = dm[...].astype(f32)
        gh = (d * uh[...].astype(f32)).astype(bf)
        gu_l = (d * u2[...].astype(f32)).astype(bf)
        gh_o[...] = gh
        gu_o[...] = gu_l
        dxd_o[...] = (d - d * upd[...].astype(f32)).astype(bf)
        s = sm[...]
        gh_w[...] += mm_tn(s, gh)
        gu[...] += mm_tn(s, gu_l)

        def onward():
            ra.to_next()
            rb.to_next()

        slot(3, onward)
        at = pl.ds(pl.multiple_of(step * RT, RT), RT)
        for j in range(vd // 256):
            c = slice(j * 256, (j + 1) * 256)
            dg = mm_nt(gh, u_h[c, :])
            gr_l = (dg * a2[:, c].astype(f32)).astype(bf)
            gr_o[:, c] = gr_l
            ascr[at, c] = (dg * rv[:, c].astype(f32)).astype(bf)
            guh[c, :] += mm_tn(gat[:, c], gh)
            gr[:, c] += mm_tn(s, gr_l)

    @pl.when(step >= tiles)
    def _():
        vd = u_h.shape[0]
        zd = aff.shape[1]
        scale = zd ** -0.5
        gsp = []
        sums = [0.0] * 4
        for b in range(RT // SPAN):
            r = slice(b * SPAN, (b + 1) * SPAN)
            p = pr[r, :]
            pf = p.astype(f32)
            ga = ascr[pl.ds(pl.multiple_of((step - tiles) * RT + b * SPAN, SPAN), SPAN), :]
            dp = mm_nt(ga, val[r, :])
            inner = jnp.sum(dp * pf, axis=-1, keepdims=True)
            gs = (pf * (dp - inner)).astype(bf)
            dq = mm(gs, qk[1, r, :]) * scale
            dk = mm_tn(gs, qk[0, r, :]) * scale
            sh = qk[2, r, :].astype(f32)
            for i, t in enumerate((dq * sh, dq, dk * sh, dk)):
                sums[i] = sums[i] + jnp.sum(t.reshape(SPAN // 8, 8, zd), axis=0)
            gsp.append(((dq * aff[0:1, :] + dk * aff[2:3, :]) * qk[3, r, :].astype(f32)).astype(bf))
            dv = mm_tn(p, ga)
            gv_o[r, :] = (dv * vsl[r, :].astype(f32)).astype(bf)
        for i in range(4):
            ga_o[i] += sums[i]
        gsp = jnp.concatenate(gsp, axis=0)

        def middle():
            ra.to_z()
            rb.to_z()

        slot(tiles, middle)
        slot(tiles + 1, lambda: send_near(rd, (guh, gu)))
        gsp_o[...] = gsp
        gz[...] += mm_tn(sm[...], gsp)
        n = nm[...]
        for j in range(vd // 256):
            c = slice(j * 256, (j + 1) * 256)
            gv[:, c] += mm_tn(n, gv_o[:, c])

    def close():
        pack((gv, gz), give_e_o, 1 - core)
        pack((gv, gz), keep_e_o, core)
        c.add_near()
        near_c_o[...] = near3[...]
        d.add_near()
        near_d_o[...] = near4[...]
        a.wait("back_z")
        half_a_o[...] = f1[a.half(a.x), :]
        piece_b_o[...] = b.add_z()

    slot(2 * tiles - 1, close)


def backward_main(dm, saved, smooth, normed, affine, u_h, chunks=None):
    rows, D = dm.shape
    vd = u_h.shape[0]
    zd = affine.shape[1]
    remote = chunks is not None
    tiles = rows // RT
    upd, u2, uh, val, vsl, gat, rv, a2, pr, qk = saved

    def early(width):
        return pl.BlockSpec((RT, width), lambda i: (jnp.minimum(i, tiles - 1), 0))

    def late(width):
        return pl.BlockSpec((RT, width), lambda i: (jnp.maximum(i - tiles, 0), 0))

    de, ve, vl, dl = early(D), early(vd), late(vd), late(D)
    accs = [(D, zd), (D, vd), (D, vd), (D, D), (D, D), (vd, D)]
    ga = jax.ShapeDtypeStruct((4, 8, zd), f32)
    both = pl.BlockSpec((RT, D), lambda i: (i % tiles, 0))
    ins = [(dm, de), (upd, de), (u2, de), (uh, de), (gat, ve), (rv, ve), (a2, ve), (smooth, both),
           (val, vl), (vsl, vl), (pr, late(SPAN)),
           (qk, pl.BlockSpec((4, RT, zd), lambda i: (0, jnp.maximum(i - tiles, 0), 0))), (normed, dl),
           (affine, const_spec(affine)), (u_h, const_spec(u_h))]
    wide = lambda n: jax.ShapeDtypeStruct((rows, n), bf)
    outs = [(wide(D), de), (wide(D), de), (wide(D), de), (wide(vd), ve), (wide(vd), vl), (wide(zd), late(zd)),
            (ga, const_spec(ga))]
    scratch = [pltpu.VMEM((rows, vd), bf)]
    comm = {}
    qs = ()
    if remote:
        n = [chunks[0].shape[1], chunks[2].shape[1], (D * vd + D * D) // 4 // LG, (vd * D + D * D) // 4 // LG,
             (D * vd + D * zd) // 4 // LG]
        qs = [a // 8 for a in n]
        ins += [(c, const_spec(c)) for c in chunks]
        buf = lambda *s: jax.ShapeDtypeStruct(s + (LG,), bf)
        outs += [(s, const_spec(s)) for s in (buf(n[0] // 2), buf(qs[1]), buf(n[2]), buf(2, n[3] // 2), buf(2, n[4]),
                                              buf(2, n[4]))]
        v = lambda *s: pltpu.VMEM(s + (LG,), bf)
        sem = pltpu.SemaphoreType.DMA((11,))
        scratch = [pltpu.VMEM(a, f32) for a in accs] + scratch
        scratch += [v(2, n[0]), v(n[0]), v(n[0] // 2), v(3, qs[0]), v(n[0]), sem, sem,
                    v(2, n[1]), v(2, n[1] // 2), v(n[1] // 2), v(3, qs[1]), sem, sem,
                    v(2, n[2]), v(2, n[2]), v(n[2]), sem, sem,
                    v(2, n[3]), v(2, n[3]), v(2, n[3] // 2), sem, sem]
        comm = dict(collective_id=2, has_side_effects=True)
    else:
        outs += [(s, const_spec(s)) for s in (jax.ShapeDtypeStruct(a, f32) for a in accs)]
    return pl.pallas_call(
        functools.partial(backward_kernel, qs, remote),
        grid=(2 * tiles,),
        in_specs=[i[1] for i in ins],
        out_specs=[o[1] for o in outs],
        out_shape=[o[0] for o in outs],
        scratch_shapes=scratch,
        compiler_params=pltpu.CompilerParams(vmem_limit_bytes=62 * 2**20, **comm),
        name="backward_main",
    )(*[i[0] for i in ins])


def lane_row(small, row):
    return jnp.concatenate([small[q, row:row + 1, :] for q in range(small.shape[0])], axis=1)


def input_kernel(nseq, seqlen, qs, remote, gh, gu, gr, gsp, gv, w_a, tok, small, dft, xs_i, ks_i, *rest):
    rest = list(rest)

    def take(n):
        out = rest[:n]
        del rest[:n]
        return out

    if remote:
        half_a, piece_b, near_c, near_d, keep_e, give_e, gain1, aff = take(8)
        dn_o, full_a, full_b, full_c, full_d, full_e, small_o = take(7)
    else:
        dn_o, dema_o, dgain_o = take(3)
    dsm, dn, xr, dyspec, dxspec, gspec, dkscr = take(7)
    step = pl.program_id(0)
    ng = dsm.shape[0]
    tiles = pl.num_programs(0) - ng
    nch = seqlen // CH
    rows = nseq * seqlen
    if remote:
        f0, s0, r0 = take(3)
        f1, s1, r1 = take(3)
        mid2, z2, f2, s2, r2 = take(5)
        mid3, z3, f3, s3, r3 = take(5)
        core4, near4, mid4, z4, f4, s4, r4 = take(7)
        sums, near, total, far, s5, r5 = take(6)
        a_ = Reduce(qs[0], "y", s0, r0, full=f0)
        b_ = Reduce(qs[1], "x", s1, r1, full=f1)
        c_ = Reduce(qs[2], "y", s2, r2, near=near_c, mid=mid2, z_in=z2, full=f2)
        d_ = Reduce(qs[3], "x", s3, r3, near=near_d, mid=mid3, z_in=z3, full=f3)
        e_ = Reduce(qs[4], "y", s4, r4, keep=keep_e, give=give_e, core_in=core4, near=near4, mid=mid4, z_in=z4, full=f4)

    def slot(at, fn):
        if remote:
            pl.when(step == at)(fn)

    if remote:
        fs = lax.axis_index("fsdp")

    def across(k, src, dst, peer):
        return pltpu.make_async_remote_copy(src_ref=src, dst_ref=dst, send_sem=s5.at[k], recv_sem=r5.at[k],
                                            device_id=peer, device_id_type=MESH)

    def gathered():
        return [across(k, sums.at[peer[1]], near.at[k], peer) for k, peer in enumerate(fsdp_peers())]

    def hand_over(block):
        for copy, peer in zip(gathered(), fsdp_peers()):
            pl.when(peer[1] == block)(copy.start)

    def open_up():
        greet(fsdp_peers() + dp_peers())
        f0[a_.half(a_.x), :] = half_a[...]
        f1[b_.own_piece(), :] = piece_b[...]
        met(10)
        c_.start("next")
        d_.start("next")
        e_.start("core")
        b_.start("back_z")

    slot(0, open_up)

    def at_one():
        e_.to_near()
        a_.start("back_x")

    slot(1, at_one)

    def at_three():
        c_.to_z()
        d_.to_z()
        b_.widen()

    slot(3, at_three)

    @pl.when(step < tiles)
    def _():
        w_z, w_r, w_u, w_h, w_v = split_pack(w_a)
        at = pl.ds(pl.multiple_of(step * RT, RT), RT)
        x = tok[...].astype(f32)
        n = (x * lax.rsqrt(jnp.mean(x * x, axis=-1, keepdims=True) + eps)).astype(bf)
        a = mm_nt(gv[...], w_v[...])
        b = mm_nt(gh[...], w_h[...]) + mm_nt(gu[...], w_u[...]) + mm_nt(gsp[...], w_z[...]) + mm_nt(gr[...], w_r[...])
        for q in range(ng):
            c = slice(q * LG, (q + 1) * LG)
            xr[q, at, :] = n[:, c]
            dn[q, at, :] = a[:, c].astype(bf)
            dsm[q, at, :] = b[:, c].astype(bf)

    @pl.when(step >= tiles)
    def _():
        g = lax.rem(step - tiles + 1 + fs, ng) if remote else step - tiles

        if remote:
            @pl.when(step > tiles)
            def _():
                hand_over(lax.rem(step - tiles + fs, ng))


        slot(tiles, lambda: e_.to_next())
        def c_first():
            e_.to_z()
            d_.back()

        slot(tiles + 2, c_first)
        slot(tiles + 3, lambda: c_.widen())
        fwd = dft[:2 * CH, CH:]
        inv = dft[3 * CH:]
        for c in range(0, nseq * nch, 2):
            dy = mm(fwd, jnp.concatenate([dsm[g, c * CH:(c + 1) * CH, :], dsm[g, (c + 1) * CH:(c + 2) * CH, :]], axis=1))
            dyspec[c] = dy[:, :LG]
            dyspec[c + 1] = dy[:, LG:]

        def a_second():
            a_.wait("back_x")
            full_a[...] = f0[...]

        slot(tiles, a_second)

        def b_second():
            c_.back()
            b_.wait("back_x")
            full_b[...] = f1[...]

        slot(tiles + 1, b_second)
        slot(tiles + 3, lambda: e_.back())

        def point(i, _):
            rc = pl.ds(pl.multiple_of(i * 16, 16), 16)
            rs = pl.ds(pl.multiple_of(CH + i * 16, 16), 16)
            kc = [ks_i[d, rc, :].astype(f32) for d in range(nch)]
            ks = [ks_i[d, rs, :].astype(f32) for d in range(nch)]
            gc = [0.] * nch
            gs = [0.] * nch
            for b in range(nseq):
                dc = [dyspec[b * nch + c, rc, :] for c in range(nch)]
                ds = [dyspec[b * nch + c, rs, :] for c in range(nch)]
                for c in range(nch):
                    oc = 0.
                    os = 0.
                    for d in range(nch - c):
                        oc = oc + kc[d] * dc[c + d] + ks[d] * ds[c + d]
                        os = os + kc[d] * ds[c + d] - ks[d] * dc[c + d]
                    dxspec[b * nch + c, rc, :] = oc.astype(bf)
                    dxspec[b * nch + c, rs, :] = os.astype(bf)
                for c in range(nch):
                    xc = xs_i[b * nch + c, rc, :].astype(f32)
                    xs = xs_i[b * nch + c, rs, :].astype(f32)
                    for d in range(nch - c):
                        gc[d] = gc[d] + xc * dc[c + d] + xs * ds[c + d]
                        gs[d] = gs[d] + xc * ds[c + d] - xs * dc[c + d]
            for d in range(nch):
                gspec[d, rc, :] = gc[d].astype(bf)
                gspec[d, rs, :] = gs[d].astype(bf)
            return 0

        lax.fori_loop(0, CH // 16, point, 0)
        dgain = 0.
        for c in range(0, nseq * nch, 2):
            both = mm(inv, jnp.concatenate([dxspec[c], dxspec[c + 1]], axis=1))
            for i in range(2):
                r = slice((c + i) * CH, (c + i + 1) * CH)
                t = both[:, i * LG:(i + 1) * LG] + dn[g, r, :].astype(f32)
                dn_o[0, r, :] = t.astype(bf)
                dgain = dgain + jnp.sum((t * xr[g, r, :].astype(f32)).reshape(CH // 8, 8, LG), axis=0)
        whole = dft[2 * CH:]
        for d in range(0, nch, 2):
            dk = mm(whole, jnp.concatenate([gspec[d], gspec[d + 1]], axis=1)) * (1.0 / CH)
            if d:
                dkscr[(d - 1) * CH:d * CH, :] += dk[:CH, :LG]
            dkscr[d * CH:(d + 1) * CH, :] = dk[CH:, :LG] + dk[:CH, LG:]
            dkscr[(d + 1) * CH:(d + 2) * CH, :] = dk[CH:, LG:]
        p = [small[g, i * NH:(i + 1) * NH, :] for i in range(4)]
        a, gg, ex, ro, keep = ema_rates(p)
        p8 = power_of(keep, 8)
        st = [jnp.broadcast_to(p8[h:h + 1, :], (8, LG)) for h in range(NH)]

        def horner(i, ab):
            A, B = ab
            v = dkscr[pl.ds(pl.multiple_of(seqlen - 8 - i * 8, 8), 8), :]
            B = tuple(B[h] * st[h] + A[h] for h in range(NH))
            A = tuple(A[h] * st[h] + v for h in range(NH))
            return (A, B)

        none = dkscr[0:8, :] * 0.0
        zero = (none,) * NH
        A, B = lax.fori_loop(0, seqlen // 8, horner, (zero, zero), unroll=8)
        rr = lax.broadcasted_iota(jnp.int32, (8, LG), 0).astype(f32)
        As = []
        Bs = []
        for h in range(NH):
            lad = ladder(keep[h:h + 1, :], 8)
            low = jnp.concatenate([jnp.zeros((1, LG), f32), lad[:7]], axis=0)
            As.append(jnp.sum(lad * A[h], axis=0, keepdims=True))
            Bs.append(jnp.sum(rr * low * A[h] + 8.0 * lad[7:8] * lad * B[h], axis=0, keepdims=True))
        As = jnp.concatenate(As, axis=0)
        Bs = jnp.concatenate(Bs, axis=0)
        dkeep = a * ex * ro * Bs
        da = ex * ro * As - gg * dkeep
        dg = -a * dkeep
        grads = (da * a * (1.0 - a), dg * gg * (1.0 - gg), a * ro * As, a * ex * As)
        for i, v in enumerate(grads):
            if remote:
                sums[g, i * NH:(i + 1) * NH, :] = v.astype(bf)
            else:
                dema_o[i] = v
        if remote:
            lead = [jnp.sum(dgain, axis=0, keepdims=True), jnp.sum(gain1[g], axis=0, keepdims=True)]
            pad = jnp.zeros((SMALL - 4 * NH - 6, LG), f32)
            sums[g, 4 * NH:, :] = jnp.concatenate(lead + [jnp.sum(aff[...], axis=1), pad], axis=0).astype(bf)
        else:
            dgain_o[...] = dgain

    def close():
        d_.widen()
        for c in gathered():
            c.wait()
        t = sums[fs].astype(f32)
        for k in range(3):
            t = t + near[k].astype(f32)
        total[...] = t.astype(bf)
        second = [across(3 + k, total, far.at[k], peer) for k, peer in enumerate(dp_peers())]
        for c in second:
            c.start()
        e_.widen()
        c_.wait("back_x")
        full_c[...] = f2[...]
        for c in second:
            c.wait()
        for k in range(7):
            t = t + far[k].astype(f32)
        small_o[...] = t
        d_.wait("back_x")
        full_d[...] = f3[...]
        e_.wait("back_x")
        full_e[...] = f4[...]

    slot(tiles + ng - 1, close)


def input_main(grads, w_a, tokens, small, dft, xspec, kspec, nseq, comm_in=None):
    rows, D = tokens.shape
    seqlen = rows // nseq
    nch = seqlen // CH
    ng = D // LG
    nchunks = nseq * nch
    tiles = rows // RT
    remote = comm_in is not None

    def early(a):
        return pl.BlockSpec((RT, a.shape[1]), lambda i: (jnp.minimum(i, tiles - 1), 0))

    def lanes(i):
        at = jnp.maximum(i - tiles, 0)
        return lax.rem(at + 1 + lax.axis_index("fsdp"), ng) if remote else at

    ins = [(a, early(a)) for a in grads] + [(w_a, const_spec(w_a)), (tokens, early(tokens)), (small, const_spec(small))]
    ins += [(dft, const_spec(dft)), (xspec, pl.BlockSpec((nchunks, 2 * CH, LG), lambda i: (0, 0, lanes(i)))),
            (kspec, pl.BlockSpec((nch, 2 * CH, LG), lambda i: (0, 0, lanes(i))))]
    outs = [(jax.ShapeDtypeStruct((ng, rows, LG), bf), pl.BlockSpec((1, rows, LG), lambda i: (lanes(i), 0, 0)))]
    scratch = [pltpu.VMEM((ng, rows, LG), bf)] * 3
    scratch += [pltpu.VMEM((nchunks, 2 * CH, LG), f32),
                pltpu.VMEM((nchunks, 2 * CH, LG), bf), pltpu.VMEM((nch, 2 * CH, LG), bf), pltpu.VMEM((seqlen, LG), f32)]
    params = {}
    qs = ()
    if remote:
        half_a, piece_b, near_c, near_d, keep_e, *_ = comm_in
        n = [half_a.shape[0] * 2, piece_b.shape[0] * 8, near_c.shape[0], near_d.shape[1] * 2, keep_e.shape[1]]
        qs = [a // 8 for a in n]
        ins += [(a, const_spec(a)) for a in comm_in]
        fulls = [jax.ShapeDtypeStruct((a, LG), bf) for a in n]
        one = jax.ShapeDtypeStruct((SMALL, LG), bf)
        outs += [(a, const_spec(a)) for a in fulls + [jax.ShapeDtypeStruct(one.shape, f32)]]
        v = lambda *s: pltpu.VMEM(s + (LG,), bf)
        w = lambda *s: pltpu.VMEM(s + one.shape, bf)
        sem = pltpu.SemaphoreType.DMA((11,))
        scratch += [v(n[0]), sem, sem, v(n[1]), sem, sem,
                    v(n[2] // 2), v(3, qs[2]), v(n[2]), sem, sem,
                    v(n[3] // 2), v(3, qs[3]), v(n[3]), sem, sem,
                    v(2, n[4]), v(n[4]), v(n[4] // 2), v(3, qs[4]), v(n[4]), sem, sem,
                    w(4), w(3), w(), w(7), sem, sem]
        params = dict(collective_id=3, has_side_effects=True)
    else:
        outs += [(jax.ShapeDtypeStruct((4, NH, D), f32), pl.BlockSpec((4, NH, LG), lambda i: (0, 0, lanes(i)))),
                 (jax.ShapeDtypeStruct((8, D), f32), pl.BlockSpec((8, LG), lambda i: (0, lanes(i))))]
    return pl.pallas_call(
        functools.partial(input_kernel, nseq, seqlen, qs, remote),
        grid=(tiles + ng,),
        in_specs=[i[1] for i in ins],
        out_specs=[o[1] for o in outs],
        out_shape=[o[0] for o in outs],
        scratch_shapes=scratch,
        compiler_params=pltpu.CompilerParams(vmem_limit_bytes=62 * 2**20, **params),
        name="input_main",
    )(*[i[0] for i in ins])


def finish_kernel(groups, fs, tok, dxd, dn, small, *rest):
    n = len(groups)
    fulls, sums = rest[:n], rest[n:n + 1]
    outs = list(rest[n + 1:] if groups else rest)
    dtok_o = outs.pop(0)
    x = tok[...].astype(f32)
    inv = lax.rsqrt(jnp.mean(x * x, axis=-1, keepdims=True) + eps)
    d = jnp.concatenate([dn[q] for q in range(dn.shape[0])], axis=1).astype(f32) * lane_row(small, 4 * NH)
    xr = x * inv
    dtok_o[...] = (dxd[...].astype(f32) + inv * (d - xr * jnp.mean(d * xr, axis=-1, keepdims=True))).astype(bf)
    if groups:
        @pl.when(pl.program_id(0) == 0)
        def _():
            gain_o, ema_o, aff_o = outs[:3]
            t = sums[0]
            gain_o[...] = t[4 * NH:4 * NH + 2, :]
            for i in range(4):
                ema_o[i] = t[i * NH:(i + 1) * NH, :]
            width = aff_o.shape[1]
            mine = 0.
            for q in range(4):
                mine = mine + jnp.where(fs[0] == q, 1.0, 0.0) * t[4 * NH + 2:4 * NH + 6, q * width:(q + 1) * width]
            aff_o[...] = mine

        at = 3
        for i, (full, count) in enumerate(zip(fulls, groups)):
            @pl.when(pl.program_id(0) == i % 2)
            def _(full=full, at=at, count=count):
                unpack(full, outs[at:at + count])
            at += count


def finish_main(fs, tokens, dxd, dn, small, fulls=(), sums=None, groups=(), shapes=()):
    rows, D = tokens.shape
    ng = dn.shape[0]
    tile = min(2 * RT, rows)
    ds = pl.BlockSpec((tile, D), lambda i: (i, 0))
    extra = list(fulls) + ([sums] if groups else [])
    outs = [jax.ShapeDtypeStruct(s, f32) for s in shapes]
    return pl.pallas_call(
        functools.partial(finish_kernel, groups),
        grid=(rows // tile,),
        in_specs=[SMEM, ds, ds, pl.BlockSpec((ng, tile, LG), lambda i: (0, i, 0))] + [const_spec(a) for a in [small] + extra],
        out_specs=[ds] + [const_spec(a) for a in outs],
        out_shape=[jax.ShapeDtypeStruct((rows, D), bf)] + outs,
        compiler_params=pltpu.CompilerParams(vmem_limit_bytes=60 * 2**20),
        name="finish",
    )(fs, tokens, dxd, dn, small, *extra)


def local_step(tokens, lengths, cotangent, fs, plain=None, shards=None):
    nseq = lengths.shape[0]
    rows, D = tokens.shape
    dft = jnp.asarray(dft_tables(), bf)
    remote = shards is not None
    if remote:
        ema_t, norm_gains, qk_affine, w_z, w_r, w_u, w_h, w_v, u_h, w_in, w_out = shards
        normed, smooth, x_spec, k_spec, small, affine, w_a, u_full = ema_forward(
            tokens, dft, nseq, comm_in=(ema_t, norm_gains, qk_affine, w_z, w_r, w_u, w_h, w_v, u_h))
        *saved, in_full, out_full = forward_main(
            lengths, smooth, normed, tokens, affine, w_a, u_full, (w_in, w_out))
    else:
        small, affine, w_a, u_full, in_full, out_full = plain
        normed, smooth, x_spec, k_spec = ema_forward(tokens, dft, nseq, small)
        saved = forward_main(lengths, smooth, normed, tokens, affine, w_a, u_full)
    middle, *saved = saved
    output, dm, g_gain1, *first = ffn_main(fs, middle, cotangent, small, in_full, out_full, remote)
    dxd, gh, gu, gr, gv, gsp, g_aff, *second = backward_main(
        dm, saved, smooth, normed, affine, u_full, first if remote else None)
    shared = ((gh, gu, gr, gsp, gv), w_a, tokens, small, dft, x_spec, k_spec, nseq)
    if not remote:
        dn, g_ema, g_gain0 = input_main(*shared)
        grad_tokens, = finish_main(fs, tokens, dxd, dn, small)
        grad_gains = jnp.stack([jnp.sum(g_gain0, axis=0), jnp.sum(g_gain1, axis=1).reshape(D)])
        return output, grad_tokens, (grad_gains, jnp.swapaxes(g_ema, 1, 2), jnp.sum(g_aff, axis=1), *second, *first)
    dn, *fulls, sums = input_main(*shared, (*second, g_gain1, g_aff))
    shapes = [norm_gains.shape, ema_t.shape, qk_affine.shape]
    shapes += [w.shape for w in (w_out, w_in, w_r, w_h, u_h, w_u, w_v, w_z)]
    grad_tokens, g_gains, g_ema, g_aff, g_out, g_in, g_r, g_h, g_uh, g_u, g_v, g_z = finish_main(
        fs, tokens, dxd, dn, small, fulls, sums, (1, 1, 2, 2, 2), shapes)
    return output, grad_tokens, (g_gains, jnp.swapaxes(g_ema, 1, 2), g_aff, g_z, g_v, g_r, g_u, g_h, g_uh, g_in, g_out)


def small_table(norm_gains, ema_params):
    d = norm_gains.shape[1]
    ema = jnp.swapaxes(ema_params, 1, 2).reshape(4 * NH, d)
    rows = jnp.concatenate([ema, norm_gains, jnp.zeros((SMALL - 4 * NH - 2, d), bf)], axis=0).astype(f32)
    return jnp.swapaxes(rows.reshape(SMALL, d // LG, LG), 0, 1)


def per_device(tokens, lengths, norm_gains, ema_params, qk_affine, w_z, w_v, w_r, w_u, w_h, u_h, w_in, w_out, cotangent):
    at = lax.axis_index("fsdp")
    parts = lax.axis_size("fsdp")
    fs = at.reshape(1)
    if parts == 4 and lax.axis_size("dp") == 8:
        shards = (jnp.swapaxes(ema_params, 1, 2), norm_gains, qk_affine, w_z, w_r, w_u, w_h, w_v, u_h, w_in, w_out)
        output, grad_tokens, pieces = local_step(tokens, lengths, cotangent, fs, shards=shards)
        return (output, grad_tokens) + pieces
    gather = lambda w, axis: lax.all_gather(w, "fsdp", axis=axis, tiled=True)
    w_a = gather(jnp.concatenate([w_z, w_r, w_u, w_h, w_v], axis=1), 0)
    plain = (small_table(gather(norm_gains, 1), gather(ema_params, 1)), gather(qk_affine, 1).astype(f32), w_a,
             gather(u_h, 0), gather(w_in, 0), gather(w_out, 0))
    output, grad_tokens, totals = local_step(tokens, lengths, cotangent, fs, plain)
    summed = lax.psum(totals, ("dp", "fsdp"))
    pieces = tuple(
        lax.dynamic_slice_in_dim(g, at * (g.shape[d] // parts), g.shape[d] // parts, d)
        for g, d in zip(summed, (1, 1, 1, 0, 0, 0, 0, 0, 0, 0, 0)))
    return (output, grad_tokens) + pieces


def solution(mesh):
    rows = P(("dp", "fsdp"), None)
    shard = P("fsdp", None)
    wide = P(None, "fsdp")
    deep = P(None, "fsdp", None)
    return jax.shard_map(
        per_device,
        mesh=mesh,
        in_specs=(rows, P(("dp", "fsdp")), wide, deep, wide) + (shard,) * 8 + (rows,),
        out_specs=(rows, rows, wide, deep, wide) + (shard,) * 8,
        check_vma=False,
    )
```

```python
import functools

import jax
import jax.numpy as jnp
import numpy as np
from jax import lax
from jax.experimental import pallas as pl
from jax.experimental.pallas import tpu as pltpu
from jax.sharding import PartitionSpec as P

bf = jnp.bfloat16
f32 = jnp.float32
SPAN = 128
CH = 256
NH = 16
LG = 128
eps = 1e-6


def dft_tables():
    f=np.arange(CH)[:,None]+0.5
    m=np.arange(-CH,CH)[None,:]
    ang=2*np.pi*f*m/(2*CH)
    both=np.concatenate([np.cos(ang),np.sin(ang)],axis=0)
    return np.concatenate([both,both.T],axis=0).astype(np.float32)

def mm(a,b): return jnp.dot(a,b,preferred_element_type=f32)
def mm_tn(a,b): return lax.dot_general(a,b,(((0,),(0,)),((),())),preferred_element_type=f32)
def mm_nt(a,b): return lax.dot_general(a,b,(((1,),(1,)),((),())),preferred_element_type=f32)

def ema_rates(p):
    a=jax.nn.sigmoid(p[0]); g=jax.nn.sigmoid(p[1])
    return a,g,p[2],p[3],1.0-a*g

def power_of(base, n):
    out=None
    sq=base
    while n:
        if n&1: out = sq if out is None else out*sq
        n>>=1
        if n: sq=sq*sq
    return out

def ladder(keep, width):
    r=lax.broadcasted_iota(jnp.int32,(width,keep.shape[-1]),0)
    acc=jnp.ones((width,keep.shape[-1]),f32)
    sq=keep
    bit=1
    while bit<width:
        acc=acc*jnp.where((r&bit)!=0, sq, 1.0)
        sq=sq*sq
        bit*=2
    return acc

MESH = pl.DeviceIdType.MESH


def flip(i, bit):
    return i + bit - 2 * bit * ((i // bit) % 2)


def const_spec(a):
    nd = len(a.shape)
    return pl.BlockSpec(a.shape, lambda i: (0,) * nd, pipeline_mode=pl.Buffered(1))


ANY = pl.BlockSpec(memory_space=pl.ANY)


class Gather:
    def __init__(self, shards, outs, pieces, send, recv, local, straight=()):
        self.shards, self.outs, self.pieces = shards, outs, pieces
        self.send, self.recv, self.local, self.straight = send, recv, local, straight
        self.dp = lax.axis_index("dp")
        self.fs = lax.axis_index("fsdp")
        self.x = self.dp % 2
        self.z = (self.dp // 2) % 2
        self.core_peer = (self.dp, flip(self.fs, 1))
        self.y_peer = (self.dp, flip(self.fs, 2))
        self.x_peer = (flip(self.dp, 1), self.fs)
        self.z_peer = (flip(self.dp, 2), self.fs)

        self.x_across = (self.x_peer[0], self.core_peer[1])
        self.z_across = (self.z_peer[0], self.core_peer[1])

    def peers(self):
        return [self.core_peer, self.y_peer, self.x_peer, self.z_peer]

    def copy(self, p, k):
        a, col, width = self.pieces[p]
        shard, out = self.shards[a], self.outs[a]
        n = shard.shape[0]
        far = flip(self.fs, 2) * n
        cols = pl.ds(col, width)
        x, z = self.x, self.z

        def at(ref, base, zz, xx, half=None):
            r = n // 4 if half is None else n // 8
            row = base + (2 * zz + xx) * (n // 4) + (0 if half is None else half * r)
            return ref.at[pl.ds(pl.multiple_of(row, r), r), cols]

        src, dst, peer = (
            (at(shard, 0, z, x), at(out, self.fs * n, z, x), self.y_peer),
            (at(out, far, z, x),) * 2 + (self.x_peer,),
            (at(out, far, z, x),) * 2 + (self.z_peer,),
            (at(out, far, 1 - z, x, 0),) * 2 + (self.x_peer,),
            (at(out, far, z, 1 - x, 1),) * 2 + (self.z_peer,),
            (at(out, far, z, x),) * 2 + (self.core_peer,),
            (at(out, far, z, 1 - x),) * 2 + (self.core_peer,),
            (at(out, far, 1 - z, x),) * 2 + (self.core_peer,),
            (at(out, far, 1 - z, 1 - x),) * 2 + (self.core_peer,),
            (at(out, far, 1 - z, x, 0),) * 2 + (self.x_across,),
            (at(out, far, z, 1 - x, 1),) * 2 + (self.z_across,),
        )[k]
        return pltpu.make_async_remote_copy(
            src_ref=src, dst_ref=dst, send_sem=self.send.at[11 * p + k], recv_sem=self.recv.at[11 * p + k],
            device_id=peer, device_id_type=MESH)

    def whole(self, a):
        n = self.shards[a].shape[0]
        slot = 11 * len(self.pieces) + a
        return pltpu.make_async_remote_copy(
            src_ref=self.shards[a], dst_ref=self.outs[a].at[pl.ds(pl.multiple_of(self.fs * n, n), n)],
            send_sem=self.send.at[slot], recv_sem=self.recv.at[slot], device_id=self.core_peer, device_id_type=MESH)

    def own(self, a):
        n = self.shards[a].shape[0]
        mine = pl.ds(pl.multiple_of(self.fs * n, n), n)
        return pltpu.make_async_copy(self.shards[a], self.outs[a].at[mine], self.local.at[a])

    def begin(self):
        for p in range(len(self.pieces)):
            self.copy(p, 0).start()
        for a in range(len(self.shards)):
            self.whole(a).start()
            self.own(a).start()

    def relay(self, p):
        self.copy(p, 0).wait_recv()
        for k in (1, 2, 5):
            self.copy(p, k).start()

    def cross(self, p):
        straight = p in self.straight
        self.copy(p, 2).wait_recv()
        for k in (3, 9, 7) if straight else (3, 7):
            self.copy(p, k).start()
        self.copy(p, 1).wait_recv()
        for k in (4, 10, 6) if straight else (4, 6):
            self.copy(p, k).start()

    def last(self, p):
        self.copy(p, 3).wait_recv()
        self.copy(p, 4).wait_recv()
        if p not in self.straight:
            self.copy(p, 8).start()

    def finish(self):
        for p in range(len(self.pieces)):
            ends = (9, 10) if p in self.straight else (8,)
            for k in (0, 1, 2, 3, 4, 5, 6, 7) + ends:
                self.copy(p, k).wait_send()
            for k in (5, 6, 7) + ends:
                self.copy(p, k).wait_recv()
        for a in range(len(self.shards)):
            self.whole(a).wait()
            self.own(a).wait()


def gather_sems(arrays, pieces):
    sem = pltpu.SemaphoreType.DMA((11 * pieces + arrays,))
    return [sem, sem, pltpu.SemaphoreType.DMA((arrays,))]


SMALL = 4 * NH + 16
PIECES = 3


def ema_fwd_kernel(nseq, seqlen, remote, tok, dft, *rest):
    rest = list(rest)

    def take(n):
        out = rest[:n]
        del rest[:n]
        return out

    g = pl.program_id(0)
    nch = seqlen // CH
    rows = nseq * seqlen
    if remote:
        ema_i, gain_i, aff_i, *parts = take(9)
    else:
        small, = take(1)
    normed_o, smooth_o, xs_o, ks_o = take(4)
    if remote:
        small_o, aff_o, w_full, u_full = take(4)
    nscr, kscr, kspec, xspec, yspec = take(5)
    if remote:
        small, sent, own, s1, r1, *sems = take(8)
        fs = lax.axis_index("fsdp")
        gather = Gather((own, parts[5]), (w_full, u_full),
                        ((0, 0, 1664), (0, 1664, own.shape[1] - 1664), (1, 0, parts[5].shape[1])), *sems, (2,))
        across = [pltpu.make_async_remote_copy(
            src_ref=sent.at[fs], dst_ref=sent.at[fs], send_sem=s1.at[k], recv_sem=r1.at[k],
            device_id=peer, device_id_type=MESH) for k, peer in enumerate(fsdp_peers())]

    def slot(at, fn):
        if remote:
            pl.when(g == at)(fn)

    def open_up():
        greet(fsdp_peers() + [gather.x_peer, gather.z_peer, gather.x_across, gather.z_across])
        for i in range(4):
            sent[fs, i * NH:(i + 1) * NH, :] = ema_i[i]
        tail = [gain_i[...].astype(f32), jnp.concatenate([aff_i[...].astype(f32)] * 4, axis=1),
                jnp.zeros((SMALL - 4 * NH - 6, LG), f32)]
        sent[fs, 4 * NH:, :] = jnp.concatenate(tail, axis=0).astype(bf)
        at = 0
        for w in parts[:5]:
            own[:, at:at + w.shape[1]] = w[...]
            at += w.shape[1]
        met(7)
        for c in across:
            c.start()
        gather.begin()

    slot(0, open_up)

    @pl.when(g == 0)
    def _():
        def body(i, _):
            r = pl.ds(pl.multiple_of(i * 256, 256), 256)
            x = tok[r, :].astype(f32)
            n = x * lax.rsqrt(jnp.mean(x * x, axis=-1, keepdims=True) + eps)
            for q in range(x.shape[1] // LG):
                nscr[q, r, :] = n[:, q * LG:(q + 1) * LG]
            return 0
        lax.fori_loop(0, rows // 256, body, 0)

    def settle():
        for c in across:
            c.wait()
        for q in range(4):
            small[q] = sent[q].astype(f32)
        small_o[...] = small[...]
        for q in range(4):
            n = aff_i.shape[1]
            aff_o[:, q * n:(q + 1) * n] = small[q, 4 * NH + 2:4 * NH + 6, 0:n]

    slot(0, settle)

    p = [small[g, i * NH:(i + 1) * NH, :] for i in range(4)]
    normed = (nscr[g] * small[g, 4 * NH:4 * NH + 1, :]).astype(bf)
    normed_o[...] = normed
    a, gg, ex, ro, keep = ema_rates(p)
    w = a * ex * ro * (1.0 / CH)
    step = power_of(keep, 16)
    z0 = []
    st = []
    for h in range(NH):
        z0.append(ladder(keep[h:h + 1, :], 16) * w[h:h + 1, :])
        st.append(jnp.broadcast_to(step[h:h + 1, :], (8, LG)))

    def kgen(i, zs):
        acc = list(zs)
        while len(acc) > 1:
            acc = [acc[j] + acc[j + 1] for j in range(0, len(acc), 2)]
        acc = acc[0]
        kscr[pl.ds(pl.multiple_of(CH + i * 16, 16), 16), :] = acc.astype(bf)
        return tuple(jnp.concatenate([zs[h][:8] * st[h], zs[h][8:] * st[h]], axis=0) for h in range(NH))

    lax.fori_loop(0, seqlen // 16, kgen, tuple(z0), unroll=4)
    kscr[0:CH, :] = jnp.zeros((CH, LG), bf)
    slot(1, lambda: gather.relay(1))
    slot(2, lambda: gather.cross(0))
    slot(3, lambda: gather.cross(2))
    both = dft[:2 * CH]
    fwd = dft[:2 * CH, CH:]
    inv = dft[3 * CH:]
    for d in range(0, nch, 2):
        kd = mm(both, jnp.concatenate([kscr[d * CH:(d + 2) * CH, :], kscr[(d + 1) * CH:(d + 3) * CH, :]], axis=1))
        for i in range(2):
            kspec[d + i] = kd[:, i * LG:(i + 1) * LG]
            ks_o[d + i] = kd[:, i * LG:(i + 1) * LG].astype(bf)
    for c in range(0, nseq * nch, 2):
        xd = mm(fwd, jnp.concatenate([normed[c * CH:(c + 1) * CH], normed[(c + 1) * CH:(c + 2) * CH]], axis=1))
        for i in range(2):
            xspec[c + i] = xd[:, i * LG:(i + 1) * LG]
            xs_o[c + i] = xd[:, i * LG:(i + 1) * LG].astype(bf)

    slot(1, lambda: gather.relay(2))
    slot(3, lambda: gather.last(0))

    def point(i, _):
        rc = pl.ds(pl.multiple_of(i * 16, 16), 16)
        rs = pl.ds(pl.multiple_of(CH + i * 16, 16), 16)
        kc = [kspec[d, rc, :] for d in range(nch)]
        ks = [kspec[d, rs, :] for d in range(nch)]
        for b in range(nseq):
            xc = [xspec[b * nch + c, rc, :] for c in range(nch)]
            xs = [xspec[b * nch + c, rs, :] for c in range(nch)]
            for c in range(nch):
                yc = 0.
                ys = 0.
                for d in range(c + 1):
                    yc = yc + kc[d] * xc[c - d] - ks[d] * xs[c - d]
                    ys = ys + kc[d] * xs[c - d] + ks[d] * xc[c - d]
                yspec[b * nch + c, rc, :] = yc.astype(bf)
                yspec[b * nch + c, rs, :] = ys.astype(bf)
        return 0

    lax.fori_loop(0, CH // 16, point, 0)
    slot(0, lambda: gather.relay(0))
    slot(2, lambda: gather.cross(1))
    slot(3, lambda: gather.last(1))
    for c in range(0, nseq * nch, 2):
        y = mm(inv, jnp.concatenate([yspec[c], yspec[c + 1]], axis=1)).astype(bf)
        smooth_o[c * CH:(c + 1) * CH, :] = y[:, :LG]
        smooth_o[(c + 1) * CH:(c + 2) * CH, :] = y[:, LG:]

    def close():
        gather.last(2)
        gather.finish()

    slot(3, close)


def ema_forward(tokens, dft, nseq, small=None, comm_in=None):
    rows, D = tokens.shape
    seqlen = rows // nseq
    nch = seqlen // CH
    ng = D // LG
    nchunks = nseq * nch
    remote = comm_in is not None
    col = pl.BlockSpec((rows, LG), lambda g: (0, g))
    ins = [tokens, dft] + (list(comm_in) if remote else [small])
    wide = jax.ShapeDtypeStruct((rows, D), bf)
    outs = [(wide, col), (wide, col),
            (jax.ShapeDtypeStruct((nchunks, 2 * CH, D), bf), pl.BlockSpec((nchunks, 2 * CH, LG), lambda g: (0, 0, g))),
            (jax.ShapeDtypeStruct((nch, 2 * CH, D), bf), pl.BlockSpec((nch, 2 * CH, LG), lambda g: (0, 0, g)))]
    scratch = [pltpu.VMEM((ng, rows, LG), f32), pltpu.VMEM((seqlen + CH, LG), bf), pltpu.VMEM((nch, 2 * CH, LG), f32),
               pltpu.VMEM((nchunks, 2 * CH, LG), f32), pltpu.VMEM((nchunks, 2 * CH, LG), bf)]
    params = {}
    if remote:
        n = sum(w.shape[1] for w in comm_in[3:8])
        u = comm_in[8]
        a = jax.ShapeDtypeStruct((4, SMALL, LG), f32)
        b = jax.ShapeDtypeStruct((4, 4 * comm_in[2].shape[1]), f32)
        outs += [(a, const_spec(a)), (b, const_spec(b)), (jax.ShapeDtypeStruct((D, n), bf), ANY),
                 (jax.ShapeDtypeStruct((4 * u.shape[0], D), bf), ANY)]
        sem = pltpu.SemaphoreType.DMA((3,))
        scratch += [pltpu.VMEM(a.shape, f32), pltpu.VMEM(a.shape, bf), pltpu.VMEM((D // 4, n), bf), sem, sem] + gather_sems(2, PIECES)
        params = dict(collective_id=1, has_side_effects=True)
    return pl.pallas_call(
        functools.partial(ema_fwd_kernel, nseq, seqlen, remote),
        grid=(ng,),
        in_specs=[const_spec(a) for a in ins],
        out_specs=[o[1] for o in outs],
        out_shape=[o[0] for o in outs],
        scratch_shapes=scratch,
        compiler_params=pltpu.CompilerParams(vmem_limit_bytes=60 * 2**20, **params),
        name="ema_fwd",
    )(*ins)


class Reduce:
    def __init__(self, q, first, send, recv, **refs):
        self.q, self.first, self.send, self.recv = q, first, send, recv
        self.__dict__.update(refs)
        self.dp = lax.axis_index("dp")
        self.fs = lax.axis_index("fsdp")
        self.x = self.dp % 2
        self.z = self.dp // 2
        self.y = self.fs // 2

    def rows(self, at, count):
        return pl.ds(pl.multiple_of(at, self.q), count)

    def half(self, x):
        return self.rows(x * 4 * self.q, 4 * self.q)

    def remote(self, src, dst, slot, device):
        return pltpu.make_async_remote_copy(
            src_ref=src, dst_ref=dst, send_sem=self.send.at[slot], recv_sem=self.recv.at[slot],
            device_id=device, device_id_type=MESH)

    def line(self):
        for i, oz in enumerate((3, 2, 1)):
            dp = self.dp
            if oz & 1:
                dp = flip(dp, 2)
            if oz & 2:
                dp = flip(dp, 4)
            yield i, dp

    def copies(self, stage):
        q = self.q
        over_y = (self.dp, flip(self.fs, 2))
        over_x = (flip(self.dp, 1), self.fs)
        if stage == "core":
            return [self.remote(self.give, self.core_in, 0, (self.dp, flip(self.fs, 1)))]
        if stage == "near" and self.first == "y":
            return [self.remote(self.core_in.at[1 - self.y], self.near, 1, over_y)]
        if stage == "near":
            return [self.remote(self.core_in.at[y, self.half(1 - self.x)], self.near.at[y], 1 + y, over_x)
                    for y in range(2)]
        if stage == "next" and self.first == "y":
            return [self.remote(self.near.at[self.half(1 - self.x)], self.mid, 3, over_x)]
        if stage == "next":
            return [self.remote(self.near.at[1 - self.y], self.mid, 3, over_y)]
        if stage == "z":
            return [self.remote(self.mid.at[self.rows((dp // 2) * q, q)], self.z_in.at[i], 4 + i, (dp, self.fs))
                    for i, dp in self.line()]
        if stage == "back_z":
            mine = self.full.at[self.own_piece()]
            return [self.remote(mine, mine, 7 + i, (dp, self.fs)) for i, dp in self.line()]
        half = self.full.at[self.half(self.x)]
        return [self.remote(half, half, 10, over_x)]

    def start(self, stage):
        for c in self.copies(stage):
            c.start()

    def wait(self, stage):
        for c in self.copies(stage):
            c.wait()

    def add(self, dst, src, count):
        @pl.loop(0, 4)
        def _(i):
            r = self.rows(i * (count // 4), count // 4)
            dst[r, :] = (dst[r, :].astype(f32) + src[r, :].astype(f32)).astype(bf)

    def to_near(self):
        self.wait("core")
        for y in range(2):
            self.add(self.core_in.at[y], self.keep.at[y], 8 * self.q)
        self.start("near")

    def add_near(self):
        self.wait("near")
        if self.first == "y":
            self.add(self.near, self.core_in.at[self.y], 8 * self.q)
        else:
            for y in range(2):
                self.add(self.near.at[y], self.core_in.at[y, self.half(self.x)], 4 * self.q)

    def to_next(self):
        self.add_near()
        self.start("next")

    def add_next(self):
        self.wait("next")
        src = self.near.at[self.half(self.x)] if self.first == "y" else self.near.at[self.y]
        self.add(self.mid, src, 4 * self.q)

    def to_z(self):
        self.add_next()
        self.start("z")

    def add_z(self):
        self.wait("z")
        total = self.mid[self.rows(self.z * self.q, self.q), :].astype(f32)
        for i in range(3):
            total += self.z_in[i].astype(f32)
        return total.astype(bf)

    def back(self):
        self.full[self.own_piece(), :] = self.add_z()
        self.start("back_z")

    def widen(self):
        self.wait("back_z")
        self.start("back_x")

    def own_piece(self):
        return self.rows((self.x * 4 + self.z) * self.q, self.q)


def greet(peers):
    sem = pltpu.get_barrier_semaphore()
    for peer in peers:
        pl.semaphore_signal(sem, inc=1, device_id=peer, device_id_type=MESH)


def met(count):
    pl.semaphore_wait(pltpu.get_barrier_semaphore(), count)


def dp_peers():
    dp, fs = lax.axis_index("dp"), lax.axis_index("fsdp")
    out = []
    for k in range(1, 8):
        d = dp
        for bit in (1, 2, 4):
            if k & bit:
                d = flip(d, bit)
        out.append((d, fs))
    return out


def fsdp_peers():
    dp, fs = lax.axis_index("dp"), lax.axis_index("fsdp")
    return [(dp, flip(fs, 1)), (dp, flip(fs, 2)), (dp, flip(flip(fs, 1), 2))]


def blocks(accs, shard):
    at = 0
    for acc in accs:
        n = acc.shape[0] // 4
        rows = pl.ds(pl.multiple_of(shard * n, n), n)
        for j in range(acc.shape[1] // LG):
            yield at, n, acc[rows, j * LG:(j + 1) * LG]
            at += n


def pack(accs, dst, core):
    for y in range(2):
        for at, n, block in blocks(accs, 2 * y + core):
            dst[y, at:at + n, :] = block.astype(bf)


def pack_add(accs, dst, core):
    for y in range(2):
        for at, n, block in blocks(accs, 2 * y + core):
            dst[y, at:at + n, :] = (block + dst[y, at:at + n, :].astype(f32)).astype(bf)


def unpack(full, outs):
    at = 0
    for out in outs:
        n = out.shape[0]
        for j in range(out.shape[1] // LG):
            out[:, j * LG:(j + 1) * LG] = full[at:at + n, :].astype(f32)
            at += n


RT = 512
TT = 1024


def sigm(v):
    return 0.5 * jnp.tanh(0.5 * v) + 0.5


def tile_valid(lens, step, seqlen):
    row0 = step * RT
    seq = row0 // seqlen
    return row0 - seq * seqlen, lens[seq]


def split_pack(w_a):
    zd = SPAN
    d = w_a.shape[0]
    vd = (w_a.shape[1] - zd - 2 * d) // 2
    cuts = [0, zd, zd + vd, zd + vd + d, zd + vd + 2 * d, zd + 2 * vd + 2 * d]
    return [w_a.at[:, lo:hi] for lo, hi in zip(cuts, cuts[1:])]


def forward_kernel(seqlen, remote, lens, sm, nm, tok, aff, w_a, u_h, *rest):
    shards, rest = (rest[:2], rest[2:]) if remote else ((), rest)
    middle_o, upd_o, u2_o, uh_o, val_o, vsl_o, gat_o, rv_o, a2_o, pr_o, qk_o = rest[:11]
    rest = rest[11:]
    if remote:
        gather = Gather(shards, rest[:2], tuple((a, 0, w.shape[1]) for a, w in enumerate(shards)), *rest[3:])
        rest = rest[2:]
    gscr = rest[0]

    def slot(at, fn):
        if remote:
            pl.when(pl.program_id(0) == at)(fn)

    slot(0, lambda: greet(gather.peers()))

    w_z, w_r, w_u, w_h, w_v = split_pack(w_a)
    base, length = tile_valid(lens, pl.program_id(0), seqlen)
    zd = w_z.shape[1]
    vd = w_v.shape[1]
    s = sm[...]
    n = nm[...]
    scale = zd ** -0.5
    zp = mm(s, w_z[...])
    sg = sigm(zp)
    sh = zp * sg
    ssl = sg + sh * (1.0 - sg)
    q = (sh * aff[0:1, :] + aff[1:2, :]).astype(bf)
    k = (sh * aff[2:3, :] + aff[3:4, :]).astype(bf)
    qk_o[0] = q
    qk_o[1] = k
    qk_o[2] = sh.astype(bf)
    qk_o[3] = ssl.astype(bf)
    probs = []
    for b in range(RT // SPAN):
        r = slice(b * SPAN, (b + 1) * SPAN)
        sc = mm_nt(q[r], k[r]) * scale
        keys = base + b * SPAN + lax.broadcasted_iota(jnp.int32, (1, SPAN), 1)
        sc = jnp.where(keys < length, sc, -1e9)
        e = jnp.exp(sc - jnp.max(sc, axis=-1, keepdims=True))
        p = (e / jnp.sum(e, axis=-1, keepdims=True)).astype(bf)
        pr_o[r, :] = p
        probs.append(p)

    def begin():
        met(4)
        gather.begin()

    slot(0, begin)

    def relay():
        gather.relay(0)
        gather.relay(1)

    slot(1, relay)

    def cross():
        gather.cross(0)
        gather.cross(1)

    slot(2, cross)

    def last():
        gather.last(0)
        gather.last(1)

    slot(3, last)
    rows = base + lax.broadcasted_iota(jnp.int32, (RT, 1), 0)
    live = (rows < length).astype(f32).astype(bf)
    for j in range(vd // 256):
        c = slice(j * 256, (j + 1) * 256)
        vp = mm(n, w_v[:, c]).astype(bf)
        sg = sigm(vp)
        v = vp * sg
        val_o[:, c] = v
        vsl_o[:, c] = sg + v - v * sg
        att = jnp.concatenate(
            [mm(probs[b], v[b * SPAN:(b + 1) * SPAN]) for b in range(RT // SPAN)], axis=0)
        rp = mm(s, w_r[:, c]).astype(bf)
        sg = sigm(rp)
        re = rp * sg
        att = att.astype(bf) * live
        ga = re * att
        gat_o[:, c] = ga
        gscr[:, c] = ga
        rv_o[:, c] = re * live
        a2_o[:, c] = att * (sg + re - re * sg)
    for j in range(w_h.shape[1] // 256):
        c = slice(j * 256, (j + 1) * 256)
        hp = mm(s, w_h[:, c]) + mm(gscr[...], u_h[:, c])
        up = sigm(mm(s, w_u[:, c]))
        x = tok[:, c].astype(f32)
        sg = sigm(hp)
        cand = hp * sg
        diff = cand - x
        ud = up * diff
        middle_o[:, c] = (x + ud).astype(bf)
        upd_o[:, c] = up.astype(bf)
        u2_o[:, c] = (ud - ud * up).astype(bf)
        uh_o[:, c] = (up * (sg + cand - cand * sg)).astype(bf)


    slot(3, lambda: gather.finish())


def row_spec(width):
    return pl.BlockSpec((RT, width), lambda i: (i, 0))


SMEM = pl.BlockSpec(memory_space=pltpu.SMEM)


def forward_main(lengths, smooth, normed, tokens, affine, w_a, u_h, shards=()):
    rows, D = tokens.shape
    nseq = lengths.shape[0]
    vd = u_h.shape[0]
    zd = affine.shape[1]
    d_out = jax.ShapeDtypeStruct((rows, D), bf)
    v_out = jax.ShapeDtypeStruct((rows, vd), bf)
    ds, vs = row_spec(D), row_spec(vd)
    ws = (affine, w_a, u_h)
    remote = len(shards) > 0
    params = dict(collective_id=4, has_side_effects=True) if remote else {}
    fulls = [jax.ShapeDtypeStruct((4 * w.shape[0], w.shape[1]), bf) for w in shards]
    return pl.pallas_call(
        functools.partial(forward_kernel, rows // nseq, remote),
        grid=(rows // RT,),
        in_specs=[SMEM, ds, ds, ds] + [const_spec(w) for w in (*ws, *shards)],
        out_specs=[ds] * 4 + [vs] * 5 + [row_spec(SPAN), pl.BlockSpec((4, RT, zd), lambda i: (0, i, 0))]
        + [ANY] * len(shards),
        out_shape=[d_out] * 4 + [v_out] * 5
        + [jax.ShapeDtypeStruct((rows, SPAN), bf), jax.ShapeDtypeStruct((4, rows, zd), bf)] + fulls,
        scratch_shapes=[pltpu.VMEM((RT, vd), bf)] + (gather_sems(2, 2) if remote else []),
        compiler_params=pltpu.CompilerParams(vmem_limit_bytes=60 * 2**20, **params),
        name="forward_main",
    )(lengths, smooth, normed, tokens, *ws, *shards)


def ffn_kernel(packed, fs, middle, cot, gain, w_in, w_out, out_o, dm_o, dg_o, *rest):
    if packed:
        keep_a, give_a, keep_b, give_b, gwi, gwo, ascr, gscr = rest
    else:
        gwi, gwo, ascr, gscr = rest

    @pl.when(pl.program_id(0) == 0)
    def _():
        gwi[...] = jnp.zeros_like(gwi)
        gwo[...] = jnp.zeros_like(gwo)
        dg_o[...] = jnp.zeros_like(dg_o)

    m = middle[...].astype(f32)
    inv = lax.rsqrt(jnp.mean(m * m, axis=-1, keepdims=True) + eps)
    gn = lane_row(gain, 4 * NH + 1)
    mr = m * inv
    y = (mr * gn).astype(bf)
    cl = cot[...]
    for j in range(w_in.shape[1] // 256):
        c = slice(j * 256, (j + 1) * 256)
        pre = mm(y, w_in[:, c])
        sg = sigm(pre)
        act = pre * sg
        al = act.astype(bf)
        ascr[:, c] = al
        ga = mm_nt(cl, w_out[c, :])
        gf = (ga * (sg + act - act * sg)).astype(bf)
        gscr[:, c] = gf
        gwo[c, :] += mm_tn(al, cl)
        gwi[:, c] += mm_tn(y, gf)
    out_o[...] = (m + mm(ascr[...], w_out[...])).astype(bf)
    dy = mm_nt(gscr[...], w_in[...])
    part = jnp.sum((dy * mr).reshape(TT // 8, 8, m.shape[1]), axis=0)
    for j in range(m.shape[1] // LG):
        dg_o[j] += part[:, j * LG:(j + 1) * LG]
    dyg = dy * gn
    inner = jnp.mean(dyg * mr, axis=-1, keepdims=True)
    dm_o[...] = (cl.astype(f32) + inv * (dyg - mr * inner)).astype(bf)
    if packed:
        @pl.when(pl.program_id(0) == pl.num_programs(0) - 1)
        def _():
            core = fs[0] % 2
            pack((gwo,), give_a, 1 - core)
            pack((gwo,), keep_a, core)
            pack((gwi,), give_b, 1 - core)
            pack((gwi,), keep_b, core)


def ffn_main(fs, middle, cot, gains, w_in, w_out, packed):
    rows, D = middle.shape
    ff = w_in.shape[1]
    ds = pl.BlockSpec((TT, D), lambda i: (i, 0))
    accs = [(D, ff), (ff, D)]
    pair = [jax.ShapeDtypeStruct((2, D * ff // 4 // LG, LG), bf)] * 4
    extra = pair if packed else [jax.ShapeDtypeStruct(s, f32) for s in accs]
    gain = jax.ShapeDtypeStruct((D // LG, 8, LG), f32)
    return pl.pallas_call(
        functools.partial(ffn_kernel, packed),
        grid=(rows // TT,),
        in_specs=[SMEM, ds, ds] + [const_spec(w) for w in (gains, w_in, w_out)],
        out_specs=[ds, ds] + [const_spec(a) for a in [gain] + extra],
        out_shape=[jax.ShapeDtypeStruct((rows, D), bf)] * 2 + [gain] + extra,
        scratch_shapes=([pltpu.VMEM(s, f32) for s in accs] if packed else [])
        + [pltpu.VMEM((TT, ff), bf), pltpu.VMEM((TT, ff), bf)],
        compiler_params=pltpu.CompilerParams(vmem_limit_bytes=60 * 2**20),
        name="ffn_main",
    )(fs, middle, cot, gains, w_in, w_out)


def backward_kernel(qs, remote, dm, upd, u2, uh, gat, rv, a2, sm, val, vsl, pr, qk, nm, aff, u_h, *rest):
    rest = list(rest)

    def take(n):
        out = rest[:n]
        del rest[:n]
        return out

    if remote:
        keep_a, give_a, keep_b, give_b = take(4)
    dxd_o, gh_o, gu_o, gr_o, gv_o, gsp_o, ga_o = take(7)
    if remote:
        half_a_o, piece_b_o, near_c_o, near_d_o, keep_e_o, give_e_o = take(6)
    gz, gv, gr, gu, gh_w, guh = take(6)
    ascr, = take(1)
    step = pl.program_id(0)
    tiles = pl.num_programs(0) // 2
    if remote:
        core1, near1, mid1, z1, f1, s1, r1 = take(7)
        core2, near2, mid2, z2, s2, r2 = take(6)
        give3, core3, near3, s3, r3 = take(5)
        give4, core4, near4, s4, r4 = take(5)
        a = Reduce(qs[0], "y", s1, r1, keep=keep_a, give=give_a, core_in=core1, near=near1, mid=mid1, z_in=z1, full=f1)
        b = Reduce(qs[1], "x", s2, r2, keep=keep_b, give=give_b, core_in=core2, near=near2, mid=mid2, z_in=z2)
        c = Reduce(qs[2], "y", s3, r3, give=give3, core_in=core3, near=near3)
        d = Reduce(qs[3], "x", s4, r4, give=give4, core_in=core4, near=near4)
        core = a.fs % 2
        ra, rb, rd = a, b, d

    def slot(at, fn):
        if remote:
            pl.when(step == at)(fn)

    @pl.when(step == 0)
    def _():
        for o in (gz, gv, gr, gu, gh_w, guh, ga_o):
            o[...] = jnp.zeros_like(o)

    def open_up():
        greet(fsdp_peers()[:2] + dp_peers())
        met(9)
        a.start("core")
        b.start("core")

    slot(0, open_up)

    def at_one():
        a.to_near()
        b.to_near()

    slot(1, at_one)

    def send_core(chunk, accs):
        pack(accs, chunk.give, 1 - core)
        chunk.start("core")

    def send_near(chunk, accs):
        chunk.wait("core")
        pack_add(accs, chunk.core_in, core)
        chunk.start("near")

    def at_four():
        send_core(c, (gr, gh_w))
        send_core(d, (guh, gu))

    slot(tiles, at_four)
    slot(tiles + 1, lambda: send_near(c, (gr, gh_w)))
    slot(tiles + 3, lambda: a.back())

    @pl.when(step < tiles)
    def _():
        vd = u_h.shape[0]
        d = dm[...].astype(f32)
        gh = (d * uh[...].astype(f32)).astype(bf)
        gu_l = (d * u2[...].astype(f32)).astype(bf)
        gh_o[...] = gh
        gu_o[...] = gu_l
        dxd_o[...] = (d - d * upd[...].astype(f32)).astype(bf)
        s = sm[...]
        gh_w[...] += mm_tn(s, gh)
        gu[...] += mm_tn(s, gu_l)

        def onward():
            ra.to_next()
            rb.to_next()

        slot(3, onward)
        at = pl.ds(pl.multiple_of(step * RT, RT), RT)
        for j in range(vd // 256):
            c = slice(j * 256, (j + 1) * 256)
            dg = mm_nt(gh, u_h[c, :])
            gr_l = (dg * a2[:, c].astype(f32)).astype(bf)
            gr_o[:, c] = gr_l
            ascr[at, c] = (dg * rv[:, c].astype(f32)).astype(bf)
            guh[c, :] += mm_tn(gat[:, c], gh)
            gr[:, c] += mm_tn(s, gr_l)

    @pl.when(step >= tiles)
    def _():
        vd = u_h.shape[0]
        zd = aff.shape[1]
        scale = zd ** -0.5
        gsp = []
        sums = [0.0] * 4
        for b in range(RT // SPAN):
            r = slice(b * SPAN, (b + 1) * SPAN)
            p = pr[r, :]
            pf = p.astype(f32)
            ga = ascr[pl.ds(pl.multiple_of((step - tiles) * RT + b * SPAN, SPAN), SPAN), :]
            dp = mm_nt(ga, val[r, :])
            inner = jnp.sum(dp * pf, axis=-1, keepdims=True)
            gs = (pf * (dp - inner)).astype(bf)
            dq = mm(gs, qk[1, r, :]) * scale
            dk = mm_tn(gs, qk[0, r, :]) * scale
            sh = qk[2, r, :].astype(f32)
            for i, t in enumerate((dq * sh, dq, dk * sh, dk)):
                sums[i] = sums[i] + jnp.sum(t.reshape(SPAN // 8, 8, zd), axis=0)
            gsp.append(((dq * aff[0:1, :] + dk * aff[2:3, :]) * qk[3, r, :].astype(f32)).astype(bf))
            dv = mm_tn(p, ga)
            gv_o[r, :] = (dv * vsl[r, :].astype(f32)).astype(bf)
        for i in range(4):
            ga_o[i] += sums[i]
        gsp = jnp.concatenate(gsp, axis=0)

        def middle():
            ra.to_z()
            rb.to_z()

        slot(tiles, middle)
        slot(tiles + 1, lambda: send_near(rd, (guh, gu)))
        gsp_o[...] = gsp
        gz[...] += mm_tn(sm[...], gsp)
        n = nm[...]
        for j in range(vd // 256):
            c = slice(j * 256, (j + 1) * 256)
            gv[:, c] += mm_tn(n, gv_o[:, c])

    def close():
        pack((gv, gz), give_e_o, 1 - core)
        pack((gv, gz), keep_e_o, core)
        c.add_near()
        near_c_o[...] = near3[...]
        d.add_near()
        near_d_o[...] = near4[...]
        a.wait("back_z")
        half_a_o[...] = f1[a.half(a.x), :]
        piece_b_o[...] = b.add_z()

    slot(2 * tiles - 1, close)


def backward_main(dm, saved, smooth, normed, affine, u_h, chunks=None):
    rows, D = dm.shape
    vd = u_h.shape[0]
    zd = affine.shape[1]
    remote = chunks is not None
    tiles = rows // RT
    upd, u2, uh, val, vsl, gat, rv, a2, pr, qk = saved

    def early(width):
        return pl.BlockSpec((RT, width), lambda i: (jnp.minimum(i, tiles - 1), 0))

    def late(width):
        return pl.BlockSpec((RT, width), lambda i: (jnp.maximum(i - tiles, 0), 0))

    de, ve, vl, dl = early(D), early(vd), late(vd), late(D)
    accs = [(D, zd), (D, vd), (D, vd), (D, D), (D, D), (vd, D)]
    ga = jax.ShapeDtypeStruct((4, 8, zd), f32)
    both = pl.BlockSpec((RT, D), lambda i: (i % tiles, 0))
    ins = [(dm, de), (upd, de), (u2, de), (uh, de), (gat, ve), (rv, ve), (a2, ve), (smooth, both),
           (val, vl), (vsl, vl), (pr, late(SPAN)),
           (qk, pl.BlockSpec((4, RT, zd), lambda i: (0, jnp.maximum(i - tiles, 0), 0))), (normed, dl),
           (affine, const_spec(affine)), (u_h, const_spec(u_h))]
    wide = lambda n: jax.ShapeDtypeStruct((rows, n), bf)
    outs = [(wide(D), de), (wide(D), de), (wide(D), de), (wide(vd), ve), (wide(vd), vl), (wide(zd), late(zd)),
            (ga, const_spec(ga))]
    scratch = [pltpu.VMEM((rows, vd), bf)]
    comm = {}
    qs = ()
    if remote:
        n = [chunks[0].shape[1], chunks[2].shape[1], (D * vd + D * D) // 4 // LG, (vd * D + D * D) // 4 // LG,
             (D * vd + D * zd) // 4 // LG]
        qs = [a // 8 for a in n]
        ins += [(c, const_spec(c)) for c in chunks]
        buf = lambda *s: jax.ShapeDtypeStruct(s + (LG,), bf)
        outs += [(s, const_spec(s)) for s in (buf(n[0] // 2), buf(qs[1]), buf(n[2]), buf(2, n[3] // 2), buf(2, n[4]),
                                              buf(2, n[4]))]
        v = lambda *s: pltpu.VMEM(s + (LG,), bf)
        sem = pltpu.SemaphoreType.DMA((11,))
        scratch = [pltpu.VMEM(a, f32) for a in accs] + scratch
        scratch += [v(2, n[0]), v(n[0]), v(n[0] // 2), v(3, qs[0]), v(n[0]), sem, sem,
                    v(2, n[1]), v(2, n[1] // 2), v(n[1] // 2), v(3, qs[1]), sem, sem,
                    v(2, n[2]), v(2, n[2]), v(n[2]), sem, sem,
                    v(2, n[3]), v(2, n[3]), v(2, n[3] // 2), sem, sem]
        comm = dict(collective_id=2, has_side_effects=True)
    else:
        outs += [(s, const_spec(s)) for s in (jax.ShapeDtypeStruct(a, f32) for a in accs)]
    return pl.pallas_call(
        functools.partial(backward_kernel, qs, remote),
        grid=(2 * tiles,),
        in_specs=[i[1] for i in ins],
        out_specs=[o[1] for o in outs],
        out_shape=[o[0] for o in outs],
        scratch_shapes=scratch,
        compiler_params=pltpu.CompilerParams(vmem_limit_bytes=62 * 2**20, **comm),
        name="backward_main",
    )(*[i[0] for i in ins])


def lane_row(small, row):
    return jnp.concatenate([small[q, row:row + 1, :] for q in range(small.shape[0])], axis=1)


def input_kernel(nseq, seqlen, qs, remote, gh, gu, gr, gsp, gv, w_a, tok, small, dft, xs_i, ks_i, *rest):
    rest = list(rest)

    def take(n):
        out = rest[:n]
        del rest[:n]
        return out

    if remote:
        half_a, piece_b, near_c, near_d, keep_e, give_e, gain1, aff = take(8)
        dn_o, full_a, full_b, full_c, full_d, full_e, small_o = take(7)
    else:
        dn_o, dema_o, dgain_o = take(3)
    dsm, dn, xr, dyspec, dxspec, gspec, dkscr = take(7)
    step = pl.program_id(0)
    ng = dsm.shape[0]
    tiles = pl.num_programs(0) - ng
    nch = seqlen // CH
    rows = nseq * seqlen
    if remote:
        f0, s0, r0 = take(3)
        f1, s1, r1 = take(3)
        mid2, z2, f2, s2, r2 = take(5)
        mid3, z3, f3, s3, r3 = take(5)
        core4, near4, mid4, z4, f4, s4, r4 = take(7)
        sums, near, total, far, s5, r5 = take(6)
        a_ = Reduce(qs[0], "y", s0, r0, full=f0)
        b_ = Reduce(qs[1], "x", s1, r1, full=f1)
        c_ = Reduce(qs[2], "y", s2, r2, near=near_c, mid=mid2, z_in=z2, full=f2)
        d_ = Reduce(qs[3], "x", s3, r3, near=near_d, mid=mid3, z_in=z3, full=f3)
        e_ = Reduce(qs[4], "y", s4, r4, keep=keep_e, give=give_e, core_in=core4, near=near4, mid=mid4, z_in=z4, full=f4)

    def slot(at, fn):
        if remote:
            pl.when(step == at)(fn)

    if remote:
        fs = lax.axis_index("fsdp")

    def across(k, src, dst, peer):
        return pltpu.make_async_remote_copy(src_ref=src, dst_ref=dst, send_sem=s5.at[k], recv_sem=r5.at[k],
                                            device_id=peer, device_id_type=MESH)

    def gathered():
        return [across(k, sums.at[peer[1]], near.at[k], peer) for k, peer in enumerate(fsdp_peers())]

    def hand_over(block):
        for copy, peer in zip(gathered(), fsdp_peers()):
            pl.when(peer[1] == block)(copy.start)

    def open_up():
        greet(fsdp_peers() + dp_peers())
        f0[a_.half(a_.x), :] = half_a[...]
        f1[b_.own_piece(), :] = piece_b[...]
        met(10)
        c_.start("next")
        d_.start("next")
        e_.start("core")
        b_.start("back_z")

    slot(0, open_up)

    def at_one():
        e_.to_near()
        a_.start("back_x")

    slot(1, at_one)

    def at_three():
        c_.to_z()
        d_.to_z()
        b_.widen()

    slot(3, at_three)

    @pl.when(step < tiles)
    def _():
        w_z, w_r, w_u, w_h, w_v = split_pack(w_a)
        at = pl.ds(pl.multiple_of(step * RT, RT), RT)
        x = tok[...].astype(f32)
        n = (x * lax.rsqrt(jnp.mean(x * x, axis=-1, keepdims=True) + eps)).astype(bf)
        a = mm_nt(gv[...], w_v[...])
        b = mm_nt(gh[...], w_h[...]) + mm_nt(gu[...], w_u[...]) + mm_nt(gsp[...], w_z[...]) + mm_nt(gr[...], w_r[...])
        for q in range(ng):
            c = slice(q * LG, (q + 1) * LG)
            xr[q, at, :] = n[:, c]
            dn[q, at, :] = a[:, c].astype(bf)
            dsm[q, at, :] = b[:, c].astype(bf)

    @pl.when(step >= tiles)
    def _():
        g = lax.rem(step - tiles + 1 + fs, ng) if remote else step - tiles

        if remote:
            @pl.when(step > tiles)
            def _():
                hand_over(lax.rem(step - tiles + fs, ng))


        slot(tiles, lambda: e_.to_next())
        def c_first():
            e_.to_z()
            d_.back()

        slot(tiles + 2, c_first)
        slot(tiles + 3, lambda: c_.widen())
        fwd = dft[:2 * CH, CH:]
        inv = dft[3 * CH:]
        for c in range(0, nseq * nch, 2):
            dy = mm(fwd, jnp.concatenate([dsm[g, c * CH:(c + 1) * CH, :], dsm[g, (c + 1) * CH:(c + 2) * CH, :]], axis=1))
            dyspec[c] = dy[:, :LG]
            dyspec[c + 1] = dy[:, LG:]

        def a_second():
            a_.wait("back_x")
            full_a[...] = f0[...]

        slot(tiles, a_second)

        def b_second():
            c_.back()
            b_.wait("back_x")
            full_b[...] = f1[...]

        slot(tiles + 1, b_second)
        slot(tiles + 3, lambda: e_.back())

        def point(i, _):
            rc = pl.ds(pl.multiple_of(i * 16, 16), 16)
            rs = pl.ds(pl.multiple_of(CH + i * 16, 16), 16)
            kc = [ks_i[d, rc, :].astype(f32) for d in range(nch)]
            ks = [ks_i[d, rs, :].astype(f32) for d in range(nch)]
            gc = [0.] * nch
            gs = [0.] * nch
            for b in range(nseq):
                dc = [dyspec[b * nch + c, rc, :] for c in range(nch)]
                ds = [dyspec[b * nch + c, rs, :] for c in range(nch)]
                for c in range(nch):
                    oc = 0.
                    os = 0.
                    for d in range(nch - c):
                        oc = oc + kc[d] * dc[c + d] + ks[d] * ds[c + d]
                        os = os + kc[d] * ds[c + d] - ks[d] * dc[c + d]
                    dxspec[b * nch + c, rc, :] = oc.astype(bf)
                    dxspec[b * nch + c, rs, :] = os.astype(bf)
                for c in range(nch):
                    xc = xs_i[b * nch + c, rc, :].astype(f32)
                    xs = xs_i[b * nch + c, rs, :].astype(f32)
                    for d in range(nch - c):
                        gc[d] = gc[d] + xc * dc[c + d] + xs * ds[c + d]
                        gs[d] = gs[d] + xc * ds[c + d] - xs * dc[c + d]
            for d in range(nch):
                gspec[d, rc, :] = gc[d].astype(bf)
                gspec[d, rs, :] = gs[d].astype(bf)
            return 0

        lax.fori_loop(0, CH // 16, point, 0)
        dgain = 0.
        for c in range(0, nseq * nch, 2):
            both = mm(inv, jnp.concatenate([dxspec[c], dxspec[c + 1]], axis=1))
            for i in range(2):
                r = slice((c + i) * CH, (c + i + 1) * CH)
                t = both[:, i * LG:(i + 1) * LG] + dn[g, r, :].astype(f32)
                dn_o[0, r, :] = t.astype(bf)
                dgain = dgain + jnp.sum((t * xr[g, r, :].astype(f32)).reshape(CH // 8, 8, LG), axis=0)
        whole = dft[2 * CH:]
        for d in range(0, nch, 2):
            dk = mm(whole, jnp.concatenate([gspec[d], gspec[d + 1]], axis=1)) * (1.0 / CH)
            if d:
                dkscr[(d - 1) * CH:d * CH, :] += dk[:CH, :LG]
            dkscr[d * CH:(d + 1) * CH, :] = dk[CH:, :LG] + dk[:CH, LG:]
            dkscr[(d + 1) * CH:(d + 2) * CH, :] = dk[CH:, LG:]
        p = [small[g, i * NH:(i + 1) * NH, :] for i in range(4)]
        a, gg, ex, ro, keep = ema_rates(p)
        p8 = power_of(keep, 8)
        st = [jnp.broadcast_to(p8[h:h + 1, :], (8, LG)) for h in range(NH)]

        def horner(i, ab):
            A, B = ab
            v = dkscr[pl.ds(pl.multiple_of(seqlen - 8 - i * 8, 8), 8), :]
            B = tuple(B[h] * st[h] + A[h] for h in range(NH))
            A = tuple(A[h] * st[h] + v for h in range(NH))
            return (A, B)

        none = dkscr[0:8, :] * 0.0
        zero = (none,) * NH
        A, B = lax.fori_loop(0, seqlen // 8, horner, (zero, zero), unroll=8)
        rr = lax.broadcasted_iota(jnp.int32, (8, LG), 0).astype(f32)
        As = []
        Bs = []
        for h in range(NH):
            lad = ladder(keep[h:h + 1, :], 8)
            low = jnp.concatenate([jnp.zeros((1, LG), f32), lad[:7]], axis=0)
            As.append(jnp.sum(lad * A[h], axis=0, keepdims=True))
            Bs.append(jnp.sum(rr * low * A[h] + 8.0 * lad[7:8] * lad * B[h], axis=0, keepdims=True))
        As = jnp.concatenate(As, axis=0)
        Bs = jnp.concatenate(Bs, axis=0)
        dkeep = a * ex * ro * Bs
        da = ex * ro * As - gg * dkeep
        dg = -a * dkeep
        grads = (da * a * (1.0 - a), dg * gg * (1.0 - gg), a * ro * As, a * ex * As)
        for i, v in enumerate(grads):
            if remote:
                sums[g, i * NH:(i + 1) * NH, :] = v.astype(bf)
            else:
                dema_o[i] = v
        if remote:
            lead = [jnp.sum(dgain, axis=0, keepdims=True), jnp.sum(gain1[g], axis=0, keepdims=True)]
            pad = jnp.zeros((SMALL - 4 * NH - 6, LG), f32)
            sums[g, 4 * NH:, :] = jnp.concatenate(lead + [jnp.sum(aff[...], axis=1), pad], axis=0).astype(bf)
        else:
            dgain_o[...] = dgain

    def close():
        d_.widen()
        for c in gathered():
            c.wait()
        t = sums[fs].astype(f32)
        for k in range(3):
            t = t + near[k].astype(f32)
        total[...] = t.astype(bf)
        second = [across(3 + k, total, far.at[k], peer) for k, peer in enumerate(dp_peers())]
        for c in second:
            c.start()
        e_.widen()
        c_.wait("back_x")
        full_c[...] = f2[...]
        for c in second:
            c.wait()
        for k in range(7):
            t = t + far[k].astype(f32)
        small_o[...] = t
        d_.wait("back_x")
        full_d[...] = f3[...]
        e_.wait("back_x")
        full_e[...] = f4[...]

    slot(tiles + ng - 1, close)


def input_main(grads, w_a, tokens, small, dft, xspec, kspec, nseq, comm_in=None):
    rows, D = tokens.shape
    seqlen = rows // nseq
    nch = seqlen // CH
    ng = D // LG
    nchunks = nseq * nch
    tiles = rows // RT
    remote = comm_in is not None

    def early(a):
        return pl.BlockSpec((RT, a.shape[1]), lambda i: (jnp.minimum(i, tiles - 1), 0))

    def lanes(i):
        at = jnp.maximum(i - tiles, 0)
        return lax.rem(at + 1 + lax.axis_index("fsdp"), ng) if remote else at

    ins = [(a, early(a)) for a in grads] + [(w_a, const_spec(w_a)), (tokens, early(tokens)), (small, const_spec(small))]
    ins += [(dft, const_spec(dft)), (xspec, pl.BlockSpec((nchunks, 2 * CH, LG), lambda i: (0, 0, lanes(i)))),
            (kspec, pl.BlockSpec((nch, 2 * CH, LG), lambda i: (0, 0, lanes(i))))]
    outs = [(jax.ShapeDtypeStruct((ng, rows, LG), bf), pl.BlockSpec((1, rows, LG), lambda i: (lanes(i), 0, 0)))]
    scratch = [pltpu.VMEM((ng, rows, LG), bf)] * 3
    scratch += [pltpu.VMEM((nchunks, 2 * CH, LG), f32),
                pltpu.VMEM((nchunks, 2 * CH, LG), bf), pltpu.VMEM((nch, 2 * CH, LG), bf), pltpu.VMEM((seqlen, LG), f32)]
    params = {}
    qs = ()
    if remote:
        half_a, piece_b, near_c, near_d, keep_e, *_ = comm_in
        n = [half_a.shape[0] * 2, piece_b.shape[0] * 8, near_c.shape[0], near_d.shape[1] * 2, keep_e.shape[1]]
        qs = [a // 8 for a in n]
        ins += [(a, const_spec(a)) for a in comm_in]
        fulls = [jax.ShapeDtypeStruct((a, LG), bf) for a in n]
        one = jax.ShapeDtypeStruct((SMALL, LG), bf)
        outs += [(a, const_spec(a)) for a in fulls + [jax.ShapeDtypeStruct(one.shape, f32)]]
        v = lambda *s: pltpu.VMEM(s + (LG,), bf)
        w = lambda *s: pltpu.VMEM(s + one.shape, bf)
        sem = pltpu.SemaphoreType.DMA((11,))
        scratch += [v(n[0]), sem, sem, v(n[1]), sem, sem,
                    v(n[2] // 2), v(3, qs[2]), v(n[2]), sem, sem,
                    v(n[3] // 2), v(3, qs[3]), v(n[3]), sem, sem,
                    v(2, n[4]), v(n[4]), v(n[4] // 2), v(3, qs[4]), v(n[4]), sem, sem,
                    w(4), w(3), w(), w(7), sem, sem]
        params = dict(collective_id=3, has_side_effects=True)
    else:
        outs += [(jax.ShapeDtypeStruct((4, NH, D), f32), pl.BlockSpec((4, NH, LG), lambda i: (0, 0, lanes(i)))),
                 (jax.ShapeDtypeStruct((8, D), f32), pl.BlockSpec((8, LG), lambda i: (0, lanes(i))))]
    return pl.pallas_call(
        functools.partial(input_kernel, nseq, seqlen, qs, remote),
        grid=(tiles + ng,),
        in_specs=[i[1] for i in ins],
        out_specs=[o[1] for o in outs],
        out_shape=[o[0] for o in outs],
        scratch_shapes=scratch,
        compiler_params=pltpu.CompilerParams(vmem_limit_bytes=62 * 2**20, **params),
        name="input_main",
    )(*[i[0] for i in ins])


def finish_kernel(groups, fs, tok, dxd, dn, small, *rest):
    n = len(groups)
    fulls, sums = rest[:n], rest[n:n + 1]
    outs = list(rest[n + 1:] if groups else rest)
    dtok_o = outs.pop(0)
    x = tok[...].astype(f32)
    inv = lax.rsqrt(jnp.mean(x * x, axis=-1, keepdims=True) + eps)
    d = jnp.concatenate([dn[q] for q in range(dn.shape[0])], axis=1).astype(f32) * lane_row(small, 4 * NH)
    xr = x * inv
    dtok_o[...] = (dxd[...].astype(f32) + inv * (d - xr * jnp.mean(d * xr, axis=-1, keepdims=True))).astype(bf)
    if groups:
        @pl.when(pl.program_id(0) == 0)
        def _():
            gain_o, ema_o, aff_o = outs[:3]
            t = sums[0]
            gain_o[...] = t[4 * NH:4 * NH + 2, :]
            for i in range(4):
                ema_o[i] = t[i * NH:(i + 1) * NH, :]
            width = aff_o.shape[1]
            mine = 0.
            for q in range(4):
                mine = mine + jnp.where(fs[0] == q, 1.0, 0.0) * t[4 * NH + 2:4 * NH + 6, q * width:(q + 1) * width]
            aff_o[...] = mine

        at = 3
        for i, (full, count) in enumerate(zip(fulls, groups)):
            @pl.when(pl.program_id(0) == i % 2)
            def _(full=full, at=at, count=count):
                unpack(full, outs[at:at + count])
            at += count


def finish_main(fs, tokens, dxd, dn, small, fulls=(), sums=None, groups=(), shapes=()):
    rows, D = tokens.shape
    ng = dn.shape[0]
    tile = min(2 * RT, rows)
    ds = pl.BlockSpec((tile, D), lambda i: (i, 0))
    extra = list(fulls) + ([sums] if groups else [])
    outs = [jax.ShapeDtypeStruct(s, f32) for s in shapes]
    return pl.pallas_call(
        functools.partial(finish_kernel, groups),
        grid=(rows // tile,),
        in_specs=[SMEM, ds, ds, pl.BlockSpec((ng, tile, LG), lambda i: (0, i, 0))] + [const_spec(a) for a in [small] + extra],
        out_specs=[ds] + [const_spec(a) for a in outs],
        out_shape=[jax.ShapeDtypeStruct((rows, D), bf)] + outs,
        compiler_params=pltpu.CompilerParams(vmem_limit_bytes=60 * 2**20),
        name="finish",
    )(fs, tokens, dxd, dn, small, *extra)


def local_step(tokens, lengths, cotangent, fs, plain=None, shards=None):
    nseq = lengths.shape[0]
    rows, D = tokens.shape
    dft = jnp.asarray(dft_tables(), bf)
    remote = shards is not None
    if remote:
        ema_t, norm_gains, qk_affine, w_z, w_r, w_u, w_h, w_v, u_h, w_in, w_out = shards
        normed, smooth, x_spec, k_spec, small, affine, w_a, u_full = ema_forward(
            tokens, dft, nseq, comm_in=(ema_t, norm_gains, qk_affine, w_z, w_r, w_u, w_h, w_v, u_h))
        *saved, in_full, out_full = forward_main(
            lengths, smooth, normed, tokens, affine, w_a, u_full, (w_in, w_out))
    else:
        small, affine, w_a, u_full, in_full, out_full = plain
        normed, smooth, x_spec, k_spec = ema_forward(tokens, dft, nseq, small)
        saved = forward_main(lengths, smooth, normed, tokens, affine, w_a, u_full)
    middle, *saved = saved
    output, dm, g_gain1, *first = ffn_main(fs, middle, cotangent, small, in_full, out_full, remote)
    dxd, gh, gu, gr, gv, gsp, g_aff, *second = backward_main(
        dm, saved, smooth, normed, affine, u_full, first if remote else None)
    shared = ((gh, gu, gr, gsp, gv), w_a, tokens, small, dft, x_spec, k_spec, nseq)
    if not remote:
        dn, g_ema, g_gain0 = input_main(*shared)
        grad_tokens, = finish_main(fs, tokens, dxd, dn, small)
        grad_gains = jnp.stack([jnp.sum(g_gain0, axis=0), jnp.sum(g_gain1, axis=1).reshape(D)])
        return output, grad_tokens, (grad_gains, jnp.swapaxes(g_ema, 1, 2), jnp.sum(g_aff, axis=1), *second, *first)
    dn, *fulls, sums = input_main(*shared, (*second, g_gain1, g_aff))
    shapes = [norm_gains.shape, ema_t.shape, qk_affine.shape]
    shapes += [w.shape for w in (w_out, w_in, w_r, w_h, u_h, w_u, w_v, w_z)]
    grad_tokens, g_gains, g_ema, g_aff, g_out, g_in, g_r, g_h, g_uh, g_u, g_v, g_z = finish_main(
        fs, tokens, dxd, dn, small, fulls, sums, (1, 1, 2, 2, 2), shapes)
    return output, grad_tokens, (g_gains, jnp.swapaxes(g_ema, 1, 2), g_aff, g_z, g_v, g_r, g_u, g_h, g_uh, g_in, g_out)


def small_table(norm_gains, ema_params):
    d = norm_gains.shape[1]
    ema = jnp.swapaxes(ema_params, 1, 2).reshape(4 * NH, d)
    rows = jnp.concatenate([ema, norm_gains, jnp.zeros((SMALL - 4 * NH - 2, d), bf)], axis=0).astype(f32)
    return jnp.swapaxes(rows.reshape(SMALL, d // LG, LG), 0, 1)


def per_device(tokens, lengths, norm_gains, ema_params, qk_affine, w_z, w_v, w_r, w_u, w_h, u_h, w_in, w_out, cotangent):
    at = lax.axis_index("fsdp")
    parts = lax.axis_size("fsdp")
    fs = at.reshape(1)
    if parts == 4 and lax.axis_size("dp") == 8:
        shards = (jnp.swapaxes(ema_params, 1, 2), norm_gains, qk_affine, w_z, w_r, w_u, w_h, w_v, u_h, w_in, w_out)
        output, grad_tokens, pieces = local_step(tokens, lengths, cotangent, fs, shards=shards)
        return (output, grad_tokens) + pieces
    gather = lambda w, axis: lax.all_gather(w, "fsdp", axis=axis, tiled=True)
    w_a = gather(jnp.concatenate([w_z, w_r, w_u, w_h, w_v], axis=1), 0)
    plain = (small_table(gather(norm_gains, 1), gather(ema_params, 1)), gather(qk_affine, 1).astype(f32), w_a,
             gather(u_h, 0), gather(w_in, 0), gather(w_out, 0))
    output, grad_tokens, totals = local_step(tokens, lengths, cotangent, fs, plain)
    summed = lax.psum(totals, ("dp", "fsdp"))
    pieces = tuple(
        lax.dynamic_slice_in_dim(g, at * (g.shape[d] // parts), g.shape[d] // parts, d)
        for g, d in zip(summed, (1, 1, 1, 0, 0, 0, 0, 0, 0, 0, 0)))
    return (output, grad_tokens) + pieces


def solution(mesh):
    rows = P(("dp", "fsdp"), None)
    shard = P("fsdp", None)
    wide = P(None, "fsdp")
    deep = P(None, "fsdp", None)
    return jax.shard_map(
        per_device,
        mesh=mesh,
        in_specs=(rows, P(("dp", "fsdp")), wide, deep, wide) + (shard,) * 8 + (rows,),
        out_specs=(rows, rows, wide, deep, wide) + (shard,) * 8,
        check_vma=False,
    )
```
